32 devices in a mesh: grp: 2 (over y), smp: 4 (over z), snp: 2 (over x), pair: 2 (over core).
Axes of the slice: x: 2, y: 2, z: 4, core: 2. Of those that a mesh axis runs over, the one named last changes fastest.
Arguments:
- dosage: bfloat16 [16384, 4096], P(('grp', 'smp'), ('snp', 'pair')), parts along dimension 0, may hold values from 0 to 2
- allele_mean: float32 [8192], P('grp'), parts along dimension 0, may hold values from 0.7 to 1.3
- snp_scale: float32 [8192], P('grp'), parts along dimension 0, may hold values from 1.5 to 4.5
- band_next: int32 [128], P('grp'), parts along dimension 0, may hold values from 1 to 2
- ld_prev: float32 [8192, 320], P(('grp', 'smp')), parts along dimension 0, may hold values from -0.95 to 1, as said below
- band_prev: int32 [128], P('grp'), parts along dimension 0, may hold values from 1 to 2
- zscores: float32 [8192, 512], P(('grp', 'smp'), ('snp', 'pair')), parts along dimension 0, may hold values from -22 to 22
- observed: int32 [8192, 8], P(('grp', 'smp'), ('snp', 'pair')), parts along dimension 0, may hold values 0 or 1
Outputs:
- ld_next: float32 [8192, 320], P(('grp', 'snp', 'pair')), parts along dimension 0
- imputed: float32 [8192, 512], P(('grp', 'smp'), ('snp', 'pair')), parts along dimension 0
The draws below stay inside these ranges and needn't reach their ends.
There are 2 independent parts, one for each index of `grp`. The reference program is written for one: setup_inputs(seed, part) draws one part's arguments, and reference() takes and returns one part's arrays. A program takes and returns all parts, laid end to end along the dimension named above; each array names one. Nothing has to cross between parts.
Inputs may be any that keep to these rules, and one draw needn't show every extreme that they name: `ld_prev`: row i holds the band of a symmetric matrix with unit diagonal: entry (i, o) belongs to column 64 * (i // 64) - 128 + o. For every band mask, the masked matrix plus the identity is positive definite.
All inputs are finite; a program needn't handle non-finite values. No bound on the sum of `observed` on one device may be relied on, other than what follows from the above.
Results may differ from the reference program's by a relative error of at most 0.00049.
Values may be sent and summed in bfloat16 or wider, within the bound.
A program may use at most 128 MiB of HBM per device.

```python
import math
import jax
import jax.numpy as jnp
from jax import lax

W = 4096
TILE = 64
BMAX = 2
TRAITS = 512
TBLK = 64
ITERS = 3
NT = 64
NBLK = 8
SAMPLES = 8192


def band_of(window, tile_size, span):
    local_rows = window.shape[0]
    tile_count = local_rows // tile_size
    blocks = window.reshape(tile_count, tile_size, tile_count + span - 1, tile_size)
    pieces = []
    for offset in range(span):
        diagonal = jnp.diagonal(blocks[:, :, offset:offset + tile_count, :], axis1=0, axis2=2)
        pieces.append(jnp.transpose(diagonal, (2, 0, 1)))
    return jnp.concatenate(pieces, axis=2).reshape(local_rows, span * tile_size)


def ld_dense(key):
    base_key = jax.random.fold_in(key, 11)
    sign_key, step_key, hot_key, jitter_key = jax.random.split(base_key, 4)
    allele_sign = jnp.where(jax.random.randint(sign_key, (W,), 0, 2) == 0, -1.0, 1.0).astype(jnp.float32)
    hotspot = jax.random.randint(hot_key, (W,), 0, 16) == 0
    base_step = jnp.exp(jax.random.uniform(step_key, (W,), jnp.float32, jnp.log(0.02), jnp.log(1.0)))
    step_sizes = jnp.where(hotspot, 4.0, base_step)
    jitter_raw = jax.random.uniform(jitter_key, (W, W), jnp.float32, 0.5, 1.5)
    position = jnp.cumsum(step_sizes)
    distance = jnp.abs(position[:, None] - position[None, :])
    jitter = 0.5 * (jitter_raw + jitter_raw.T)
    tile_of = jnp.arange(W, dtype=jnp.int32) // TILE
    in_band = jnp.abs(tile_of[:, None] - tile_of[None, :]) <= BMAX
    identity = jnp.eye(W, dtype=jnp.float32)
    kernel = jnp.where(in_band, jnp.exp(-distance) * jitter, 0.0) * (1.0 - identity)
    row_weight = jnp.sum(kernel, axis=1)
    balance = 1.0 / jnp.sqrt(row_weight)
    balanced = balance[:, None] * kernel * balance[None, :]
    largest = jnp.max(jnp.sum(balanced, axis=1))
    scaled = jnp.minimum(1.8 * balanced / largest, 0.95)
    return allele_sign[:, None] * scaled * allele_sign[None, :] + identity


def draw_dosage(key, part):
    block_rows = SAMPLES // 8
    hot_key = jax.random.fold_in(key, 7)
    hotspot = jax.random.randint(hot_key, (W,), 0, 8) == 0
    threshold = jnp.where(hotspot, 32, 1)
    column = lax.broadcasted_iota(jnp.int32, (block_rows, W), 1)

    def one_block(block_index):
        block_key = jax.random.fold_in(key, block_index + 100)
        summed = jnp.zeros((block_rows, W), jnp.float32)
        for haplotype in range(2):
            hap_key = jax.random.fold_in(block_key, haplotype)
            break_key, fresh_key, jitter_key = jax.random.split(hap_key, 3)
            breaks = jax.random.randint(break_key, (block_rows, W), 0, 64)
            starts = (breaks < threshold[None, :]) | (column == 0)
            source = lax.cummax(jnp.where(starts, column, 0), axis=1)
            fresh_draw = jax.random.uniform(fresh_key, (block_rows, W), jnp.float32)
            carried = jnp.take_along_axis(fresh_draw, source, axis=1)
            jitter = jax.random.uniform(jitter_key, (block_rows, W), jnp.float32)
            summed = summed + 0.8 * carried + 0.2 * jitter
        return summed.astype(jnp.bfloat16)
    blocks = lax.map(one_block, jnp.arange(8, dtype=jnp.int32))
    return blocks.reshape(SAMPLES, W)


def draw_ld_prev(key, part):
    symmetric = ld_dense(key)
    band_reach = TILE * BMAX
    padded = jnp.pad(symmetric, ((0, 0), (band_reach, band_reach)))
    return band_of(padded, TILE, 2 * BMAX + 1)


def draw_zscores(key, part):
    base_key = jax.random.fold_in(key, 13)
    column_key = jax.random.fold_in(base_key, 0)
    value_key = jax.random.fold_in(base_key, 1)
    causal_key = jax.random.fold_in(base_key, 3)
    effect_key = jax.random.fold_in(base_key, 4)
    amp_key = jax.random.fold_in(base_key, 5)
    linkage = ld_dense(key)
    positions = jnp.arange(W, dtype=jnp.float32)
    row_factor = 0.6 * jnp.exp(jnp.log(3.0) * positions / (W - 1))
    column_factor = jnp.exp(jax.random.uniform(column_key, (TRAITS,), jnp.float32, jnp.log(0.3), jnp.log(2.0)))
    amplitude = jnp.exp(jax.random.uniform(amp_key, (TRAITS,), jnp.float32, jnp.log(0.1), jnp.log(2.0)))
    causal = jax.random.randint(causal_key, (W, TRAITS), 0, 64) == 0
    effect = jnp.where(causal, jax.random.uniform(effect_key, (W, TRAITS), jnp.float32, -1.0, 1.0), 0.0)
    signal = jnp.dot(linkage, effect, precision=lax.Precision.HIGHEST)
    background = jnp.clip(jax.random.normal(value_key, (W, TRAITS), jnp.float32), -2.8, 2.8)
    values = row_factor[:, None] * background + amplitude[None, :] * signal
    return column_factor[None, :] * values


def place_ends(entries, stream_key, smallest, top_value):
    place = [jax.random.randint(jax.random.fold_in(stream_key, axis), (), 0, length) for axis, length in enumerate(entries.shape)]
    widest = entries.shape.index(max(entries.shape))
    beside = place[:widest] + [(place[widest] + 1) % entries.shape[widest]] + place[widest + 1:]
    return entries.at[tuple(place)].set(smallest).at[tuple(beside)].set(top_value)


def setup_inputs(seed: int = 0, part: int = 0) -> dict:
    arg_keys = jax.random.split(jax.random.key(seed), 9)
    own_keys = jax.random.split(jax.random.fold_in(arg_keys[8], part), 9)
    return {
        "dosage": draw_dosage(jax.random.fold_in(jax.random.fold_in(arg_keys[8], part), 71), part),
        "allele_mean": jnp.clip(jax.random.uniform(own_keys[1], (W,), jnp.float32, 0.7, 1.3), 0.7, 1.3),
        "snp_scale": jnp.clip(jnp.exp(jax.random.uniform(own_keys[2], (W,), jnp.float32, math.log(1.5), math.log(4.5))), 1.5, 4.5),
        "band_next": place_ends(jax.random.randint(own_keys[3], (NT,), 1, BMAX + 1), jax.random.fold_in(own_keys[3], 1), 1, BMAX).astype(jnp.int32),
        "ld_prev": draw_ld_prev(jax.random.fold_in(jax.random.fold_in(arg_keys[8], part), 71), part),
        "band_prev": place_ends(jax.random.randint(own_keys[5], (NT,), 1, BMAX + 1), jax.random.fold_in(own_keys[5], 1), 1, BMAX).astype(jnp.int32),
        "zscores": draw_zscores(jax.random.fold_in(jax.random.fold_in(arg_keys[8], part), 71), part),
        "observed": place_ends((jax.random.randint(own_keys[7], (W, NBLK), 0, 4) < 3).astype(jnp.int32), jax.random.fold_in(own_keys[7], 1), 0, 1),
    }


ridge_term = 1.0


def tile_table(widths, reach_tiles):
    tile_total = widths.shape[0]
    padded = jnp.pad(widths, reach_tiles)
    columns = []
    for offset in range(-reach_tiles, reach_tiles + 1):
        beside = padded[reach_tiles + offset:reach_tiles + offset + tile_total]
        columns.append(abs(offset) <= jnp.minimum(widths, beside))
    return jnp.stack(columns, axis=1).astype(jnp.float32)


def expand_table(table, tile_size):
    return jnp.repeat(jnp.repeat(table, tile_size, axis=0), tile_size, axis=1)


def reference(dosage, allele_mean, snp_scale, band_next, ld_prev, band_prev, zscores, observed):
    band_reach = TILE * BMAX
    band_cols = (2 * BMAX + 1) * TILE
    padded_dose = jnp.pad(dosage, ((0, 0), (band_reach, band_reach)))
    padded_mean = jnp.pad(allele_mean, band_reach)
    padded_scale = jnp.pad(snp_scale, band_reach)

    def tile_gram(tile_index):
        first_col = (tile_index * TILE).astype(jnp.int32)
        columns = lax.dynamic_slice_in_dim(padded_dose, first_col, band_cols, 1)
        mean_part = lax.dynamic_slice_in_dim(padded_mean, first_col, band_cols, 0)
        scale_part = lax.dynamic_slice_in_dim(padded_scale, first_col, band_cols, 0)
        normed = ((columns.astype(jnp.float32) - mean_part) * scale_part).astype(jnp.bfloat16)
        own_block = normed[:, band_reach:band_reach + TILE]
        return jnp.dot(own_block.T, normed, preferred_element_type=jnp.float32)

    gram = lax.map(tile_gram, jnp.arange(NT, dtype=jnp.int32)).reshape(W, band_cols)
    next_mask = expand_table(tile_table(band_next, BMAX), TILE)
    ld_next = next_mask * gram / SAMPLES

    band = expand_table(tile_table(band_prev, BMAX), TILE) * ld_prev
    seen = jnp.repeat(observed.astype(jnp.float32), TBLK, axis=1)
    tiles = band.reshape(NT, TILE, band_cols)

    def apply_band(vector):
        padded = jnp.pad(vector, ((band_reach, band_reach), (0, 0)))
        stacked = padded.reshape(NT + 2 * BMAX, TILE, TRAITS)
        windows = jnp.concatenate([stacked[offset:offset + NT] for offset in range(2 * BMAX + 1)], axis=1)
        result = jnp.einsum("uio,uot->uit", tiles, windows, precision=lax.Precision.HIGHEST)
        return result.reshape(W, TRAITS)

    def operate(vector):
        masked = seen * vector
        return seen * (apply_band(masked) + ridge_term * masked) + (1.0 - seen) * vector

    rhs = seen * zscores
    solution = jnp.zeros_like(rhs)
    residual = rhs
    direction = rhs
    norm_now = jnp.sum(residual * residual, axis=0)
    for turn_index in range(ITERS):
        image = operate(direction)
        step_size = norm_now / jnp.sum(direction * image, axis=0)
        solution = solution + step_size * direction
        residual = residual - step_size * image
        norm_next = jnp.sum(residual * residual, axis=0)
        direction = residual + (norm_next / norm_now) * direction
        norm_now = norm_next
    imputed = apply_band(seen * solution)
    return ld_next, imputed
```

```python
import functools
import jax
import jax.numpy as jnp
from jax import lax
from jax.sharding import PartitionSpec as P
from jax.experimental import pallas as pl
from jax.experimental.pallas import tpu as pltpu

TILE = 64
BMAX = 2
TBLK = 64
SPAN = 2 * BMAX + 1
REACH = TILE * BMAX
PAIR = 2 * TILE
LANES = 128
WIDE = 384
CHUNK = 256
STEP = 64
F32 = jnp.float32
BF16 = jnp.bfloat16
MESH = pl.DeviceIdType.MESH

ridge_term = 1.0


def split_two(value):
    high = value.astype(BF16)
    low = (value - high.astype(F32)).astype(BF16)
    return high, low


def folded(value):
    return jnp.sum(value.reshape(value.shape[0] // 8, 8, value.shape[1]), axis=0)


def total_row(value):
    return jnp.sum(value, axis=0, keepdims=True)


def tile_flags(widths, tile, count):
    here = widths[tile]
    flags = []
    for offset in range(-BMAX, BMAX + 1):
        place = tile + offset
        inside = (place >= 0) & (place < count)
        beside = widths[jnp.clip(place, 0, count - 1)]
        reach = abs(offset)
        flags.append(jnp.where(inside & (here >= reach) & (beside >= reach), 1.0, 0.0).astype(F32))
    return flags


def mask_row(flags, rows, width):
    lane_tile = lax.broadcasted_iota(jnp.int32, (rows, width), 1) // TILE
    mask = jnp.zeros((rows, width), F32)
    for index, flag in enumerate(flags):
        mask = jnp.where(lane_tile == index, flag, mask)
    return mask


def kernel(
    sizes,
    dosage, mean, scale, band_next, ld_prev, band_prev, zscores, seen,
    ld_next, imputed,
    dos, dos_side, normed, gram, moving, edge_in, edge_out,
    vec, vec_two, band_two, image, res1, img0, red,
    dos_sem, side_sem, vec_send, vec_recv, red_send, red_recv, mov_send, mov_recv, edge_sem,
):
    n_smp, n_snp, n_pair = sizes
    samples, cols = dos.shape
    rows = zscores.shape[0]
    tiles = rows // TILE
    chunks = cols // CHUNK
    blocks = cols // PAIR
    tile_total = band_next.shape[0]
    me = lax.axis_index("smp")
    place = lax.axis_index("snp") * n_pair + lax.axis_index("pair")
    places = n_snp * n_pair
    first_col = place * cols
    order = list(range(1, chunks)) + [0]

    def at_place(index):
        return {"snp": index // n_pair, "pair": index % n_pair}

    has_left, has_right = place > 0, place < places - 1
    has_prev, has_next = me > 0, me < n_smp - 1
    left_id = at_place(jnp.maximum(place - 1, 0))
    right_id = at_place(jnp.minimum(place + 1, places - 1))

    fetches = []
    for chunk in order:
        span = pl.ds(chunk * CHUNK, CHUNK)
        fetch = pltpu.make_async_copy(dosage.at[:, span], dos.at[:, span], dos_sem.at[chunk])
        fetch.start()
        fetches.append(fetch)

    barrier = pltpu.get_barrier_semaphore()
    for step in range(1, n_smp):
        pl.semaphore_signal(
            barrier, inc=1, device_id={"smp": lax.rem(me + step, n_smp)}, device_id_type=MESH
        )

    @pl.when(has_left)
    def _():
        pl.semaphore_signal(barrier, inc=1, device_id=left_id, device_id_type=MESH)

    @pl.when(has_right)
    def _():
        pl.semaphore_signal(barrier, inc=1, device_id=right_id, device_id_type=MESH)

    tail = vec_two.shape[1] - REACH - rows
    for turn in range(3):
        vec_two[turn, pl.ds(REACH + rows, tail), :] = jnp.zeros((tail, 2 * LANES), BF16)

        @pl.when(me == 0)
        def _():
            vec[turn, pl.ds(0, REACH), :] = jnp.zeros((REACH, LANES), F32)

        @pl.when(me == n_smp - 1)
        def _():
            vec[turn, pl.ds(REACH + rows, REACH), :] = jnp.zeros((REACH, LANES), F32)

    def put_vector(turn, tile, value):
        span = pl.ds(pl.multiple_of(REACH + tile * TILE, TILE), TILE)
        vec[turn, span, :] = value
        high, low = split_two(value)
        vec_two[turn, span, 0:LANES] = high
        vec_two[turn, span, LANES : 2 * LANES] = low

    def own_rows(tile):
        return pl.ds(pl.multiple_of(tile * TILE, TILE), TILE)

    def vec_rows(tile):
        return pl.ds(pl.multiple_of(REACH + tile * TILE, TILE), TILE)

    def first_vector(tile, carry):
        put_vector(0, tile, seen[own_rows(tile), :] * zscores[own_rows(tile), :])
        return carry

    lax.fori_loop(0, tiles, first_vector, 0)

    pl.semaphore_wait(
        barrier,
        n_smp - 1 + jnp.where(has_left, 1, 0) + jnp.where(has_right, 1, 0),
    )

    side_copy = pltpu.make_async_remote_copy(
        src_ref=dosage.at[:, pl.ds(0, REACH)],
        dst_ref=dos_side,
        send_sem=side_sem.at[0],
        recv_sem=side_sem.at[1],
        device_id=left_id,
        device_id_type=MESH,
    )

    def halo_copies(turn):
        up = pltpu.make_async_remote_copy(
            src_ref=vec.at[turn, pl.ds(REACH, REACH)],
            dst_ref=vec.at[turn, pl.ds(REACH + rows, REACH)],
            send_sem=vec_send.at[turn, 0],
            recv_sem=vec_recv.at[turn, 0],
            device_id={"smp": jnp.maximum(me - 1, 0)},
            device_id_type=MESH,
        )
        down = pltpu.make_async_remote_copy(
            src_ref=vec.at[turn, pl.ds(rows, REACH)],
            dst_ref=vec.at[turn, pl.ds(0, REACH)],
            send_sem=vec_send.at[turn, 1],
            recv_sem=vec_recv.at[turn, 1],
            device_id={"smp": jnp.minimum(me + 1, n_smp - 1)},
            device_id_type=MESH,
        )
        return up, down

    def send_halos(turn):
        up, down = halo_copies(turn)

        @pl.when(has_prev)
        def _():
            up.start()

        @pl.when(has_next)
        def _():
            down.start()

    def take_halos(turn):
        up, down = halo_copies(turn)

        @pl.when(has_next)
        def _():
            up.wait_recv()

        @pl.when(has_prev)
        def _():
            down.wait_recv()

        for start in (0, REACH + rows):
            high, low = split_two(vec[turn, pl.ds(start, REACH), :])
            vec_two[turn, pl.ds(start, REACH), 0:LANES] = high
            vec_two[turn, pl.ds(start, REACH), LANES : 2 * LANES] = low

    def red_copy(turn, step):
        return pltpu.make_async_remote_copy(
            src_ref=red.at[turn, me],
            dst_ref=red.at[turn, me],
            send_sem=red_send.at[turn, step],
            recv_sem=red_recv.at[turn, step],
            device_id={"smp": lax.rem(me + step, n_smp)},
            device_id_type=MESH,
        )

    def red_arrival(turn, step):
        sender = lax.rem(me - step + n_smp, n_smp)
        return pltpu.make_async_remote_copy(
            src_ref=red.at[turn, sender],
            dst_ref=red.at[turn, sender],
            send_sem=red_send.at[turn, step],
            recv_sem=red_recv.at[turn, step],
            device_id={"smp": lax.rem(me + step, n_smp)},
            device_id_type=MESH,
        )

    def send_sums(turn, sums):
        lines = [total_row(value) for value in sums]
        lines += [jnp.zeros((1, LANES), F32)] * (8 - len(lines))
        red[turn, me] = jnp.concatenate(lines, axis=0)
        for step in range(1, n_smp):
            red_copy(turn, step).start()

    def take_sums(turn):
        for step in range(1, n_smp):
            red_arrival(turn, step).wait_recv()
        whole = red[turn, 0]
        for index in range(1, n_smp):
            whole = whole + red[turn, index]
        return whole

    @pl.when(has_left)
    def _():
        side_copy.start()

    send_halos(0)

    def band_tile(tile, carry):
        flags = tile_flags(band_prev, me * tiles + tile, tile_total)
        here = ld_prev[own_rows(tile), :] * mask_row(flags, TILE, SPAN * TILE)
        here = jnp.concatenate([here, jnp.zeros((TILE, WIDE - SPAN * TILE), F32)], axis=1)
        high, low = split_two(here)
        band_two[tile, 0:TILE, :] = high
        band_two[tile, TILE : 2 * TILE, :] = low
        return carry

    lax.fori_loop(0, tiles, band_tile, 0)

    def normalise(source, source_col, width, global_col, target_col):
        where = pl.ds(pl.multiple_of(global_col, LANES), width)
        mean_part = mean[:, where]
        scale_part = scale[:, where]

        def body(index, carry):
            span = pl.ds(pl.multiple_of(index * STEP, STEP), STEP)
            value = source[span, source_col : source_col + width].astype(F32)
            normed[span, target_col : target_col + width] = (
                (value - mean_part) * scale_part
            ).astype(BF16)
            return carry

        lax.fori_loop(0, samples // STEP, body, 0)

    ready = set()

    def make_ready(chunk):
        if chunk in ready:
            return
        ready.add(chunk)
        if chunk < chunks:
            fetches[order.index(chunk)].wait()
            normalise(dos, chunk * CHUNK, CHUNK, first_col + chunk * CHUNK, chunk * CHUNK)
            return

        @pl.when(has_right)
        def _():
            side_copy.wait_recv()
            normalise(dos_side, 0, REACH, first_col + cols, cols)

        @pl.when(jnp.logical_not(has_right))
        def _():
            normed[:, cols : cols + REACH] = jnp.zeros((samples, REACH), BF16)

    def make_gram(chunk):
        make_ready(chunk)
        make_ready(chunk + 1)
        low = chunk * CHUNK
        own = normed[:, low : low + CHUNK]
        window = normed[:, low : low + CHUNK + REACH]
        part = lax.dot_general(own, window, (((0,), (0,)), ((), ())), preferred_element_type=F32)
        gram[2 * chunk] = part[0:PAIR, 0 : 2 * PAIR]
        gram[2 * chunk + 1] = part[PAIR : 2 * PAIR, PAIR : 3 * PAIR]

    half = n_smp // 2
    first_way = jnp.where(me < half, 0, 1)
    second_way = 1 - first_way
    at_end = (me == 0) | (me == n_smp - 1)

    def running_copy(way, chunk):
        return pltpu.make_async_remote_copy(
            src_ref=moving.at[way, pl.ds(2 * chunk, 2)],
            dst_ref=moving.at[way, pl.ds(2 * chunk, 2)],
            send_sem=mov_send.at[way, chunk],
            recv_sem=mov_recv.at[way, chunk],
            device_id={"smp": jnp.clip(me + 1 - 2 * way, 0, n_smp - 1)},
            device_id_type=MESH,
        )

    def first_pass_end(chunk):
        @pl.when(at_end)
        def _():
            moving[first_way, pl.ds(2 * chunk, 2)] = gram[pl.ds(2 * chunk, 2)]
            running_copy(first_way, chunk).start()

    def first_pass_inner(chunk):
        @pl.when(jnp.logical_not(at_end))
        def _():
            running_copy(first_way, chunk).wait_recv()
            moving[first_way, pl.ds(2 * chunk, 2)] += gram[pl.ds(2 * chunk, 2)]
            running_copy(first_way, chunk).start()

    def edge_copy():
        return pltpu.make_async_remote_copy(
            src_ref=edge_out,
            dst_ref=edge_in,
            send_sem=edge_sem.at[0],
            recv_sem=edge_sem.at[1],
            device_id=right_id,
            device_id_type=MESH,
        )

    def second_pass(chunk):
        span = pl.ds(2 * chunk, 2)
        running_copy(second_way, chunk).wait_recv()
        other = moving[second_way, span]
        summed = moving[first_way, span] + other

        @pl.when(jnp.logical_not(at_end))
        def _():
            moving[second_way, span] = other + gram[span]
            running_copy(second_way, chunk).start()

        gram[span] = summed
        if chunk == chunks - 1:
            edge_out[...] = gram[blocks - 1, :, PAIR : 2 * PAIR]

            @pl.when(has_right)
            def _():
                edge_copy().start()

    def product(turn, tile):
        window = vec_two[turn, pl.ds(pl.multiple_of(tile * TILE, TILE), WIDE), :]
        out = jnp.dot(band_two[tile], window, preferred_element_type=F32)
        value = (out[0:TILE, 0:LANES] + out[TILE:, LANES:]) + (
            out[0:TILE, LANES:] + out[TILE:, 0:LANES]
        )
        image[turn, own_rows(tile), :] = value
        return value

    def operated(turn, tile, vector):
        flag = seen[own_rows(tile), :]
        masked = flag * vector
        return flag * (product(turn, tile) + ridge_term * masked) + (1.0 - flag) * vector

    def over_tiles(turn, body, start):
        inner = max(tiles - 2 * BMAX, 0)
        edges = list(range(min(BMAX, tiles))) + list(range(max(tiles - BMAX, BMAX), tiles))
        carry = start
        if inner:
            unroll = 4 if inner % 4 == 0 else 1
            carry = lax.fori_loop(BMAX, BMAX + inner, body, carry, unroll=unroll)
        take_halos(turn)
        for tile in edges:
            carry = body(tile, carry)
        return carry

    nothing = jnp.zeros((8, LANES), F32)

    def start_solver():
        def body(tile, carry):
            square, cross = carry
            here = vec[0, vec_rows(tile), :]
            out = operated(0, tile, here)
            put_vector(1, tile, seen[own_rows(tile), :] * out)
            return square + folded(here * here), cross + folded(here * out)

        square, cross = over_tiles(0, body, (nothing, nothing))
        send_halos(1)
        send_sums(0, [square, cross])

    def next_solver():
        def body(tile, carry):
            img0[own_rows(tile), :] = operated(1, tile, vec[1, vec_rows(tile), :])
            return carry

        over_tiles(1, body, 0)
        whole = take_sums(0)
        norm0, curve0 = whole[0:1], whole[1:2]
        alpha0 = norm0 / curve0

        def update(tile, carry):
            square, cross, mixed = carry
            r0 = vec[0, vec_rows(tile), :]
            w0 = vec[1, vec_rows(tile), :]
            r1 = r0 - alpha0 * w0
            w1 = w0 - alpha0 * img0[own_rows(tile), :]
            res1[own_rows(tile), :] = r1
            put_vector(2, tile, seen[own_rows(tile), :] * w1)
            return (
                square + folded(r1 * r1),
                cross + folded(r1 * w1),
                mixed + folded(r1 * w0 + r0 * w1),
            )

        sums = lax.fori_loop(0, tiles, update, (nothing, nothing, nothing), unroll=2)
        send_halos(2)
        send_sums(1, list(sums))
        return norm0, curve0, alpha0

    def last_solver(norm0, curve0, alpha0):
        def body(tile, carry):
            here = vec[2, vec_rows(tile), :]
            imputed[own_rows(tile), :] = operated(2, tile, here)
            return carry

        over_tiles(2, body, 0)
        whole = take_sums(1)
        norm1 = whole[0:1]
        beta1 = norm1 / norm0
        curve1 = whole[1:2] + beta1 * whole[2:3] + beta1 * beta1 * curve0
        alpha1 = norm1 / curve1

        def update(tile, carry):
            square, cross, mixed = carry
            r0 = vec[0, vec_rows(tile), :]
            w0 = vec[1, vec_rows(tile), :]
            r1 = res1[own_rows(tile), :]
            w1 = vec[2, vec_rows(tile), :]
            p1 = r1 + beta1 * r0
            s1 = w1 + beta1 * w0
            z1 = imputed[own_rows(tile), :] + beta1 * img0[own_rows(tile), :]
            r2 = r1 - alpha1 * s1
            w2 = w1 - alpha1 * z1
            return (
                square + folded(r2 * r2),
                cross + folded(r2 * w2),
                mixed + folded(r2 * s1 + p1 * w2),
            )

        sums = lax.fori_loop(0, tiles, update, (nothing, nothing, nothing), unroll=2)
        send_sums(2, list(sums))
        return norm1, curve1, alpha1, beta1

    def end_solver(alpha0, norm1, curve1, alpha1, beta1):
        whole = take_sums(2)
        beta2 = whole[0:1] / norm1
        curve2 = whole[1:2] + beta2 * whole[2:3] + beta2 * beta2 * curve1
        alpha2 = whole[0:1] / curve2
        first = (1.0 + beta1, -alpha0)
        second = (
            1.0 + beta2 * first[0],
            -alpha0 - alpha1 * beta1 + beta2 * first[1],
            -alpha1,
        )
        part0 = alpha0 + alpha1 * first[0] + alpha2 * second[0]
        part1 = alpha1 * first[1] + alpha2 * second[1]
        part2 = alpha2 * second[2]

        def body(tile, carry):
            span = own_rows(tile)
            imputed[span, :] = (
                part0 * image[0, span, :] + part1 * image[1, span, :] + part2 * image[2, span, :]
            )
            return carry

        lax.fori_loop(0, tiles, body, 0, unroll=2)

    middle = (chunks + 1) // 2
    for chunk in order[:middle]:
        make_gram(chunk)
        first_pass_end(chunk)
    start_solver()
    for chunk in order[middle:]:
        make_gram(chunk)
        first_pass_end(chunk)
    scalars0 = next_solver()
    for chunk in order:
        first_pass_inner(chunk)
    scalars1 = last_solver(*scalars0)
    for chunk in order[:middle]:
        second_pass(chunk)
    end_solver(scalars0[2], *scalars1)
    for chunk in order[middle:]:
        second_pass(chunk)

    inverse = 1.0 / (samples * n_smp)

    def assemble(block, before):
        turned = jnp.transpose(before)
        tile = 2 * block
        whole = jnp.concatenate([turned, gram[block]], axis=1)
        for side in range(2):
            flags = tile_flags(band_next, place * (cols // TILE) + tile + side, tile_total)
            flags = [flag * inverse for flag in flags]
            part = whole[side * TILE : (side + 1) * TILE]
            if side:
                part = pltpu.roll(part, WIDE - TILE, 1)
            part = part * mask_row(flags, TILE, WIDE)
            ld_next[pl.ds((tile + side) * TILE, TILE), :] = part[:, 0 : SPAN * TILE]

    for block in range(1, blocks):
        assemble(block, gram[block - 1, :, PAIR : 2 * PAIR])

    @pl.when(has_left)
    def _():
        edge_copy().wait_recv()

    @pl.when(jnp.logical_not(has_left))
    def _():
        edge_in[...] = jnp.zeros((PAIR, PAIR), F32)

    assemble(0, edge_in[...])

    @pl.when(has_left)
    def _():
        side_copy.wait_send()

    @pl.when(has_right)
    def _():
        edge_copy().wait_send()

    for turn in range(3):
        up, down = halo_copies(turn)

        @pl.when(has_prev)
        def _():
            up.wait_send()

        @pl.when(has_next)
        def _():
            down.wait_send()

        for step in range(1, n_smp):
            red_copy(turn, step).wait_send()

    for chunk in range(chunks):
        running_copy(first_way, chunk).wait_send()

        @pl.when(jnp.logical_not(at_end))
        def _():
            running_copy(second_way, chunk).wait_send()


def local(sizes, dosage, allele_mean, snp_scale, band_next, ld_prev, band_prev, zscores, observed):
    n_smp = sizes[0]
    samples, cols = dosage.shape
    rows, traits = zscores.shape
    tiles = rows // TILE
    chunks, blocks = cols // CHUNK, cols // PAIR
    seen = jnp.repeat(observed.astype(F32), TBLK, axis=1)
    if traits < LANES:
        seen = jnp.pad(seen, ((0, 0), (0, LANES - traits)))
        zscores = jnp.pad(zscores, ((0, 0), (0, LANES - traits)))
    vmem = pl.BlockSpec(memory_space=pltpu.VMEM)
    smem = pl.BlockSpec(memory_space=pltpu.SMEM)
    dma = pltpu.SemaphoreType.DMA
    ld_next, imputed = pl.pallas_call(
        functools.partial(kernel, sizes),
        out_shape=(
            jax.ShapeDtypeStruct((cols, SPAN * TILE), F32),
            jax.ShapeDtypeStruct((rows, LANES), F32),
        ),
        in_specs=[
            pl.BlockSpec(memory_space=pl.ANY), vmem, vmem, smem, vmem, smem, vmem, vmem,
        ],
        out_specs=(vmem, vmem),
        scratch_shapes=[
            pltpu.VMEM((samples, cols), BF16),
            pltpu.VMEM((samples, REACH), BF16),
            pltpu.VMEM((samples, cols + REACH), BF16),
            pltpu.VMEM((blocks, PAIR, 2 * PAIR), F32),
            pltpu.VMEM((2, blocks, PAIR, 2 * PAIR), F32),
            pltpu.VMEM((PAIR, PAIR), F32),
            pltpu.VMEM((PAIR, PAIR), F32),
            pltpu.VMEM((3, rows + 2 * REACH, LANES), F32),
            pltpu.VMEM((3, rows + 2 * REACH + WIDE - SPAN * TILE, 2 * LANES), BF16),
            pltpu.VMEM((tiles, 2 * TILE, WIDE), BF16),
            pltpu.VMEM((3, rows, LANES), F32),
            pltpu.VMEM((rows, LANES), F32),
            pltpu.VMEM((rows, LANES), F32),
            pltpu.VMEM((3, n_smp, 8, LANES), F32),
            dma((chunks,)),
            dma((2,)),
            dma((3, 2)),
            dma((3, 2)),
            dma((3, n_smp)),
            dma((3, n_smp)),
            dma((2, chunks)),
            dma((2, chunks)),
            dma((2,)),
        ],
        compiler_params=pltpu.CompilerParams(
            collective_id=0, has_side_effects=True, vmem_limit_bytes=48 * 1024 * 1024
        ),
    )(
        dosage,
        allele_mean.reshape(1, -1),
        snp_scale.reshape(1, -1),
        band_next,
        ld_prev,
        band_prev,
        zscores,
        seen,
    )
    return ld_next, imputed[:, :traits]


def solution(mesh):
    sizes = (mesh.shape["smp"], mesh.shape["snp"], mesh.shape["pair"])
    return jax.shard_map(
        functools.partial(local, sizes),
        mesh=mesh,
        in_specs=(
            P(("grp", "smp"), ("snp", "pair")),
            P("grp"),
            P("grp"),
            P("grp"),
            P(("grp", "smp"), None),
            P("grp"),
            P(("grp", "smp"), ("snp", "pair")),
            P(("grp", "smp"), ("snp", "pair")),
        ),
        out_specs=(P(("grp", "snp", "pair"), None), P(("grp", "smp"), ("snp", "pair"))),
        check_vma=False,
    )
```

```python
import functools
import jax
import jax.numpy as jnp
from jax import lax
from jax.sharding import PartitionSpec as P
from jax.experimental import pallas as pl
from jax.experimental.pallas import tpu as pltpu

TILE = 64
BMAX = 2
TBLK = 64
SPAN = 2 * BMAX + 1
REACH = TILE * BMAX
PAIR = 2 * TILE
LANES = 128
WIDE = 384
CHUNK = 256
STEP = 128
CODE_TOP = 32767.0
CODE_LEAST = 1e-30
F32 = jnp.float32
BF16 = jnp.bfloat16
MESH = pl.DeviceIdType.MESH

ridge_term = 1.0


def split_two(value):
    high = value.astype(BF16)
    low = (value - high.astype(F32)).astype(BF16)
    return high, low


def folded(value):
    return jnp.sum(value.reshape(value.shape[0] // 8, 8, value.shape[1]), axis=0)


def total_row(value):
    return jnp.sum(value, axis=0, keepdims=True)


def tile_flags(widths, tile, count):
    here = widths[tile]
    flags = []
    for offset in range(-BMAX, BMAX + 1):
        place = tile + offset
        inside = (place >= 0) & (place < count)
        beside = widths[jnp.clip(place, 0, count - 1)]
        reach = abs(offset)
        flags.append(jnp.where(inside & (here >= reach) & (beside >= reach), 1.0, 0.0).astype(F32))
    return flags


def kernel(
    sizes,
    dosage, mean, scale, band_next, ld_hbm, band_prev, z_hbm, observed,
    ld_next, imputed,
    ld_prev, zscores, seen,
    dos, dos_side, normed, gram, summed, code_out, code_in, peak_out, peak_in, edge_in,
    vec, vec_two, band_two, image, res1, img0, red,
    in_sem, dos_sem, side_sem, vec_send, vec_recv, red_send, red_recv,
    code_send, code_recv, peak_send, peak_recv, edge_sem,
):
    n_smp, n_snp, n_pair = sizes
    samples, cols = dos.shape
    rows = zscores.shape[0]
    tiles = rows // TILE
    chunks = cols // CHUNK
    blocks = cols // PAIR
    row_blocks = rows // PAIR
    tile_total = band_next.shape[0]
    me = lax.axis_index("smp")
    place = lax.axis_index("snp") * n_pair + lax.axis_index("pair")
    places = n_snp * n_pair
    first_col = place * cols
    order = list(range(1, chunks)) + [0]

    def at_place(index):
        return {"snp": index // n_pair, "pair": index % n_pair}

    has_left, has_right = place > 0, place < places - 1
    has_prev, has_next = me > 0, me < n_smp - 1
    left_id = at_place(jnp.maximum(place - 1, 0))
    right_id = at_place(jnp.minimum(place + 1, places - 1))

    z_fetch = pltpu.make_async_copy(z_hbm, zscores, in_sem.at[0])
    ld_fetch = pltpu.make_async_copy(ld_hbm, ld_prev, in_sem.at[1])
    z_fetch.start()
    ld_fetch.start()
    fetches = []
    for chunk in order:
        span = pl.ds(chunk * CHUNK, CHUNK)
        fetch = pltpu.make_async_copy(dosage.at[:, span], dos.at[:, span], dos_sem.at[chunk])
        fetch.start()
        fetches.append(fetch)

    barrier = pltpu.get_barrier_semaphore()
    for step in range(1, n_smp):
        pl.semaphore_signal(
            barrier, inc=1, device_id={"smp": lax.rem(me + step, n_smp)}, device_id_type=MESH
        )

    @pl.when(has_left)
    def _():
        pl.semaphore_signal(barrier, inc=1, device_id=left_id, device_id_type=MESH)

    @pl.when(has_right)
    def _():
        pl.semaphore_signal(barrier, inc=1, device_id=right_id, device_id_type=MESH)

    side_copy = pltpu.make_async_remote_copy(
        src_ref=dosage.at[:, pl.ds(0, REACH)],
        dst_ref=dos_side,
        send_sem=side_sem.at[0],
        recv_sem=side_sem.at[1],
        device_id=left_id,
        device_id_type=MESH,
    )

    for turn in range(3):

        @pl.when(me == 0)
        def _():
            vec[turn, pl.ds(0, REACH), :] = jnp.zeros((REACH, LANES), F32)

        @pl.when(me == n_smp - 1)
        def _():
            vec[turn, pl.ds(REACH + rows, REACH), :] = jnp.zeros((REACH, LANES), F32)

    pl.semaphore_wait(
        barrier,
        n_smp - 1 + jnp.where(has_left, 1, 0) + jnp.where(has_right, 1, 0),
    )

    @pl.when(has_left)
    def _():
        side_copy.start()

    def put_vector(turn, tile, value):
        span = pl.ds(pl.multiple_of(REACH + tile * PAIR, PAIR), PAIR)
        vec[turn, span, :] = value
        high, low = split_two(value)
        vec_two[turn, span, 0:LANES] = high
        vec_two[turn, span, LANES : 2 * LANES] = low

    def own_rows(tile):
        return pl.ds(pl.multiple_of(tile * PAIR, PAIR), PAIR)

    def vec_rows(tile):
        return pl.ds(pl.multiple_of(REACH + tile * PAIR, PAIR), PAIR)

    def halo_copies(turn):
        up = pltpu.make_async_remote_copy(
            src_ref=vec.at[turn, pl.ds(REACH, REACH)],
            dst_ref=vec.at[turn, pl.ds(REACH + rows, REACH)],
            send_sem=vec_send.at[turn, 0],
            recv_sem=vec_recv.at[turn, 0],
            device_id={"smp": jnp.maximum(me - 1, 0)},
            device_id_type=MESH,
        )
        down = pltpu.make_async_remote_copy(
            src_ref=vec.at[turn, pl.ds(rows, REACH)],
            dst_ref=vec.at[turn, pl.ds(0, REACH)],
            send_sem=vec_send.at[turn, 1],
            recv_sem=vec_recv.at[turn, 1],
            device_id={"smp": jnp.minimum(me + 1, n_smp - 1)},
            device_id_type=MESH,
        )
        return up, down

    def send_halos(turn):
        up, down = halo_copies(turn)

        @pl.when(has_prev)
        def _():
            up.start()

        @pl.when(has_next)
        def _():
            down.start()

    def take_halos(turn):
        up, down = halo_copies(turn)

        @pl.when(has_next)
        def _():
            up.wait_recv()

        @pl.when(has_prev)
        def _():
            down.wait_recv()

        for start in (0, REACH + rows):
            high, low = split_two(vec[turn, pl.ds(start, REACH), :])
            vec_two[turn, pl.ds(start, REACH), 0:LANES] = high
            vec_two[turn, pl.ds(start, REACH), LANES : 2 * LANES] = low

    def red_copy(turn, step):
        return pltpu.make_async_remote_copy(
            src_ref=red.at[turn, me],
            dst_ref=red.at[turn, me],
            send_sem=red_send.at[turn, step],
            recv_sem=red_recv.at[turn, step],
            device_id={"smp": lax.rem(me + step, n_smp)},
            device_id_type=MESH,
        )

    def red_arrival(turn, step):
        sender = lax.rem(me - step + n_smp, n_smp)
        return pltpu.make_async_remote_copy(
            src_ref=red.at[turn, sender],
            dst_ref=red.at[turn, sender],
            send_sem=red_send.at[turn, step],
            recv_sem=red_recv.at[turn, step],
            device_id={"smp": lax.rem(me + step, n_smp)},
            device_id_type=MESH,
        )

    def send_sums(turn, sums):
        lines = [total_row(value) for value in sums]
        lines += [jnp.zeros((1, LANES), F32)] * (8 - len(lines))
        red[turn, me] = jnp.concatenate(lines, axis=0)
        for step in range(1, n_smp):
            red_copy(turn, step).start()

    def take_sums(turn):
        for step in range(1, n_smp):
            red_arrival(turn, step).wait_recv()
        whole = red[turn, 0]
        for index in range(1, n_smp):
            whole = whole + red[turn, index]
        return whole

    lane = lax.broadcasted_iota(jnp.int32, (PAIR, LANES), 1)
    line = lax.broadcasted_iota(jnp.int32, (PAIR, LANES), 0)

    z_fetch.wait()
    for tile in range(row_blocks):
        here = observed[:, pl.ds(tile * PAIR, PAIR)].astype(F32)
        flags = jnp.zeros((LANES, PAIR), F32)
        for index in range(here.shape[0]):
            flags = jnp.where(line // TBLK == index, here[index : index + 1], flags)
        flags = jnp.transpose(flags)
        seen[pl.ds(tile * PAIR, PAIR), :] = flags
        put_vector(0, tile, flags * zscores[pl.ds(tile * PAIR, PAIR), :])

    send_halos(0)

    ld_fetch.wait()

    def two_flags(widths, first_tile, factor):
        left = tile_flags(widths, first_tile, tile_total)
        right = tile_flags(widths, first_tile + 1, tile_total)
        first_lanes = lane[0:1] < TILE
        return [jnp.where(first_lanes, a * factor, b * factor) for a, b in zip(left, right)]

    for tile in range(row_blocks):
        flags = two_flags(band_prev, me * tiles + 2 * tile, 1.0)
        columns = pl.ds(tile * PAIR, PAIR)
        parts = [
            ld_prev[pl.ds(index * TILE, TILE), columns] * flag for index, flag in enumerate(flags)
        ]
        blank = jnp.zeros((TILE, PAIR), F32)
        left, right = parts + [blank], [blank] + parts
        for third in range(3):
            pieces = [
                jnp.where(lane[0:TILE] < TILE, left[index], right[index])
                for index in (2 * third, 2 * third + 1)
            ]
            high, low = split_two(jnp.transpose(jnp.concatenate(pieces, axis=0)))
            band_two[tile, 0:PAIR, third * PAIR : (third + 1) * PAIR] = high
            band_two[tile, PAIR : 2 * PAIR, third * PAIR : (third + 1) * PAIR] = low

    def normalise(source, source_col, width, global_col, target_col):
        where = pl.ds(pl.multiple_of(global_col, LANES), width)
        mean_part = mean[:, where]
        scale_part = scale[:, where]

        def body(index, carry):
            span = pl.ds(pl.multiple_of(index * STEP, STEP), STEP)
            value = source[span, source_col : source_col + width].astype(F32)
            normed[span, target_col : target_col + width] = (
                (value - mean_part) * scale_part
            ).astype(BF16)
            return carry

        lax.fori_loop(0, samples // STEP, body, 0)

    ready = set()

    def make_ready(chunk):
        if chunk in ready:
            return
        ready.add(chunk)
        if chunk < chunks:
            fetches[order.index(chunk)].wait()
            normalise(dos, chunk * CHUNK, CHUNK, first_col + chunk * CHUNK, chunk * CHUNK)
            return

        @pl.when(has_right)
        def _():
            side_copy.wait_recv()
            normalise(dos_side, 0, REACH, first_col + cols, cols)

        @pl.when(jnp.logical_not(has_right))
        def _():
            normed[:, cols : cols + REACH] = jnp.zeros((samples, REACH), BF16)

    def make_gram(chunk):
        make_ready(chunk)
        make_ready(chunk + 1)
        low = chunk * CHUNK
        own = normed[:, low : low + CHUNK]
        window = normed[:, low : low + CHUNK + REACH]
        part = lax.dot_general(own, window, (((0,), (0,)), ((), ())), preferred_element_type=F32)
        first, second = part[0:PAIR, 0:PAIR], part[PAIR:, PAIR : 2 * PAIR]
        gram[chunk, 0] = jnp.where(line <= lane, first, second)
        spare = total_row(jnp.where(line == lane, second, 0.0))
        unused = (line < TILE) & (lane >= TILE)
        for side in range(2):
            beside = part[side * PAIR : (side + 1) * PAIR, (side + 1) * PAIR : (side + 2) * PAIR]
            held = spare if side == 0 else pltpu.roll(spare, TILE, 1)
            held = jnp.where(line == 0, held, 0.0)
            gram[chunk, 1 + side] = jnp.where(unused, held, beside)

    half = n_smp // 2
    first_way = jnp.where(me < half, 0, 1)
    second_way = 1 - first_way
    at_end = (me == 0) | (me == n_smp - 1)

    def running_copies(way, chunk):
        ahead = {"smp": jnp.clip(me + 1 - 2 * way, 0, n_smp - 1)}
        return [
            pltpu.make_async_remote_copy(
                src_ref=source.at[way, chunk],
                dst_ref=target.at[way, chunk],
                send_sem=send.at[way, chunk],
                recv_sem=recv.at[way, chunk],
                device_id=ahead,
                device_id_type=MESH,
            )
            for source, target, send, recv in (
                (code_out, code_in, code_send, code_recv),
                (peak_out, peak_in, peak_send, peak_recv),
            )
        ]

    def send_running(way, chunk, values):
        peaks = []
        for index, value in enumerate(values):
            peak = jnp.max(jnp.abs(value), axis=0, keepdims=True)
            factor = CODE_TOP / jnp.maximum(peak, CODE_LEAST)
            code = jnp.round(value * factor).astype(jnp.int32)
            code_out[way, chunk, index] = code.astype(jnp.int16)
            peaks.append(peak)
        peaks += [jnp.zeros((1, LANES), F32)] * (8 - len(peaks))
        peak_out[way, chunk] = jnp.concatenate(peaks, axis=0)
        for copy in running_copies(way, chunk):
            copy.start()

    def take_running(way, chunk):
        for copy in running_copies(way, chunk):
            copy.wait_recv()
        peaks = peak_in[way, chunk] * (1.0 / CODE_TOP)
        return [
            code_in[way, chunk, index].astype(jnp.int32).astype(F32) * peaks[index : index + 1]
            for index in range(3)
        ]

    def first_pass_end(chunk):
        @pl.when(at_end)
        def _():
            values = [gram[chunk, index] for index in range(3)]
            for index in range(3):
                summed[chunk, index] = values[index]
            send_running(first_way, chunk, values)

    def first_pass_inner(chunk):
        @pl.when(jnp.logical_not(at_end))
        def _():
            values = take_running(first_way, chunk)
            values = [value + gram[chunk, index] for index, value in enumerate(values)]
            for index in range(3):
                summed[chunk, index] = values[index]
            send_running(first_way, chunk, values)

    def edge_copy():
        return pltpu.make_async_remote_copy(
            src_ref=summed.at[chunks - 1, 2],
            dst_ref=edge_in,
            send_sem=edge_sem.at[0],
            recv_sem=edge_sem.at[1],
            device_id=right_id,
            device_id_type=MESH,
        )

    def second_pass(chunk):
        values = take_running(second_way, chunk)

        @pl.when(jnp.logical_not(at_end))
        def _():
            send_running(
                second_way,
                chunk,
                [value + gram[chunk, index] for index, value in enumerate(values)],
            )

        for index in range(3):
            summed[chunk, index] += values[index]
        if chunk == chunks - 1:

            @pl.when(has_right)
            def _():
                edge_copy().start()

    def product(turn, tile):
        window = vec_two[turn, pl.ds(pl.multiple_of(tile * PAIR, PAIR), WIDE), :]
        out = jnp.dot(band_two[tile], window, preferred_element_type=F32)
        value = (out[0:PAIR, 0:LANES] + out[PAIR:, LANES:]) + (
            out[0:PAIR, LANES:] + out[PAIR:, 0:LANES]
        )
        image[turn, own_rows(tile), :] = value
        return value

    def operated(turn, tile, vector):
        flag = seen[own_rows(tile), :]
        masked = flag * vector
        return flag * (product(turn, tile) + ridge_term * masked) + (1.0 - flag) * vector

    def over_tiles(turn, body, start):
        inner = max(row_blocks - 2, 0)
        edges = sorted({0, row_blocks - 1})
        carry = start
        if inner:
            unroll = 2 if inner % 2 == 0 else 1
            carry = lax.fori_loop(1, 1 + inner, body, carry, unroll=unroll)
        take_halos(turn)
        for tile in edges:
            carry = body(tile, carry)
        return carry

    nothing = jnp.zeros((8, LANES), F32)

    def start_solver():
        def body(tile, carry):
            square, cross = carry
            here = vec[0, vec_rows(tile), :]
            out = operated(0, tile, here)
            put_vector(1, tile, seen[own_rows(tile), :] * out)
            return square + folded(here * here), cross + folded(here * out)

        square, cross = over_tiles(0, body, (nothing, nothing))
        send_halos(1)
        send_sums(0, [square, cross])

    def next_solver():
        def body(tile, carry):
            img0[own_rows(tile), :] = operated(1, tile, vec[1, vec_rows(tile), :])
            return carry

        over_tiles(1, body, 0)
        whole = take_sums(0)
        norm0, curve0 = whole[0:1], whole[1:2]
        alpha0 = norm0 / curve0

        def update(tile, carry):
            square, cross, mixed = carry
            r0 = vec[0, vec_rows(tile), :]
            w0 = vec[1, vec_rows(tile), :]
            r1 = r0 - alpha0 * w0
            w1 = w0 - alpha0 * img0[own_rows(tile), :]
            res1[own_rows(tile), :] = r1
            put_vector(2, tile, seen[own_rows(tile), :] * w1)
            return (
                square + folded(r1 * r1),
                cross + folded(r1 * w1),
                mixed + folded(r1 * w0 + r0 * w1),
            )

        sums = lax.fori_loop(0, row_blocks, update, (nothing, nothing, nothing))
        send_halos(2)
        send_sums(1, list(sums))
        return norm0, curve0, alpha0

    def last_solver(norm0, curve0, alpha0):
        def body(tile, carry):
            here = vec[2, vec_rows(tile), :]
            imputed[own_rows(tile), :] = operated(2, tile, here)
            return carry

        over_tiles(2, body, 0)
        whole = take_sums(1)
        norm1 = whole[0:1]
        beta1 = norm1 / norm0
        curve1 = whole[1:2] + beta1 * whole[2:3] + beta1 * beta1 * curve0
        alpha1 = norm1 / curve1

        def update(tile, carry):
            square, cross, mixed = carry
            r0 = vec[0, vec_rows(tile), :]
            w0 = vec[1, vec_rows(tile), :]
            r1 = res1[own_rows(tile), :]
            w1 = vec[2, vec_rows(tile), :]
            p1 = r1 + beta1 * r0
            s1 = w1 + beta1 * w0
            z1 = imputed[own_rows(tile), :] + beta1 * img0[own_rows(tile), :]
            r2 = r1 - alpha1 * s1
            w2 = w1 - alpha1 * z1
            return (
                square + folded(r2 * r2),
                cross + folded(r2 * w2),
                mixed + folded(r2 * s1 + p1 * w2),
            )

        sums = lax.fori_loop(0, row_blocks, update, (nothing, nothing, nothing))
        send_sums(2, list(sums))
        return norm1, curve1, alpha1, beta1

    def end_solver(alpha0, norm1, curve1, alpha1, beta1):
        whole = take_sums(2)
        beta2 = whole[0:1] / norm1
        curve2 = whole[1:2] + beta2 * whole[2:3] + beta2 * beta2 * curve1
        alpha2 = whole[0:1] / curve2
        first = (1.0 + beta1, -alpha0)
        second = (
            1.0 + beta2 * first[0],
            -alpha0 - alpha1 * beta1 + beta2 * first[1],
            -alpha1,
        )
        part0 = alpha0 + alpha1 * first[0] + alpha2 * second[0]
        part1 = alpha1 * first[1] + alpha2 * second[1]
        part2 = alpha2 * second[2]

        def body(tile, carry):
            span = own_rows(tile)
            imputed[span, :] = (
                part0 * image[0, span, :] + part1 * image[1, span, :] + part2 * image[2, span, :]
            )
            return carry

        lax.fori_loop(0, row_blocks, body, 0)

    middle = (chunks + 1) // 2
    for chunk in order[:middle]:
        make_gram(chunk)
        first_pass_end(chunk)
    start_solver()
    for chunk in order[middle:]:
        make_gram(chunk)
        first_pass_end(chunk)
    scalars0 = next_solver()
    for chunk in order:
        first_pass_inner(chunk)
    scalars1 = last_solver(*scalars0)
    for chunk in order[:middle]:
        second_pass(chunk)
    end_solver(scalars0[2], *scalars1)

    inverse = 1.0 / (samples * n_smp)

    def assemble(block, before):
        chunk, side = block // 2, block % 2
        packed = summed[chunk, 0]
        turned = jnp.transpose(packed)
        if side:
            spare = jnp.where(
                lane[0:1] >= TILE,
                summed[chunk, 1, 0:1],
                pltpu.roll(summed[chunk, 2, 0:1], TILE, 1),
            )
            diagonal = jnp.where(line > lane, packed, jnp.where(line < lane, turned, spare))
        else:
            diagonal = jnp.where(line <= lane, packed, turned)
        after = jnp.transpose(summed[chunk, 1 + side])
        stack = [before[0:TILE], before[TILE:], diagonal[0:TILE], diagonal[TILE:]]
        stack += [after[0:TILE], after[TILE:]]
        flags = two_flags(band_next, place * (cols // TILE) + 2 * block, inverse)
        for index, flag in enumerate(flags):
            value = jnp.where(lane[0:TILE] < TILE, stack[index], stack[index + 1])
            ld_next[pl.ds(index * TILE, TILE), pl.ds(block * PAIR, PAIR)] = value * flag

    done = set()

    def assemble_ready():
        for block in range(1, blocks):
            needed = {block // 2, (block - 1) // 2}
            if block not in assembled and needed <= done:
                assembled.add(block)
                assemble(block, summed[(block - 1) // 2, 1 + (block - 1) % 2])

    assembled = set()
    for chunk in order[:middle]:
        done.add(chunk)
    assemble_ready()
    for chunk in order[middle:]:
        second_pass(chunk)
        done.add(chunk)
        assemble_ready()

    @pl.when(has_left)
    def _():
        edge_copy().wait_recv()

    @pl.when(jnp.logical_not(has_left))
    def _():
        edge_in[...] = jnp.zeros((PAIR, PAIR), F32)

    assemble(0, edge_in[...])

    @pl.when(has_left)
    def _():
        side_copy.wait_send()

    @pl.when(has_right)
    def _():
        edge_copy().wait_send()

    for turn in range(3):
        up, down = halo_copies(turn)

        @pl.when(has_prev)
        def _():
            up.wait_send()

        @pl.when(has_next)
        def _():
            down.wait_send()

        for step in range(1, n_smp):
            red_copy(turn, step).wait_send()

    for chunk in range(chunks):
        for copy in running_copies(first_way, chunk):
            copy.wait_send()

        @pl.when(jnp.logical_not(at_end))
        def _():
            for copy in running_copies(second_way, chunk):
                copy.wait_send()


def local(sizes, dosage, allele_mean, snp_scale, band_next, ld_prev, band_prev, zscores, observed):
    n_smp = sizes[0]
    samples, cols = dosage.shape
    rows, traits = zscores.shape
    chunks = cols // CHUNK
    if traits < LANES:
        zscores = jnp.pad(zscores, ((0, 0), (0, LANES - traits)))
    vmem = pl.BlockSpec(memory_space=pltpu.VMEM)
    far = pl.BlockSpec(memory_space=pl.ANY)
    smem = pl.BlockSpec(memory_space=pltpu.SMEM)
    dma = pltpu.SemaphoreType.DMA
    ld_next, imputed = pl.pallas_call(
        functools.partial(kernel, sizes),
        out_shape=(
            jax.ShapeDtypeStruct((SPAN * TILE, cols), F32),
            jax.ShapeDtypeStruct((rows, LANES), F32),
        ),
        in_specs=[
            far, vmem, vmem, smem, far, smem, far, vmem,
        ],
        out_specs=(vmem, vmem),
        scratch_shapes=[
            pltpu.VMEM((SPAN * TILE, rows), F32),
            pltpu.VMEM((rows, LANES), F32),
            pltpu.VMEM((rows, LANES), F32),
            pltpu.VMEM((samples, cols), BF16),
            pltpu.VMEM((samples, REACH), BF16),
            pltpu.VMEM((samples, cols + REACH), BF16),
            pltpu.VMEM((chunks, 3, PAIR, PAIR), F32),
            pltpu.VMEM((chunks, 3, PAIR, PAIR), F32),
            pltpu.VMEM((2, chunks, 3, PAIR, PAIR), jnp.int16),
            pltpu.VMEM((2, chunks, 3, PAIR, PAIR), jnp.int16),
            pltpu.VMEM((2, chunks, 8, PAIR), F32),
            pltpu.VMEM((2, chunks, 8, PAIR), F32),
            pltpu.VMEM((PAIR, PAIR), F32),
            pltpu.VMEM((3, rows + 2 * REACH, LANES), F32),
            pltpu.VMEM((3, rows + 2 * REACH, 2 * LANES), BF16),
            pltpu.VMEM((rows // PAIR, 2 * PAIR, WIDE), BF16),
            pltpu.VMEM((3, rows, LANES), F32),
            pltpu.VMEM((rows, LANES), F32),
            pltpu.VMEM((rows, LANES), F32),
            pltpu.VMEM((3, n_smp, 8, LANES), F32),
            dma((2,)),
            dma((chunks,)),
            dma((2,)),
            dma((3, 2)),
            dma((3, 2)),
            dma((3, n_smp)),
            dma((3, n_smp)),
            dma((2, chunks)),
            dma((2, chunks)),
            dma((2, chunks)),
            dma((2, chunks)),
            dma((2,)),
        ],
        compiler_params=pltpu.CompilerParams(
            collective_id=0, has_side_effects=True, vmem_limit_bytes=48 * 1024 * 1024
        ),
    )(
        dosage,
        allele_mean.reshape(1, -1),
        snp_scale.reshape(1, -1),
        band_next,
        jnp.transpose(ld_prev),
        band_prev,
        zscores,
        jnp.transpose(observed),
    )
    return jnp.transpose(ld_next), imputed[:, :traits]


def solution(mesh):
    sizes = (mesh.shape["smp"], mesh.shape["snp"], mesh.shape["pair"])
    return jax.shard_map(
        functools.partial(local, sizes),
        mesh=mesh,
        in_specs=(
            P(("grp", "smp"), ("snp", "pair")),
            P("grp"),
            P("grp"),
            P("grp"),
            P(("grp", "smp"), None),
            P("grp"),
            P(("grp", "smp"), ("snp", "pair")),
            P(("grp", "smp"), ("snp", "pair")),
        ),
        out_specs=(P(("grp", "snp", "pair"), None), P(("grp", "smp"), ("snp", "pair"))),
        check_vma=False,
    )
```

```python
import functools
import jax
import jax.numpy as jnp
from jax import lax
from jax.sharding import PartitionSpec as P
from jax.experimental import pallas as pl
from jax.experimental.pallas import tpu as pltpu

TILE = 64
BMAX = 2
TBLK = 64
SPAN = 2 * BMAX + 1
REACH = TILE * BMAX
PAIR = 2 * TILE
LANES = 128
WIDE = 384
CHUNK = 256
STEP = 128
CODE_TOP = 32767.0
CODE_LEAST = 1e-30
F32 = jnp.float32
BF16 = jnp.bfloat16
MESH = pl.DeviceIdType.MESH

ridge_term = 1.0


def split_two(value):
    high = value.astype(BF16)
    low = (value - high.astype(F32)).astype(BF16)
    return high, low


def folded(value):
    return jnp.sum(value.reshape(value.shape[0] // 8, 8, value.shape[1]), axis=0)


def total_row(value):
    return jnp.sum(value, axis=0, keepdims=True)


def tile_flags(widths, tile, count):
    here = widths[tile]
    flags = []
    for offset in range(-BMAX, BMAX + 1):
        place = tile + offset
        inside = (place >= 0) & (place < count)
        beside = widths[jnp.clip(place, 0, count - 1)]
        reach = abs(offset)
        flags.append(jnp.where(inside & (here >= reach) & (beside >= reach), 1.0, 0.0).astype(F32))
    return flags


def kernel(
    sizes,
    dosage, mean_far, scale_far, next_far, ld_far, prev_far, z_far, observed_far,
    ld_out, imputed_out,
    ld_next, imputed,
    mean, scale, band_next, ld_prev, band_prev, zscores, observed, seen,
    dos, dos_side, normed, gram, summed, code_out, code_in, peak_out, peak_in, edge_in,
    vec, vec_two, band_two, image, res1, img0, red,
    in_sem, dos_sem, side_sem, vec_send, vec_recv, red_send, red_recv,
    code_send, code_recv, peak_send, peak_recv, edge_sem, out_sem,
):
    n_smp, n_snp, n_pair = sizes
    samples, cols = dos.shape
    rows = zscores.shape[0]
    tiles = rows // TILE
    chunks = cols // CHUNK
    blocks = cols // PAIR
    row_blocks = rows // PAIR
    tile_total = band_next.shape[0]
    me = lax.axis_index("smp")
    place = lax.axis_index("snp") * n_pair + lax.axis_index("pair")
    places = n_snp * n_pair
    first_col = place * cols
    order = list(range(1, chunks)) + [0]

    def at_place(index):
        return {"snp": index // n_pair, "pair": index % n_pair}

    has_left, has_right = place > 0, place < places - 1
    has_prev, has_next = me > 0, me < n_smp - 1
    left_id = at_place(jnp.maximum(place - 1, 0))
    right_id = at_place(jnp.minimum(place + 1, places - 1))

    small = []
    for index, (far, near) in enumerate(
        (
            (z_far, zscores),
            (observed_far, observed),
            (prev_far, band_prev),
            (ld_far, ld_prev),
            (mean_far, mean),
            (scale_far, scale),
            (next_far, band_next),
        )
    ):
        small.append(pltpu.make_async_copy(far, near, in_sem.at[index]))
        small[-1].start()
    fetches = []
    for chunk in order:
        span = pl.ds(chunk * CHUNK, CHUNK)
        fetch = pltpu.make_async_copy(dosage.at[:, span], dos.at[:, span], dos_sem.at[chunk])
        fetch.start()
        fetches.append(fetch)

    barrier = pltpu.get_barrier_semaphore()
    for step in range(1, n_smp):
        pl.semaphore_signal(
            barrier, inc=1, device_id={"smp": lax.rem(me + step, n_smp)}, device_id_type=MESH
        )

    @pl.when(has_left)
    def _():
        pl.semaphore_signal(barrier, inc=1, device_id=left_id, device_id_type=MESH)

    @pl.when(has_right)
    def _():
        pl.semaphore_signal(barrier, inc=1, device_id=right_id, device_id_type=MESH)

    side_copy = pltpu.make_async_remote_copy(
        src_ref=dosage.at[:, pl.ds(0, REACH)],
        dst_ref=dos_side,
        send_sem=side_sem.at[0],
        recv_sem=side_sem.at[1],
        device_id=left_id,
        device_id_type=MESH,
    )

    for turn in range(3):

        @pl.when(me == 0)
        def _():
            vec[turn, pl.ds(0, REACH), :] = jnp.zeros((REACH, LANES), F32)

        @pl.when(me == n_smp - 1)
        def _():
            vec[turn, pl.ds(REACH + rows, REACH), :] = jnp.zeros((REACH, LANES), F32)

    def put_vector(turn, tile, value):
        span = pl.ds(pl.multiple_of(REACH + tile * PAIR, PAIR), PAIR)
        vec[turn, span, :] = value
        high, low = split_two(value)
        vec_two[turn, span, 0:LANES] = high
        vec_two[turn, span, LANES : 2 * LANES] = low

    def own_rows(tile):
        return pl.ds(pl.multiple_of(tile * PAIR, PAIR), PAIR)

    def vec_rows(tile):
        return pl.ds(pl.multiple_of(REACH + tile * PAIR, PAIR), PAIR)

    def halo_copies(turn):
        up = pltpu.make_async_remote_copy(
            src_ref=vec.at[turn, pl.ds(REACH, REACH)],
            dst_ref=vec.at[turn, pl.ds(REACH + rows, REACH)],
            send_sem=vec_send.at[turn, 0],
            recv_sem=vec_recv.at[turn, 0],
            device_id={"smp": jnp.maximum(me - 1, 0)},
            device_id_type=MESH,
        )
        down = pltpu.make_async_remote_copy(
            src_ref=vec.at[turn, pl.ds(rows, REACH)],
            dst_ref=vec.at[turn, pl.ds(0, REACH)],
            send_sem=vec_send.at[turn, 1],
            recv_sem=vec_recv.at[turn, 1],
            device_id={"smp": jnp.minimum(me + 1, n_smp - 1)},
            device_id_type=MESH,
        )
        return up, down

    def send_halos(turn):
        up, down = halo_copies(turn)

        @pl.when(has_prev)
        def _():
            up.start()

        @pl.when(has_next)
        def _():
            down.start()

    def take_halos(turn):
        up, down = halo_copies(turn)

        @pl.when(has_next)
        def _():
            up.wait_recv()

        @pl.when(has_prev)
        def _():
            down.wait_recv()

        for start in (0, REACH + rows):
            high, low = split_two(vec[turn, pl.ds(start, REACH), :])
            vec_two[turn, pl.ds(start, REACH), 0:LANES] = high
            vec_two[turn, pl.ds(start, REACH), LANES : 2 * LANES] = low

    def red_copy(turn, step):
        return pltpu.make_async_remote_copy(
            src_ref=red.at[turn, me],
            dst_ref=red.at[turn, me],
            send_sem=red_send.at[turn, step],
            recv_sem=red_recv.at[turn, step],
            device_id={"smp": lax.rem(me + step, n_smp)},
            device_id_type=MESH,
        )

    def red_arrival(turn, step):
        sender = lax.rem(me - step + n_smp, n_smp)
        return pltpu.make_async_remote_copy(
            src_ref=red.at[turn, sender],
            dst_ref=red.at[turn, sender],
            send_sem=red_send.at[turn, step],
            recv_sem=red_recv.at[turn, step],
            device_id={"smp": lax.rem(me + step, n_smp)},
            device_id_type=MESH,
        )

    def send_sums(turn, sums):
        lines = [total_row(value) for value in sums]
        lines += [jnp.zeros((1, LANES), F32)] * (8 - len(lines))
        red[turn, me] = jnp.concatenate(lines, axis=0)
        for step in range(1, n_smp):
            red_copy(turn, step).start()

    def take_sums(turn):
        for step in range(1, n_smp):
            red_arrival(turn, step).wait_recv()
        whole = red[turn, 0]
        for index in range(1, n_smp):
            whole = whole + red[turn, index]
        return whole

    lane = lax.broadcasted_iota(jnp.int32, (PAIR, LANES), 1)
    line = lax.broadcasted_iota(jnp.int32, (PAIR, LANES), 0)

    small[0].wait()
    small[1].wait()
    for tile in range(row_blocks):
        here = observed[:, pl.ds(tile * PAIR, PAIR)].astype(F32)
        flags = jnp.zeros((LANES, PAIR), F32)
        for index in range(here.shape[0]):
            flags = jnp.where(line // TBLK == index, here[index : index + 1], flags)
        flags = jnp.transpose(flags)
        seen[pl.ds(tile * PAIR, PAIR), :] = flags
        put_vector(0, tile, flags * zscores[pl.ds(tile * PAIR, PAIR), :])

    pl.semaphore_wait(
        barrier,
        n_smp - 1 + jnp.where(has_left, 1, 0) + jnp.where(has_right, 1, 0),
    )

    @pl.when(has_left)
    def _():
        side_copy.start()

    send_halos(0)

    small[2].wait()
    small[3].wait()

    def two_flags(widths, first_tile, factor):
        left = tile_flags(widths, first_tile, tile_total)
        right = tile_flags(widths, first_tile + 1, tile_total)
        first_lanes = lane[0:1] < TILE
        return [jnp.where(first_lanes, a * factor, b * factor) for a, b in zip(left, right)]

    for tile in range(row_blocks):
        flags = two_flags(band_prev, me * tiles + 2 * tile, 1.0)
        columns = pl.ds(tile * PAIR, PAIR)
        parts = [
            ld_prev[pl.ds(index * TILE, TILE), columns] * flag for index, flag in enumerate(flags)
        ]
        blank = jnp.zeros((TILE, PAIR), F32)
        left, right = parts + [blank], [blank] + parts
        for third in range(3):
            pieces = [
                jnp.where(lane[0:TILE] < TILE, left[index], right[index])
                for index in (2 * third, 2 * third + 1)
            ]
            high, low = split_two(jnp.transpose(jnp.concatenate(pieces, axis=0)))
            band_two[tile, 0:PAIR, third * PAIR : (third + 1) * PAIR] = high
            band_two[tile, PAIR : 2 * PAIR, third * PAIR : (third + 1) * PAIR] = low

    for copy in small[4:]:
        copy.wait()

    def normalise(source, source_col, width, global_col, target_col):
        where = pl.ds(pl.multiple_of(global_col, LANES), width)
        mean_part = mean[:, where]
        scale_part = scale[:, where]

        def body(index, carry):
            span = pl.ds(pl.multiple_of(index * STEP, STEP), STEP)
            value = source[span, source_col : source_col + width].astype(F32)
            normed[span, target_col : target_col + width] = (
                (value - mean_part) * scale_part
            ).astype(BF16)
            return carry

        lax.fori_loop(0, samples // STEP, body, 0)

    ready = set()

    def make_ready(chunk):
        if chunk in ready:
            return
        ready.add(chunk)
        if chunk < chunks:
            fetches[order.index(chunk)].wait()
            normalise(dos, chunk * CHUNK, CHUNK, first_col + chunk * CHUNK, chunk * CHUNK)
            return

        @pl.when(has_right)
        def _():
            side_copy.wait_recv()
            normalise(dos_side, 0, REACH, first_col + cols, cols)

        @pl.when(jnp.logical_not(has_right))
        def _():
            normed[:, cols : cols + REACH] = jnp.zeros((samples, REACH), BF16)

    def make_gram(chunk):
        make_ready(chunk)
        make_ready(chunk + 1)
        low = chunk * CHUNK
        own = normed[:, low : low + CHUNK]
        window = normed[:, low : low + CHUNK + REACH]
        part = lax.dot_general(own, window, (((0,), (0,)), ((), ())), preferred_element_type=F32)
        first, second = part[0:PAIR, 0:PAIR], part[PAIR:, PAIR : 2 * PAIR]
        gram[chunk, 0] = jnp.where(line <= lane, first, second)
        spare = total_row(jnp.where(line == lane, second, 0.0))
        unused = (line < TILE) & (lane >= TILE)
        for side in range(2):
            beside = part[side * PAIR : (side + 1) * PAIR, (side + 1) * PAIR : (side + 2) * PAIR]
            held = spare if side == 0 else pltpu.roll(spare, TILE, 1)
            held = jnp.where(line == 0, held, 0.0)
            gram[chunk, 1 + side] = jnp.where(unused, held, beside)

    half = n_smp // 2
    first_way = jnp.where(me < half, 0, 1)
    second_way = 1 - first_way
    at_end = (me == 0) | (me == n_smp - 1)

    def running_copies(way, chunk):
        ahead = {"smp": jnp.clip(me + 1 - 2 * way, 0, n_smp - 1)}
        return [
            pltpu.make_async_remote_copy(
                src_ref=source.at[way, chunk],
                dst_ref=target.at[way, chunk],
                send_sem=send.at[way, chunk],
                recv_sem=recv.at[way, chunk],
                device_id=ahead,
                device_id_type=MESH,
            )
            for source, target, send, recv in (
                (code_out, code_in, code_send, code_recv),
                (peak_out, peak_in, peak_send, peak_recv),
            )
        ]

    def send_running(way, chunk, values):
        peaks = []
        for index, value in enumerate(values):
            peak = jnp.max(jnp.abs(value), axis=0, keepdims=True)
            factor = CODE_TOP / jnp.maximum(peak, CODE_LEAST)
            code = jnp.round(value * factor).astype(jnp.int32)
            code_out[way, chunk, index] = code.astype(jnp.int16)
            peaks.append(peak)
        peaks += [jnp.zeros((1, LANES), F32)] * (8 - len(peaks))
        peak_out[way, chunk] = jnp.concatenate(peaks, axis=0)
        for copy in running_copies(way, chunk):
            copy.start()

    def take_running(way, chunk):
        for copy in running_copies(way, chunk):
            copy.wait_recv()
        peaks = peak_in[way, chunk] * (1.0 / CODE_TOP)
        return [
            code_in[way, chunk, index].astype(jnp.int32).astype(F32) * peaks[index : index + 1]
            for index in range(3)
        ]

    def first_pass_end(chunk):
        @pl.when(at_end)
        def _():
            values = [gram[chunk, index] for index in range(3)]
            for index in range(3):
                summed[chunk, index] = values[index]
            send_running(first_way, chunk, values)

    def first_pass_inner(chunk):
        @pl.when(jnp.logical_not(at_end))
        def _():
            values = take_running(first_way, chunk)
            values = [value + gram[chunk, index] for index, value in enumerate(values)]
            for index in range(3):
                summed[chunk, index] = values[index]
            send_running(first_way, chunk, values)

    def edge_copy():
        return pltpu.make_async_remote_copy(
            src_ref=summed.at[chunks - 1, 2],
            dst_ref=edge_in,
            send_sem=edge_sem.at[0],
            recv_sem=edge_sem.at[1],
            device_id=right_id,
            device_id_type=MESH,
        )

    def second_pass(chunk):
        values = take_running(second_way, chunk)

        @pl.when(jnp.logical_not(at_end))
        def _():
            send_running(
                second_way,
                chunk,
                [value + gram[chunk, index] for index, value in enumerate(values)],
            )

        for index in range(3):
            summed[chunk, index] += values[index]
        if chunk == chunks - 1:

            @pl.when(has_right)
            def _():
                edge_copy().start()

    def product(turn, tile):
        window = vec_two[turn, pl.ds(pl.multiple_of(tile * PAIR, PAIR), WIDE), :]
        out = jnp.dot(band_two[tile], window, preferred_element_type=F32)
        value = (out[0:PAIR, 0:LANES] + out[PAIR:, LANES:]) + (
            out[0:PAIR, LANES:] + out[PAIR:, 0:LANES]
        )
        image[turn, own_rows(tile), :] = value
        return value

    def operated(turn, tile, vector):
        flag = seen[own_rows(tile), :]
        masked = flag * vector
        return flag * (product(turn, tile) + ridge_term * masked) + (1.0 - flag) * vector

    def over_tiles(turn, body, start):
        inner = max(row_blocks - 2, 0)
        edges = sorted({0, row_blocks - 1})
        carry = start
        if inner:
            unroll = 2 if inner % 2 == 0 else 1
            carry = lax.fori_loop(1, 1 + inner, body, carry, unroll=unroll)
        take_halos(turn)
        for tile in edges:
            carry = body(tile, carry)
        return carry

    nothing = jnp.zeros((8, LANES), F32)

    def start_solver():
        def body(tile, carry):
            square, cross = carry
            here = vec[0, vec_rows(tile), :]
            out = operated(0, tile, here)
            put_vector(1, tile, seen[own_rows(tile), :] * out)
            return square + folded(here * here), cross + folded(here * out)

        square, cross = over_tiles(0, body, (nothing, nothing))
        send_halos(1)
        send_sums(0, [square, cross])

    def next_solver():
        def body(tile, carry):
            img0[own_rows(tile), :] = operated(1, tile, vec[1, vec_rows(tile), :])
            return carry

        over_tiles(1, body, 0)
        whole = take_sums(0)
        norm0, curve0 = whole[0:1], whole[1:2]
        alpha0 = norm0 / curve0

        def update(tile, carry):
            square, cross, mixed = carry
            r0 = vec[0, vec_rows(tile), :]
            w0 = vec[1, vec_rows(tile), :]
            r1 = r0 - alpha0 * w0
            w1 = w0 - alpha0 * img0[own_rows(tile), :]
            res1[own_rows(tile), :] = r1
            put_vector(2, tile, seen[own_rows(tile), :] * w1)
            return (
                square + folded(r1 * r1),
                cross + folded(r1 * w1),
                mixed + folded(r1 * w0 + r0 * w1),
            )

        sums = lax.fori_loop(0, row_blocks, update, (nothing, nothing, nothing))
        send_halos(2)
        send_sums(1, list(sums))
        return norm0, curve0, alpha0

    def last_solver(norm0, curve0, alpha0):
        def body(tile, carry):
            here = vec[2, vec_rows(tile), :]
            imputed[own_rows(tile), :] = operated(2, tile, here)
            return carry

        over_tiles(2, body, 0)
        whole = take_sums(1)
        norm1 = whole[0:1]
        beta1 = norm1 / norm0
        curve1 = whole[1:2] + beta1 * whole[2:3] + beta1 * beta1 * curve0
        alpha1 = norm1 / curve1

        def update(tile, carry):
            square, cross, mixed = carry
            r0 = vec[0, vec_rows(tile), :]
            w0 = vec[1, vec_rows(tile), :]
            r1 = res1[own_rows(tile), :]
            w1 = vec[2, vec_rows(tile), :]
            p1 = r1 + beta1 * r0
            s1 = w1 + beta1 * w0
            z1 = imputed[own_rows(tile), :] + beta1 * img0[own_rows(tile), :]
            r2 = r1 - alpha1 * s1
            w2 = w1 - alpha1 * z1
            return (
                square + folded(r2 * r2),
                cross + folded(r2 * w2),
                mixed + folded(r2 * s1 + p1 * w2),
            )

        sums = lax.fori_loop(0, row_blocks, update, (nothing, nothing, nothing))
        send_sums(2, list(sums))
        return norm1, curve1, alpha1, beta1

    def end_solver(alpha0, norm1, curve1, alpha1, beta1):
        whole = take_sums(2)
        beta2 = whole[0:1] / norm1
        curve2 = whole[1:2] + beta2 * whole[2:3] + beta2 * beta2 * curve1
        alpha2 = whole[0:1] / curve2
        first = (1.0 + beta1, -alpha0)
        second = (
            1.0 + beta2 * first[0],
            -alpha0 - alpha1 * beta1 + beta2 * first[1],
            -alpha1,
        )
        part0 = alpha0 + alpha1 * first[0] + alpha2 * second[0]
        part1 = alpha1 * first[1] + alpha2 * second[1]
        part2 = alpha2 * second[2]

        def body(tile, carry):
            span = own_rows(tile)
            imputed[span, :] = (
                part0 * image[0, span, :] + part1 * image[1, span, :] + part2 * image[2, span, :]
            )
            return carry

        lax.fori_loop(0, row_blocks, body, 0)

    def make_and_send(chunk):
        make_gram(chunk)
        first_pass_end(chunk)

    middle = (chunks + 1) // 2
    make_and_send(order[0])
    start_solver()
    for chunk in order[1:middle]:
        make_and_send(chunk)
    scalars0 = next_solver()
    for chunk in order[middle:]:
        make_and_send(chunk)
    for chunk in order[:middle]:
        first_pass_inner(chunk)
    scalars1 = last_solver(*scalars0)
    for chunk in order[middle:]:
        first_pass_inner(chunk)
    for chunk in order[:middle]:
        second_pass(chunk)
    end_solver(scalars0[2], *scalars1)
    results = [pltpu.make_async_copy(imputed, imputed_out, out_sem.at[blocks])]
    results[0].start()

    inverse = 1.0 / (samples * n_smp)

    def assemble(block, before):
        chunk, side = block // 2, block % 2
        packed = summed[chunk, 0]
        turned = jnp.transpose(packed)
        if side:
            spare = jnp.where(
                lane[0:1] >= TILE,
                summed[chunk, 1, 0:1],
                pltpu.roll(summed[chunk, 2, 0:1], TILE, 1),
            )
            diagonal = jnp.where(line > lane, packed, jnp.where(line < lane, turned, spare))
        else:
            diagonal = jnp.where(line <= lane, packed, turned)
        after = jnp.transpose(summed[chunk, 1 + side])
        stack = [before[0:TILE], before[TILE:], diagonal[0:TILE], diagonal[TILE:]]
        stack += [after[0:TILE], after[TILE:]]
        flags = two_flags(band_next, place * (cols // TILE) + 2 * block, inverse)
        for index, flag in enumerate(flags):
            value = jnp.where(lane[0:TILE] < TILE, stack[index], stack[index + 1])
            ld_next[pl.ds(index * TILE, TILE), pl.ds(block * PAIR, PAIR)] = value * flag
        columns = pl.ds(block * PAIR, PAIR)
        results.append(
            pltpu.make_async_copy(ld_next.at[:, columns], ld_out.at[:, columns], out_sem.at[block])
        )
        results[-1].start()

    done = set()

    def assemble_ready():
        for block in range(1, blocks):
            needed = {block // 2, (block - 1) // 2}
            if block not in assembled and needed <= done:
                assembled.add(block)
                assemble(block, summed[(block - 1) // 2, 1 + (block - 1) % 2])

    assembled = set()
    for chunk in order[:middle]:
        done.add(chunk)
    assemble_ready()
    for chunk in order[middle:]:
        second_pass(chunk)
        done.add(chunk)
        assemble_ready()

    @pl.when(has_left)
    def _():
        edge_copy().wait_recv()

    @pl.when(jnp.logical_not(has_left))
    def _():
        edge_in[...] = jnp.zeros((PAIR, PAIR), F32)

    assemble(0, edge_in[...])

    for copy in results:
        copy.wait()

    @pl.when(has_left)
    def _():
        side_copy.wait_send()

    @pl.when(has_right)
    def _():
        edge_copy().wait_send()

    for turn in range(3):
        up, down = halo_copies(turn)

        @pl.when(has_prev)
        def _():
            up.wait_send()

        @pl.when(has_next)
        def _():
            down.wait_send()

        for step in range(1, n_smp):
            red_copy(turn, step).wait_send()

    for chunk in range(chunks):
        for copy in running_copies(first_way, chunk):
            copy.wait_send()

        @pl.when(jnp.logical_not(at_end))
        def _():
            for copy in running_copies(second_way, chunk):
                copy.wait_send()


def local(sizes, dosage, allele_mean, snp_scale, band_next, ld_prev, band_prev, zscores, observed):
    n_smp = sizes[0]
    samples, cols = dosage.shape
    rows, traits = zscores.shape
    chunks = cols // CHUNK
    if traits < LANES:
        zscores = jnp.pad(zscores, ((0, 0), (0, LANES - traits)))
    far = pl.BlockSpec(memory_space=pltpu.HBM)
    dma = pltpu.SemaphoreType.DMA
    ld_next, imputed = pl.pallas_call(
        functools.partial(kernel, sizes),
        out_shape=(
            jax.ShapeDtypeStruct((SPAN * TILE, cols), F32),
            jax.ShapeDtypeStruct((rows, LANES), F32),
        ),
        in_specs=[far] * 8,
        out_specs=(far, far),
        scratch_shapes=[
            pltpu.VMEM((SPAN * TILE, cols), F32),
            pltpu.VMEM((rows, LANES), F32),
            pltpu.VMEM((1, allele_mean.shape[0]), F32),
            pltpu.VMEM((1, allele_mean.shape[0]), F32),
            pltpu.SMEM(band_next.shape, jnp.int32),
            pltpu.VMEM((SPAN * TILE, rows), F32),
            pltpu.SMEM(band_prev.shape, jnp.int32),
            pltpu.VMEM((rows, LANES), F32),
            pltpu.VMEM((observed.shape[1], rows), jnp.int32),
            pltpu.VMEM((rows, LANES), F32),
            pltpu.VMEM((samples, cols), BF16),
            pltpu.VMEM((samples, REACH), BF16),
            pltpu.VMEM((samples, cols + REACH), BF16),
            pltpu.VMEM((chunks, 3, PAIR, PAIR), F32),
            pltpu.VMEM((chunks, 3, PAIR, PAIR), F32),
            pltpu.VMEM((2, chunks, 3, PAIR, PAIR), jnp.int16),
            pltpu.VMEM((2, chunks, 3, PAIR, PAIR), jnp.int16),
            pltpu.VMEM((2, chunks, 8, PAIR), F32),
            pltpu.VMEM((2, chunks, 8, PAIR), F32),
            pltpu.VMEM((PAIR, PAIR), F32),
            pltpu.VMEM((3, rows + 2 * REACH, LANES), F32),
            pltpu.VMEM((3, rows + 2 * REACH, 2 * LANES), BF16),
            pltpu.VMEM((rows // PAIR, 2 * PAIR, WIDE), BF16),
            pltpu.VMEM((3, rows, LANES), F32),
            pltpu.VMEM((rows, LANES), F32),
            pltpu.VMEM((rows, LANES), F32),
            pltpu.VMEM((3, n_smp, 8, LANES), F32),
            dma((7,)),
            dma((chunks,)),
            dma((2,)),
            dma((3, 2)),
            dma((3, 2)),
            dma((3, n_smp)),
            dma((3, n_smp)),
            dma((2, chunks)),
            dma((2, chunks)),
            dma((2, chunks)),
            dma((2, chunks)),
            dma((2,)),
            dma((cols // PAIR + 1,)),
        ],
        compiler_params=pltpu.CompilerParams(
            collective_id=0, has_side_effects=True, vmem_limit_bytes=60 * 1024 * 1024
        ),
    )(
        dosage,
        allele_mean.reshape(1, -1),
        snp_scale.reshape(1, -1),
        band_next,
        jnp.transpose(ld_prev),
        band_prev,
        zscores,
        jnp.transpose(observed),
    )
    return jnp.transpose(ld_next), imputed[:, :traits]


def solution(mesh):
    sizes = (mesh.shape["smp"], mesh.shape["snp"], mesh.shape["pair"])
    return jax.shard_map(
        functools.partial(local, sizes),
        mesh=mesh,
        in_specs=(
            P(("grp", "smp"), ("snp", "pair")),
            P("grp"),
            P("grp"),
            P("grp"),
            P(("grp", "smp"), None),
            P("grp"),
            P(("grp", "smp"), ("snp", "pair")),
            P(("grp", "smp"), ("snp", "pair")),
        ),
        out_specs=(P(("grp", "snp", "pair"), None), P(("grp", "smp"), ("snp", "pair"))),
        check_vma=False,
    )
```

```python
import functools
import jax
import jax.numpy as jnp
from jax import lax
from jax.sharding import PartitionSpec as P
from jax.experimental import pallas as pl
from jax.experimental.pallas import tpu as pltpu

TILE = 64
BMAX = 2
TBLK = 64
SPAN = 2 * BMAX + 1
REACH = TILE * BMAX
PAIR = 2 * TILE
LANES = 128
WIDE = 384
CHUNK = 256
STEP = 512
CODE_TOP = 32767.0
CODE_LEAST = 1e-30
F32 = jnp.float32
BF16 = jnp.bfloat16
MESH = pl.DeviceIdType.MESH

ridge_term = 1.0


def split_two(value):
    high = value.astype(BF16)
    low = (value - high.astype(F32)).astype(BF16)
    return high, low


def folded(value):
    return jnp.sum(value.reshape(value.shape[0] // 8, 8, value.shape[1]), axis=0)


def total_row(value):
    return jnp.sum(value, axis=0, keepdims=True)


def tile_flags(widths, tile, count):
    here = widths[tile]
    flags = []
    for offset in range(-BMAX, BMAX + 1):
        place = tile + offset
        inside = (place >= 0) & (place < count)
        beside = widths[jnp.clip(place, 0, count - 1)]
        reach = abs(offset)
        flags.append(jnp.where(inside & (here >= reach) & (beside >= reach), 1.0, 0.0).astype(F32))
    return flags


def kernel(
    sizes,
    dosage, mean_far, scale_far, next_far, ld_far, prev_far, z_far, observed_far,
    ld_out, imputed_out,
    ld_next, imputed,
    mean, scale, band_next, ld_prev, band_prev, zscores, observed, seen,
    dos, dos_side, part_own, part_next, gram, summed, code_out, code_in, peak_out, peak_in, edge_in,
    vec, vec_two, band_two, image, res1, img0, red,
    in_sem, dos_sem, side_sem, vec_send, vec_recv, red_send, red_recv,
    code_send, code_recv, peak_send, peak_recv, edge_sem, out_sem,
):
    n_smp, n_snp, n_pair = sizes
    samples, cols = dos.shape
    rows = zscores.shape[0]
    tiles = rows // TILE
    chunks = cols // CHUNK
    blocks = cols // PAIR
    row_blocks = rows // PAIR
    tile_total = band_next.shape[0]
    me = lax.axis_index("smp")
    place = lax.axis_index("snp") * n_pair + lax.axis_index("pair")
    places = n_snp * n_pair
    first_col = place * cols
    order = list(range(1, chunks)) + [0]

    def at_place(index):
        return {"snp": index // n_pair, "pair": index % n_pair}

    has_left, has_right = place > 0, place < places - 1
    has_prev, has_next = me > 0, me < n_smp - 1
    left_id = at_place(jnp.maximum(place - 1, 0))
    right_id = at_place(jnp.minimum(place + 1, places - 1))

    small = []
    for index, (far, near) in enumerate(
        (
            (z_far, zscores),
            (observed_far, observed),
            (prev_far, band_prev),
            (ld_far, ld_prev),
            (mean_far, mean),
            (scale_far, scale),
            (next_far, band_next),
        )
    ):
        small.append(pltpu.make_async_copy(far, near, in_sem.at[index]))
        small[-1].start()
    fetches = []
    for chunk in order:
        span = pl.ds(chunk * CHUNK, CHUNK)
        fetch = pltpu.make_async_copy(dosage.at[:, span], dos.at[:, span], dos_sem.at[chunk])
        fetch.start()
        fetches.append(fetch)

    barrier = pltpu.get_barrier_semaphore()
    for step in range(1, n_smp):
        pl.semaphore_signal(
            barrier, inc=1, device_id={"smp": lax.rem(me + step, n_smp)}, device_id_type=MESH
        )

    @pl.when(has_left)
    def _():
        pl.semaphore_signal(barrier, inc=1, device_id=left_id, device_id_type=MESH)

    @pl.when(has_right)
    def _():
        pl.semaphore_signal(barrier, inc=1, device_id=right_id, device_id_type=MESH)

    side_copy = pltpu.make_async_remote_copy(
        src_ref=dosage.at[:, pl.ds(0, REACH)],
        dst_ref=dos_side,
        send_sem=side_sem.at[0],
        recv_sem=side_sem.at[1],
        device_id=left_id,
        device_id_type=MESH,
    )

    for turn in range(3):

        @pl.when(me == 0)
        def _():
            vec[turn, pl.ds(0, REACH), :] = jnp.zeros((REACH, LANES), F32)

        @pl.when(me == n_smp - 1)
        def _():
            vec[turn, pl.ds(REACH + rows, REACH), :] = jnp.zeros((REACH, LANES), F32)

    def put_vector(turn, tile, value):
        span = pl.ds(pl.multiple_of(REACH + tile * PAIR, PAIR), PAIR)
        vec[turn, span, :] = value
        high, low = split_two(value)
        vec_two[turn, span, 0:LANES] = high
        vec_two[turn, span, LANES : 2 * LANES] = low

    def own_rows(tile):
        return pl.ds(pl.multiple_of(tile * PAIR, PAIR), PAIR)

    def vec_rows(tile):
        return pl.ds(pl.multiple_of(REACH + tile * PAIR, PAIR), PAIR)

    def halo_copies(turn):
        up = pltpu.make_async_remote_copy(
            src_ref=vec.at[turn, pl.ds(REACH, REACH)],
            dst_ref=vec.at[turn, pl.ds(REACH + rows, REACH)],
            send_sem=vec_send.at[turn, 0],
            recv_sem=vec_recv.at[turn, 0],
            device_id={"smp": jnp.maximum(me - 1, 0)},
            device_id_type=MESH,
        )
        down = pltpu.make_async_remote_copy(
            src_ref=vec.at[turn, pl.ds(rows, REACH)],
            dst_ref=vec.at[turn, pl.ds(0, REACH)],
            send_sem=vec_send.at[turn, 1],
            recv_sem=vec_recv.at[turn, 1],
            device_id={"smp": jnp.minimum(me + 1, n_smp - 1)},
            device_id_type=MESH,
        )
        return up, down

    def send_halos(turn):
        up, down = halo_copies(turn)

        @pl.when(has_prev)
        def _():
            up.start()

        @pl.when(has_next)
        def _():
            down.start()

    def take_halos(turn):
        up, down = halo_copies(turn)

        @pl.when(has_next)
        def _():
            up.wait_recv()

        @pl.when(has_prev)
        def _():
            down.wait_recv()

        for start in (0, REACH + rows):
            high, low = split_two(vec[turn, pl.ds(start, REACH), :])
            vec_two[turn, pl.ds(start, REACH), 0:LANES] = high
            vec_two[turn, pl.ds(start, REACH), LANES : 2 * LANES] = low

    def red_copy(turn, step):
        return pltpu.make_async_remote_copy(
            src_ref=red.at[turn, me],
            dst_ref=red.at[turn, me],
            send_sem=red_send.at[turn, step],
            recv_sem=red_recv.at[turn, step],
            device_id={"smp": lax.rem(me + step, n_smp)},
            device_id_type=MESH,
        )

    def red_arrival(turn, step):
        sender = lax.rem(me - step + n_smp, n_smp)
        return pltpu.make_async_remote_copy(
            src_ref=red.at[turn, sender],
            dst_ref=red.at[turn, sender],
            send_sem=red_send.at[turn, step],
            recv_sem=red_recv.at[turn, step],
            device_id={"smp": lax.rem(me + step, n_smp)},
            device_id_type=MESH,
        )

    def send_sums(turn, sums):
        lines = [total_row(value) for value in sums]
        lines += [jnp.zeros((1, LANES), F32)] * (8 - len(lines))
        red[turn, me] = jnp.concatenate(lines, axis=0)
        for step in range(1, n_smp):
            red_copy(turn, step).start()

    def take_sums(turn):
        for step in range(1, n_smp):
            red_arrival(turn, step).wait_recv()
        whole = red[turn, 0]
        for index in range(1, n_smp):
            whole = whole + red[turn, index]
        return whole

    lane = lax.broadcasted_iota(jnp.int32, (PAIR, LANES), 1)
    line = lax.broadcasted_iota(jnp.int32, (PAIR, LANES), 0)

    small[0].wait()
    small[1].wait()
    for tile in range(row_blocks):
        here = observed[:, pl.ds(tile * PAIR, PAIR)].astype(F32)
        flags = jnp.zeros((LANES, PAIR), F32)
        for index in range(here.shape[0]):
            flags = jnp.where(line // TBLK == index, here[index : index + 1], flags)
        flags = jnp.transpose(flags)
        seen[pl.ds(tile * PAIR, PAIR), :] = flags
        put_vector(0, tile, flags * zscores[pl.ds(tile * PAIR, PAIR), :])

    pl.semaphore_wait(
        barrier,
        n_smp - 1 + jnp.where(has_left, 1, 0) + jnp.where(has_right, 1, 0),
    )

    @pl.when(has_left)
    def _():
        side_copy.start()

    send_halos(0)

    small[2].wait()
    small[3].wait()

    def two_flags(widths, first_tile, factor):
        left = tile_flags(widths, first_tile, tile_total)
        right = tile_flags(widths, first_tile + 1, tile_total)
        first_lanes = lane[0:1] < TILE
        return [jnp.where(first_lanes, a * factor, b * factor) for a, b in zip(left, right)]

    for tile in range(row_blocks):
        flags = two_flags(band_prev, me * tiles + 2 * tile, 1.0)
        columns = pl.ds(tile * PAIR, PAIR)
        parts = [
            ld_prev[pl.ds(index * TILE, TILE), columns] * flag for index, flag in enumerate(flags)
        ]
        blank = jnp.zeros((TILE, PAIR), F32)
        left, right = parts + [blank], [blank] + parts
        for third in range(3):
            pieces = [
                jnp.where(lane[0:TILE] < TILE, left[index], right[index])
                for index in (2 * third, 2 * third + 1)
            ]
            high, low = split_two(jnp.transpose(jnp.concatenate(pieces, axis=0)))
            band_two[tile, 0:PAIR, third * PAIR : (third + 1) * PAIR] = high
            band_two[tile, PAIR : 2 * PAIR, third * PAIR : (third + 1) * PAIR] = low

    for copy in small[4:]:
        copy.wait()

    ready = set()

    def make_ready(chunk):
        if chunk in ready:
            return
        ready.add(chunk)
        if chunk < chunks:
            fetches[order.index(chunk)].wait()
            return

        @pl.when(has_right)
        def _():
            side_copy.wait_recv()

        @pl.when(jnp.logical_not(has_right))
        def _():
            dos_side[...] = jnp.zeros((samples, REACH), BF16)

    def standards(column, width):
        column = jnp.minimum(first_col + column, mean.shape[1] - width)
        where = pl.ds(pl.multiple_of(column, LANES), width)
        return mean[:, where], scale[:, where]

    def make_gram(chunk):
        make_ready(chunk)
        make_ready(chunk + 1)
        low = chunk * CHUNK
        mean_own, scale_own = standards(low, CHUNK)
        mean_next, scale_next = standards(low + CHUNK, REACH)
        keep = jnp.where(has_right, 1.0, 0.0) if chunk == chunks - 1 else 1.0
        scale_next = scale_next * keep

        def body(index, carry):
            span = pl.ds(pl.multiple_of(index * STEP, STEP), STEP)
            own = dos[span, low : low + CHUNK].astype(F32)
            own = ((own - mean_own) * scale_own).astype(BF16)
            if chunk < chunks - 1:
                beside = dos[span, low + CHUNK : low + CHUNK + REACH].astype(F32)
            else:
                beside = dos_side[span, :].astype(F32)
            beside = ((beside - mean_next) * scale_next).astype(BF16)
            dims = (((0,), (0,)), ((), ()))
            wide = lax.dot_general(own, own, dims, preferred_element_type=F32)
            late = lax.dot_general(own[:, PAIR:], beside, dims, preferred_element_type=F32)
            part_own[...] += wide
            part_next[...] += late
            return carry

        part_own[...] = jnp.zeros((CHUNK, CHUNK), F32)
        part_next[...] = jnp.zeros((PAIR, REACH), F32)
        lax.fori_loop(0, samples // STEP, body, 0)
        first, second = part_own[0:PAIR, 0:PAIR], part_own[PAIR:, PAIR:]
        gram[chunk, 0] = jnp.where(line <= lane, first, second)
        spare = total_row(jnp.where(line == lane, second, 0.0))
        unused = (line < TILE) & (lane >= TILE)
        for side in range(2):
            beside = part_own[0:PAIR, PAIR:] if side == 0 else part_next[...]
            held = spare if side == 0 else pltpu.roll(spare, TILE, 1)
            held = jnp.where(line == 0, held, 0.0)
            gram[chunk, 1 + side] = jnp.where(unused, held, beside)

    half = n_smp // 2
    first_way = jnp.where(me < half, 0, 1)
    second_way = 1 - first_way
    at_end = (me == 0) | (me == n_smp - 1)

    def running_copies(way, chunk):
        ahead = {"smp": jnp.clip(me + 1 - 2 * way, 0, n_smp - 1)}
        return [
            pltpu.make_async_remote_copy(
                src_ref=source.at[way, chunk],
                dst_ref=target.at[way, chunk],
                send_sem=send.at[way, chunk],
                recv_sem=recv.at[way, chunk],
                device_id=ahead,
                device_id_type=MESH,
            )
            for source, target, send, recv in (
                (code_out, code_in, code_send, code_recv),
                (peak_out, peak_in, peak_send, peak_recv),
            )
        ]

    def send_running(way, chunk, values):
        peaks = []
        for index, value in enumerate(values):
            peak = jnp.max(jnp.abs(value), axis=0, keepdims=True)
            factor = CODE_TOP / jnp.maximum(peak, CODE_LEAST)
            code = jnp.round(value * factor).astype(jnp.int32)
            code_out[way, chunk, index] = code.astype(jnp.int16)
            peaks.append(peak)
        peaks += [jnp.zeros((1, LANES), F32)] * (8 - len(peaks))
        peak_out[way, chunk] = jnp.concatenate(peaks, axis=0)
        for copy in running_copies(way, chunk):
            copy.start()

    def take_running(way, chunk):
        for copy in running_copies(way, chunk):
            copy.wait_recv()
        peaks = peak_in[way, chunk] * (1.0 / CODE_TOP)
        return [
            code_in[way, chunk, index].astype(jnp.int32).astype(F32) * peaks[index : index + 1]
            for index in range(3)
        ]

    def first_pass_end(chunk):
        @pl.when(at_end)
        def _():
            values = [gram[chunk, index] for index in range(3)]
            for index in range(3):
                summed[chunk, index] = values[index]
            send_running(first_way, chunk, values)

    def first_pass_inner(chunk):
        @pl.when(jnp.logical_not(at_end))
        def _():
            values = take_running(first_way, chunk)
            values = [value + gram[chunk, index] for index, value in enumerate(values)]
            for index in range(3):
                summed[chunk, index] = values[index]
            send_running(first_way, chunk, values)

    def edge_copy():
        return pltpu.make_async_remote_copy(
            src_ref=summed.at[chunks - 1, 2],
            dst_ref=edge_in,
            send_sem=edge_sem.at[0],
            recv_sem=edge_sem.at[1],
            device_id=right_id,
            device_id_type=MESH,
        )

    def second_pass(chunk):
        values = take_running(second_way, chunk)

        @pl.when(jnp.logical_not(at_end))
        def _():
            send_running(
                second_way,
                chunk,
                [value + gram[chunk, index] for index, value in enumerate(values)],
            )

        for index in range(3):
            summed[chunk, index] += values[index]
        if chunk == chunks - 1:

            @pl.when(has_right)
            def _():
                edge_copy().start()

    def product(turn, tile):
        window = vec_two[turn, pl.ds(pl.multiple_of(tile * PAIR, PAIR), WIDE), :]
        out = jnp.dot(band_two[tile], window, preferred_element_type=F32)
        value = (out[0:PAIR, 0:LANES] + out[PAIR:, LANES:]) + (
            out[0:PAIR, LANES:] + out[PAIR:, 0:LANES]
        )
        image[turn, own_rows(tile), :] = value
        return value

    def operated(turn, tile, vector):
        flag = seen[own_rows(tile), :]
        masked = flag * vector
        return flag * (product(turn, tile) + ridge_term * masked) + (1.0 - flag) * vector

    def over_tiles(turn, body, start):
        inner = max(row_blocks - 2, 0)
        edges = sorted({0, row_blocks - 1})
        carry = start
        if inner:
            unroll = 2 if inner % 2 == 0 else 1
            carry = lax.fori_loop(1, 1 + inner, body, carry, unroll=unroll)
        take_halos(turn)
        for tile in edges:
            carry = body(tile, carry)
        return carry

    nothing = jnp.zeros((8, LANES), F32)

    def start_solver():
        def body(tile, carry):
            square, cross = carry
            here = vec[0, vec_rows(tile), :]
            out = operated(0, tile, here)
            put_vector(1, tile, seen[own_rows(tile), :] * out)
            return square + folded(here * here), cross + folded(here * out)

        square, cross = over_tiles(0, body, (nothing, nothing))
        send_halos(1)
        send_sums(0, [square, cross])

    def next_solver():
        def body(tile, carry):
            img0[own_rows(tile), :] = operated(1, tile, vec[1, vec_rows(tile), :])
            return carry

        over_tiles(1, body, 0)
        whole = take_sums(0)
        norm0, curve0 = whole[0:1], whole[1:2]
        alpha0 = norm0 / curve0

        def update(tile, carry):
            square, cross, mixed = carry
            r0 = vec[0, vec_rows(tile), :]
            w0 = vec[1, vec_rows(tile), :]
            r1 = r0 - alpha0 * w0
            w1 = w0 - alpha0 * img0[own_rows(tile), :]
            res1[own_rows(tile), :] = r1
            put_vector(2, tile, seen[own_rows(tile), :] * w1)
            return (
                square + folded(r1 * r1),
                cross + folded(r1 * w1),
                mixed + folded(r1 * w0 + r0 * w1),
            )

        sums = lax.fori_loop(0, row_blocks, update, (nothing, nothing, nothing))
        send_halos(2)
        send_sums(1, list(sums))
        return norm0, curve0, alpha0

    def last_solver(norm0, curve0, alpha0):
        def body(tile, carry):
            here = vec[2, vec_rows(tile), :]
            imputed[own_rows(tile), :] = operated(2, tile, here)
            return carry

        over_tiles(2, body, 0)
        whole = take_sums(1)
        norm1 = whole[0:1]
        beta1 = norm1 / norm0
        curve1 = whole[1:2] + beta1 * whole[2:3] + beta1 * beta1 * curve0
        alpha1 = norm1 / curve1

        def update(tile, carry):
            square, cross, mixed = carry
            r0 = vec[0, vec_rows(tile), :]
            w0 = vec[1, vec_rows(tile), :]
            r1 = res1[own_rows(tile), :]
            w1 = vec[2, vec_rows(tile), :]
            p1 = r1 + beta1 * r0
            s1 = w1 + beta1 * w0
            z1 = imputed[own_rows(tile), :] + beta1 * img0[own_rows(tile), :]
            r2 = r1 - alpha1 * s1
            w2 = w1 - alpha1 * z1
            return (
                square + folded(r2 * r2),
                cross + folded(r2 * w2),
                mixed + folded(r2 * s1 + p1 * w2),
            )

        sums = lax.fori_loop(0, row_blocks, update, (nothing, nothing, nothing))
        send_sums(2, list(sums))
        return norm1, curve1, alpha1, beta1

    def end_solver(alpha0, norm1, curve1, alpha1, beta1):
        whole = take_sums(2)
        beta2 = whole[0:1] / norm1
        curve2 = whole[1:2] + beta2 * whole[2:3] + beta2 * beta2 * curve1
        alpha2 = whole[0:1] / curve2
        first = (1.0 + beta1, -alpha0)
        second = (
            1.0 + beta2 * first[0],
            -alpha0 - alpha1 * beta1 + beta2 * first[1],
            -alpha1,
        )
        part0 = alpha0 + alpha1 * first[0] + alpha2 * second[0]
        part1 = alpha1 * first[1] + alpha2 * second[1]
        part2 = alpha2 * second[2]

        def body(tile, carry):
            span = own_rows(tile)
            imputed[span, :] = (
                part0 * image[0, span, :] + part1 * image[1, span, :] + part2 * image[2, span, :]
            )
            return carry

        lax.fori_loop(0, row_blocks, body, 0)

    def make_and_send(chunk):
        make_gram(chunk)
        first_pass_end(chunk)

    make_and_send(order[0])
    start_solver()
    if chunks > 2:
        make_and_send(order[1])
        first_pass_inner(order[0])
    scalars0 = next_solver()
    for place_in_order in range(2 if chunks > 2 else 1, chunks):
        make_and_send(order[place_in_order])
        first_pass_inner(order[place_in_order - 1])
    scalars1 = last_solver(*scalars0)
    first_pass_inner(order[-1])

    @pl.when(jnp.logical_not(at_end))
    def _():
        for chunk in order:
            second_pass(chunk)

    end_solver(scalars0[2], *scalars1)
    results = [pltpu.make_async_copy(imputed, imputed_out, out_sem.at[blocks])]
    results[0].start()

    inverse = 1.0 / (samples * n_smp)

    def assemble(block, before):
        chunk, side = block // 2, block % 2
        packed = summed[chunk, 0]
        turned = jnp.transpose(packed)
        if side:
            spare = jnp.where(
                lane[0:1] >= TILE,
                summed[chunk, 1, 0:1],
                pltpu.roll(summed[chunk, 2, 0:1], TILE, 1),
            )
            diagonal = jnp.where(line > lane, packed, jnp.where(line < lane, turned, spare))
        else:
            diagonal = jnp.where(line <= lane, packed, turned)
        after = jnp.transpose(summed[chunk, 1 + side])
        stack = [before[0:TILE], before[TILE:], diagonal[0:TILE], diagonal[TILE:]]
        stack += [after[0:TILE], after[TILE:]]
        flags = two_flags(band_next, place * (cols // TILE) + 2 * block, inverse)
        for index, flag in enumerate(flags):
            value = jnp.where(lane[0:TILE] < TILE, stack[index], stack[index + 1])
            ld_next[pl.ds(index * TILE, TILE), pl.ds(block * PAIR, PAIR)] = value * flag
        columns = pl.ds(block * PAIR, PAIR)
        results.append(
            pltpu.make_async_copy(ld_next.at[:, columns], ld_out.at[:, columns], out_sem.at[block])
        )
        results[-1].start()

    done = set()

    def assemble_ready():
        for block in range(1, blocks):
            needed = {block // 2, (block - 1) // 2}
            if block not in assembled and needed <= done:
                assembled.add(block)
                assemble(block, summed[(block - 1) // 2, 1 + (block - 1) % 2])

    assembled = set()
    for chunk in order:

        @pl.when(at_end)
        def _():
            second_pass(chunk)

        done.add(chunk)
        assemble_ready()

    @pl.when(has_left)
    def _():
        edge_copy().wait_recv()

    @pl.when(jnp.logical_not(has_left))
    def _():
        edge_in[...] = jnp.zeros((PAIR, PAIR), F32)

    assemble(0, edge_in[...])

    for copy in results:
        copy.wait()

    @pl.when(has_left)
    def _():
        side_copy.wait_send()

    @pl.when(has_right)
    def _():
        edge_copy().wait_send()

    for turn in range(3):
        up, down = halo_copies(turn)

        @pl.when(has_prev)
        def _():
            up.wait_send()

        @pl.when(has_next)
        def _():
            down.wait_send()

        for step in range(1, n_smp):
            red_copy(turn, step).wait_send()

    for chunk in range(chunks):
        for copy in running_copies(first_way, chunk):
            copy.wait_send()

        @pl.when(jnp.logical_not(at_end))
        def _():
            for copy in running_copies(second_way, chunk):
                copy.wait_send()


def local(sizes, dosage, allele_mean, snp_scale, band_next, ld_prev, band_prev, zscores, observed):
    n_smp = sizes[0]
    samples, cols = dosage.shape
    rows, traits = zscores.shape
    chunks = cols // CHUNK
    if traits < LANES:
        zscores = jnp.pad(zscores, ((0, 0), (0, LANES - traits)))
    far = pl.BlockSpec(memory_space=pltpu.HBM)
    dma = pltpu.SemaphoreType.DMA
    ld_next, imputed = pl.pallas_call(
        functools.partial(kernel, sizes),
        out_shape=(
            jax.ShapeDtypeStruct((SPAN * TILE, cols), F32),
            jax.ShapeDtypeStruct((rows, LANES), F32),
        ),
        in_specs=[far] * 8,
        out_specs=(far, far),
        scratch_shapes=[
            pltpu.VMEM((SPAN * TILE, cols), F32),
            pltpu.VMEM((rows, LANES), F32),
            pltpu.VMEM((1, allele_mean.shape[0]), F32),
            pltpu.VMEM((1, allele_mean.shape[0]), F32),
            pltpu.SMEM(band_next.shape, jnp.int32),
            pltpu.VMEM((SPAN * TILE, rows), F32),
            pltpu.SMEM(band_prev.shape, jnp.int32),
            pltpu.VMEM((rows, LANES), F32),
            pltpu.VMEM((observed.shape[1], rows), jnp.int32),
            pltpu.VMEM((rows, LANES), F32),
            pltpu.VMEM((samples, cols), BF16),
            pltpu.VMEM((samples, REACH), BF16),
            pltpu.VMEM((CHUNK, CHUNK), F32),
            pltpu.VMEM((PAIR, REACH), F32),
            pltpu.VMEM((chunks, 3, PAIR, PAIR), F32),
            pltpu.VMEM((chunks, 3, PAIR, PAIR), F32),
            pltpu.VMEM((2, chunks, 3, PAIR, PAIR), jnp.int16),
            pltpu.VMEM((2, chunks, 3, PAIR, PAIR), jnp.int16),
            pltpu.VMEM((2, chunks, 8, PAIR), F32),
            pltpu.VMEM((2, chunks, 8, PAIR), F32),
            pltpu.VMEM((PAIR, PAIR), F32),
            pltpu.VMEM((3, rows + 2 * REACH, LANES), F32),
            pltpu.VMEM((3, rows + 2 * REACH, 2 * LANES), BF16),
            pltpu.VMEM((rows // PAIR, 2 * PAIR, WIDE), BF16),
            pltpu.VMEM((3, rows, LANES), F32),
            pltpu.VMEM((rows, LANES), F32),
            pltpu.VMEM((rows, LANES), F32),
            pltpu.VMEM((3, n_smp, 8, LANES), F32),
            dma((7,)),
            dma((chunks,)),
            dma((2,)),
            dma((3, 2)),
            dma((3, 2)),
            dma((3, n_smp)),
            dma((3, n_smp)),
            dma((2, chunks)),
            dma((2, chunks)),
            dma((2, chunks)),
            dma((2, chunks)),
            dma((2,)),
            dma((cols // PAIR + 1,)),
        ],
        compiler_params=pltpu.CompilerParams(
            collective_id=0, has_side_effects=True, vmem_limit_bytes=60 * 1024 * 1024
        ),
    )(
        dosage,
        allele_mean.reshape(1, -1),
        snp_scale.reshape(1, -1),
        band_next,
        jnp.transpose(ld_prev),
        band_prev,
        zscores,
        jnp.transpose(observed),
    )
    return jnp.transpose(ld_next), imputed[:, :traits]


def solution(mesh):
    sizes = (mesh.shape["smp"], mesh.shape["snp"], mesh.shape["pair"])
    return jax.shard_map(
        functools.partial(local, sizes),
        mesh=mesh,
        in_specs=(
            P(("grp", "smp"), ("snp", "pair")),
            P("grp"),
            P("grp"),
            P("grp"),
            P(("grp", "smp"), None),
            P("grp"),
            P(("grp", "smp"), ("snp", "pair")),
            P(("grp", "smp"), ("snp", "pair")),
        ),
        out_specs=(P(("grp", "snp", "pair"), None), P(("grp", "smp"), ("snp", "pair"))),
        check_vma=False,
    )
```

```python
import functools
import jax
import jax.numpy as jnp
from jax import lax
from jax.sharding import PartitionSpec as P
from jax.experimental import pallas as pl
from jax.experimental.pallas import tpu as pltpu

TILE = 64
BMAX = 2
TBLK = 64
SPAN = 2 * BMAX + 1
REACH = TILE * BMAX
PAIR = 2 * TILE
LANES = 128
WIDE = 384
CHUNK = 256
STEP = 512
SIDES = 4
CODE_TOP = 32767.0
CODE_LEAST = 1e-30
F32 = jnp.float32
BF16 = jnp.bfloat16
MESH = pl.DeviceIdType.MESH

ridge_term = 1.0


def split_two(value):
    high = value.astype(BF16)
    low = (value - high.astype(F32)).astype(BF16)
    return high, low


def folded(value):
    return jnp.sum(value.reshape(value.shape[0] // 8, 8, value.shape[1]), axis=0)


def total_row(value):
    return jnp.sum(value, axis=0, keepdims=True)


def tile_flags(widths, tile, count):
    here = widths[tile]
    flags = []
    for offset in range(-BMAX, BMAX + 1):
        place = tile + offset
        inside = (place >= 0) & (place < count)
        beside = widths[jnp.clip(place, 0, count - 1)]
        reach = abs(offset)
        flags.append(jnp.where(inside & (here >= reach) & (beside >= reach), 1.0, 0.0).astype(F32))
    return flags


def kernel(
    sizes,
    dosage, mean_far, scale_far, next_far, ld_far, prev_far, z_far, observed_far,
    ld_out, imputed_out,
    ld_next, imputed,
    mean, scale, band_next, ld_prev, band_prev, zscores, observed, seen,
    dos, dos_edge, dos_side, part_own, part_next, gram, summed, code_out, code_in, peak_out, peak_in, edge_in,
    vec, vec_two, band_two, image, res1, img0, red,
    in_sem, dos_sem, side_sem, vec_send, vec_recv, red_send, red_recv,
    code_send, code_recv, peak_send, peak_recv, edge_sem, out_sem,
):
    n_smp, n_snp, n_pair = sizes
    samples, cols = dos.shape
    rows = zscores.shape[0]
    tiles = rows // TILE
    chunks = cols // CHUNK
    blocks = cols // PAIR
    row_blocks = rows // PAIR
    tile_total = band_next.shape[0]
    me = lax.axis_index("smp")
    place = lax.axis_index("snp") * n_pair + lax.axis_index("pair")
    places = n_snp * n_pair
    first_col = place * cols
    order = list(range(1, chunks)) + [0]

    def at_place(index):
        return {"snp": index // n_pair, "pair": index % n_pair}

    has_left, has_right = place > 0, place < places - 1
    has_prev, has_next = me > 0, me < n_smp - 1
    left_id = at_place(jnp.maximum(place - 1, 0))
    right_id = at_place(jnp.minimum(place + 1, places - 1))

    edge_fetch = pltpu.make_async_copy(dosage.at[:, pl.ds(0, REACH)], dos_edge, in_sem.at[7])
    edge_fetch.start()
    small = []
    for index, (far, near) in enumerate(
        (
            (z_far, zscores),
            (observed_far, observed),
            (prev_far, band_prev),
            (ld_far, ld_prev),
            (mean_far, mean),
            (scale_far, scale),
            (next_far, band_next),
        )
    ):
        small.append(pltpu.make_async_copy(far, near, in_sem.at[index]))
        small[-1].start()
    fetches = []
    for chunk in order:
        span = pl.ds(chunk * CHUNK, CHUNK)
        fetch = pltpu.make_async_copy(dosage.at[:, span], dos.at[:, span], dos_sem.at[chunk])
        fetch.start()
        fetches.append(fetch)

    barrier = pltpu.get_barrier_semaphore()
    for step in range(1, n_smp):
        pl.semaphore_signal(
            barrier, inc=1, device_id={"smp": lax.rem(me + step, n_smp)}, device_id_type=MESH
        )

    @pl.when(has_left)
    def _():
        pl.semaphore_signal(barrier, inc=1, device_id=left_id, device_id_type=MESH)

    @pl.when(has_right)
    def _():
        pl.semaphore_signal(barrier, inc=1, device_id=right_id, device_id_type=MESH)

    def side_copies():
        part = samples // SIDES
        return [
            pltpu.make_async_remote_copy(
                src_ref=dos_edge.at[pl.ds(index * part, part)],
                dst_ref=dos_side.at[pl.ds(index * part, part)],
                send_sem=side_sem.at[0, index],
                recv_sem=side_sem.at[1, index],
                device_id=left_id,
                device_id_type=MESH,
            )
            for index in range(SIDES)
        ]

    for turn in range(3):

        @pl.when(me == 0)
        def _():
            vec[turn, pl.ds(0, REACH), :] = jnp.zeros((REACH, LANES), F32)

        @pl.when(me == n_smp - 1)
        def _():
            vec[turn, pl.ds(REACH + rows, REACH), :] = jnp.zeros((REACH, LANES), F32)

    edge_fetch.wait()
    pl.semaphore_wait(
        barrier,
        n_smp - 1 + jnp.where(has_left, 1, 0) + jnp.where(has_right, 1, 0),
    )

    @pl.when(has_left)
    def _():
        for copy in side_copies():
            copy.start()

    def put_vector(turn, tile, value):
        span = pl.ds(pl.multiple_of(REACH + tile * PAIR, PAIR), PAIR)
        vec[turn, span, :] = value
        high, low = split_two(value)
        vec_two[turn, span, 0:LANES] = high
        vec_two[turn, span, LANES : 2 * LANES] = low

    def own_rows(tile):
        return pl.ds(pl.multiple_of(tile * PAIR, PAIR), PAIR)

    def vec_rows(tile):
        return pl.ds(pl.multiple_of(REACH + tile * PAIR, PAIR), PAIR)

    def halo_copies(turn):
        up = pltpu.make_async_remote_copy(
            src_ref=vec.at[turn, pl.ds(REACH, REACH)],
            dst_ref=vec.at[turn, pl.ds(REACH + rows, REACH)],
            send_sem=vec_send.at[turn, 0],
            recv_sem=vec_recv.at[turn, 0],
            device_id={"smp": jnp.maximum(me - 1, 0)},
            device_id_type=MESH,
        )
        down = pltpu.make_async_remote_copy(
            src_ref=vec.at[turn, pl.ds(rows, REACH)],
            dst_ref=vec.at[turn, pl.ds(0, REACH)],
            send_sem=vec_send.at[turn, 1],
            recv_sem=vec_recv.at[turn, 1],
            device_id={"smp": jnp.minimum(me + 1, n_smp - 1)},
            device_id_type=MESH,
        )
        return up, down

    def send_halos(turn):
        up, down = halo_copies(turn)

        @pl.when(has_prev)
        def _():
            up.start()

        @pl.when(has_next)
        def _():
            down.start()

    def take_halos(turn):
        up, down = halo_copies(turn)

        @pl.when(has_next)
        def _():
            up.wait_recv()

        @pl.when(has_prev)
        def _():
            down.wait_recv()

        for start in (0, REACH + rows):
            high, low = split_two(vec[turn, pl.ds(start, REACH), :])
            vec_two[turn, pl.ds(start, REACH), 0:LANES] = high
            vec_two[turn, pl.ds(start, REACH), LANES : 2 * LANES] = low

    def red_copy(turn, step):
        return pltpu.make_async_remote_copy(
            src_ref=red.at[turn, me],
            dst_ref=red.at[turn, me],
            send_sem=red_send.at[turn, step],
            recv_sem=red_recv.at[turn, step],
            device_id={"smp": lax.rem(me + step, n_smp)},
            device_id_type=MESH,
        )

    def red_arrival(turn, step):
        sender = lax.rem(me - step + n_smp, n_smp)
        return pltpu.make_async_remote_copy(
            src_ref=red.at[turn, sender],
            dst_ref=red.at[turn, sender],
            send_sem=red_send.at[turn, step],
            recv_sem=red_recv.at[turn, step],
            device_id={"smp": lax.rem(me + step, n_smp)},
            device_id_type=MESH,
        )

    def send_sums(turn, sums):
        lines = [total_row(value) for value in sums]
        lines += [jnp.zeros((1, LANES), F32)] * (8 - len(lines))
        red[turn, me] = jnp.concatenate(lines, axis=0)
        for step in range(1, n_smp):
            red_copy(turn, step).start()

    def take_sums(turn):
        for step in range(1, n_smp):
            red_arrival(turn, step).wait_recv()
        whole = red[turn, 0]
        for index in range(1, n_smp):
            whole = whole + red[turn, index]
        return whole

    lane = lax.broadcasted_iota(jnp.int32, (PAIR, LANES), 1)
    line = lax.broadcasted_iota(jnp.int32, (PAIR, LANES), 0)

    small[0].wait()
    small[1].wait()
    for tile in range(row_blocks):
        here = observed[:, pl.ds(tile * PAIR, PAIR)].astype(F32)
        flags = jnp.zeros((LANES, PAIR), F32)
        for index in range(here.shape[0]):
            flags = jnp.where(line // TBLK == index, here[index : index + 1], flags)
        flags = jnp.transpose(flags)
        seen[pl.ds(tile * PAIR, PAIR), :] = flags
        put_vector(0, tile, flags * zscores[pl.ds(tile * PAIR, PAIR), :])

    send_halos(0)

    small[2].wait()
    small[3].wait()

    def two_flags(widths, first_tile, factor):
        left = tile_flags(widths, first_tile, tile_total)
        right = tile_flags(widths, first_tile + 1, tile_total)
        first_lanes = lane[0:1] < TILE
        return [jnp.where(first_lanes, a * factor, b * factor) for a, b in zip(left, right)]

    for tile in range(row_blocks):
        flags = two_flags(band_prev, me * tiles + 2 * tile, 1.0)
        columns = pl.ds(tile * PAIR, PAIR)
        parts = [
            ld_prev[pl.ds(index * TILE, TILE), columns] * flag for index, flag in enumerate(flags)
        ]
        blank = jnp.zeros((TILE, PAIR), F32)
        left, right = parts + [blank], [blank] + parts
        for third in range(3):
            pieces = [
                jnp.where(lane[0:TILE] < TILE, left[index], right[index])
                for index in (2 * third, 2 * third + 1)
            ]
            high, low = split_two(jnp.transpose(jnp.concatenate(pieces, axis=0)))
            band_two[tile, 0:PAIR, third * PAIR : (third + 1) * PAIR] = high
            band_two[tile, PAIR : 2 * PAIR, third * PAIR : (third + 1) * PAIR] = low

    for copy in small[4:]:
        copy.wait()

    ready = set()

    def make_ready(chunk):
        if chunk in ready:
            return
        ready.add(chunk)
        if chunk < chunks:
            fetches[order.index(chunk)].wait()
            return

        @pl.when(has_right)
        def _():
            for copy in side_copies():
                copy.wait_recv()

        @pl.when(jnp.logical_not(has_right))
        def _():
            dos_side[...] = jnp.zeros((samples, REACH), BF16)

    def standards(column, width):
        column = jnp.minimum(first_col + column, mean.shape[1] - width)
        where = pl.ds(pl.multiple_of(column, LANES), width)
        return mean[:, where], scale[:, where]

    def make_gram(chunk):
        make_ready(chunk)
        make_ready(chunk + 1)
        low = chunk * CHUNK
        mean_own, scale_own = standards(low, CHUNK)
        mean_next, scale_next = standards(low + CHUNK, REACH)
        keep = jnp.where(has_right, 1.0, 0.0) if chunk == chunks - 1 else 1.0
        scale_next = scale_next * keep

        def body(index, carry):
            span = pl.ds(pl.multiple_of(index * STEP, STEP), STEP)
            own = dos[span, low : low + CHUNK].astype(F32)
            own = ((own - mean_own) * scale_own).astype(BF16)
            if chunk < chunks - 1:
                beside = dos[span, low + CHUNK : low + CHUNK + REACH].astype(F32)
            else:
                beside = dos_side[span, :].astype(F32)
            beside = ((beside - mean_next) * scale_next).astype(BF16)
            dims = (((0,), (0,)), ((), ()))
            wide = lax.dot_general(own, own, dims, preferred_element_type=F32)
            late = lax.dot_general(own[:, PAIR:], beside, dims, preferred_element_type=F32)
            part_own[...] += wide
            part_next[...] += late
            return carry

        part_own[...] = jnp.zeros((CHUNK, CHUNK), F32)
        part_next[...] = jnp.zeros((PAIR, REACH), F32)
        lax.fori_loop(0, samples // STEP, body, 0)
        first, second = part_own[0:PAIR, 0:PAIR], part_own[PAIR:, PAIR:]
        gram[chunk, 0] = jnp.where(line <= lane, first, second)
        spare = total_row(jnp.where(line == lane, second, 0.0))
        unused = (line < TILE) & (lane >= TILE)
        for side in range(2):
            beside = part_own[0:PAIR, PAIR:] if side == 0 else part_next[...]
            held = spare if side == 0 else pltpu.roll(spare, TILE, 1)
            held = jnp.where(line == 0, held, 0.0)
            gram[chunk, 1 + side] = jnp.where(unused, held, beside)

    half = n_smp // 2
    first_way = jnp.where(me < half, 0, 1)
    second_way = 1 - first_way
    at_end = (me == 0) | (me == n_smp - 1)

    def running_copies(way, chunk):
        ahead = {"smp": jnp.clip(me + 1 - 2 * way, 0, n_smp - 1)}
        return [
            pltpu.make_async_remote_copy(
                src_ref=source.at[way, chunk],
                dst_ref=target.at[way, chunk],
                send_sem=send.at[way, chunk],
                recv_sem=recv.at[way, chunk],
                device_id=ahead,
                device_id_type=MESH,
            )
            for source, target, send, recv in (
                (code_out, code_in, code_send, code_recv),
                (peak_out, peak_in, peak_send, peak_recv),
            )
        ]

    def send_running(way, chunk, values):
        peaks = []
        for index, value in enumerate(values):
            peak = jnp.max(jnp.abs(value), axis=0, keepdims=True)
            factor = CODE_TOP / jnp.maximum(peak, CODE_LEAST)
            code = jnp.round(value * factor).astype(jnp.int32)
            code_out[way, chunk, index] = code.astype(jnp.int16)
            peaks.append(peak)
        peaks += [jnp.zeros((1, LANES), F32)] * (8 - len(peaks))
        peak_out[way, chunk] = jnp.concatenate(peaks, axis=0)
        for copy in running_copies(way, chunk):
            copy.start()

    def take_running(way, chunk):
        for copy in running_copies(way, chunk):
            copy.wait_recv()
        peaks = peak_in[way, chunk] * (1.0 / CODE_TOP)
        return [
            code_in[way, chunk, index].astype(jnp.int32).astype(F32) * peaks[index : index + 1]
            for index in range(3)
        ]

    def first_pass_end(chunk):
        @pl.when(at_end)
        def _():
            values = [gram[chunk, index] for index in range(3)]
            for index in range(3):
                summed[chunk, index] = values[index]
            send_running(first_way, chunk, values)

    def first_pass_inner(chunk):
        @pl.when(jnp.logical_not(at_end))
        def _():
            values = take_running(first_way, chunk)
            values = [value + gram[chunk, index] for index, value in enumerate(values)]
            for index in range(3):
                summed[chunk, index] = values[index]
            send_running(first_way, chunk, values)

    def edge_copy():
        return pltpu.make_async_remote_copy(
            src_ref=summed.at[chunks - 1, 2],
            dst_ref=edge_in,
            send_sem=edge_sem.at[0],
            recv_sem=edge_sem.at[1],
            device_id=right_id,
            device_id_type=MESH,
        )

    def second_pass(chunk):
        values = take_running(second_way, chunk)

        @pl.when(jnp.logical_not(at_end))
        def _():
            send_running(
                second_way,
                chunk,
                [value + gram[chunk, index] for index, value in enumerate(values)],
            )

        for index in range(3):
            summed[chunk, index] += values[index]
        if chunk == chunks - 1:

            @pl.when(has_right)
            def _():
                edge_copy().start()

    def product(turn, tile):
        window = vec_two[turn, pl.ds(pl.multiple_of(tile * PAIR, PAIR), WIDE), :]
        out = jnp.dot(band_two[tile], window, preferred_element_type=F32)
        value = (out[0:PAIR, 0:LANES] + out[PAIR:, LANES:]) + (
            out[0:PAIR, LANES:] + out[PAIR:, 0:LANES]
        )
        image[turn, own_rows(tile), :] = value
        return value

    def operated(turn, tile, vector):
        flag = seen[own_rows(tile), :]
        masked = flag * vector
        return flag * (product(turn, tile) + ridge_term * masked) + (1.0 - flag) * vector

    def over_tiles(turn, body, start):
        inner = max(row_blocks - 2, 0)
        edges = sorted({0, row_blocks - 1})
        carry = start
        if inner:
            unroll = 2 if inner % 2 == 0 else 1
            carry = lax.fori_loop(1, 1 + inner, body, carry, unroll=unroll)
        take_halos(turn)
        for tile in edges:
            carry = body(tile, carry)
        return carry

    nothing = jnp.zeros((8, LANES), F32)

    def start_solver():
        def body(tile, carry):
            square, cross = carry
            here = vec[0, vec_rows(tile), :]
            out = operated(0, tile, here)
            put_vector(1, tile, seen[own_rows(tile), :] * out)
            return square + folded(here * here), cross + folded(here * out)

        square, cross = over_tiles(0, body, (nothing, nothing))
        send_halos(1)
        send_sums(0, [square, cross])

    def next_solver():
        def body(tile, carry):
            img0[own_rows(tile), :] = operated(1, tile, vec[1, vec_rows(tile), :])
            return carry

        over_tiles(1, body, 0)
        whole = take_sums(0)
        norm0, curve0 = whole[0:1], whole[1:2]
        alpha0 = norm0 / curve0

        def update(tile, carry):
            square, cross, mixed = carry
            r0 = vec[0, vec_rows(tile), :]
            w0 = vec[1, vec_rows(tile), :]
            r1 = r0 - alpha0 * w0
            w1 = w0 - alpha0 * img0[own_rows(tile), :]
            res1[own_rows(tile), :] = r1
            put_vector(2, tile, seen[own_rows(tile), :] * w1)
            return (
                square + folded(r1 * r1),
                cross + folded(r1 * w1),
                mixed + folded(r1 * w0 + r0 * w1),
            )

        sums = lax.fori_loop(0, row_blocks, update, (nothing, nothing, nothing))
        send_halos(2)
        send_sums(1, list(sums))
        return norm0, curve0, alpha0

    def last_solver(norm0, curve0, alpha0):
        def body(tile, carry):
            here = vec[2, vec_rows(tile), :]
            imputed[own_rows(tile), :] = operated(2, tile, here)
            return carry

        over_tiles(2, body, 0)
        whole = take_sums(1)
        norm1 = whole[0:1]
        beta1 = norm1 / norm0
        curve1 = whole[1:2] + beta1 * whole[2:3] + beta1 * beta1 * curve0
        alpha1 = norm1 / curve1

        def update(tile, carry):
            square, cross, mixed = carry
            r0 = vec[0, vec_rows(tile), :]
            w0 = vec[1, vec_rows(tile), :]
            r1 = res1[own_rows(tile), :]
            w1 = vec[2, vec_rows(tile), :]
            p1 = r1 + beta1 * r0
            s1 = w1 + beta1 * w0
            z1 = imputed[own_rows(tile), :] + beta1 * img0[own_rows(tile), :]
            r2 = r1 - alpha1 * s1
            w2 = w1 - alpha1 * z1
            return (
                square + folded(r2 * r2),
                cross + folded(r2 * w2),
                mixed + folded(r2 * s1 + p1 * w2),
            )

        sums = lax.fori_loop(0, row_blocks, update, (nothing, nothing, nothing))
        send_sums(2, list(sums))
        return norm1, curve1, alpha1, beta1

    def end_solver(alpha0, norm1, curve1, alpha1, beta1):
        whole = take_sums(2)
        beta2 = whole[0:1] / norm1
        curve2 = whole[1:2] + beta2 * whole[2:3] + beta2 * beta2 * curve1
        alpha2 = whole[0:1] / curve2
        first = (1.0 + beta1, -alpha0)
        second = (
            1.0 + beta2 * first[0],
            -alpha0 - alpha1 * beta1 + beta2 * first[1],
            -alpha1,
        )
        part0 = alpha0 + alpha1 * first[0] + alpha2 * second[0]
        part1 = alpha1 * first[1] + alpha2 * second[1]
        part2 = alpha2 * second[2]

        def body(tile, carry):
            span = own_rows(tile)
            imputed[span, :] = (
                part0 * image[0, span, :] + part1 * image[1, span, :] + part2 * image[2, span, :]
            )
            return carry

        lax.fori_loop(0, row_blocks, body, 0)

    def make_and_send(chunk):
        make_gram(chunk)
        first_pass_end(chunk)

    make_and_send(order[0])
    start_solver()
    if chunks > 2:
        make_and_send(order[1])
        first_pass_inner(order[0])
    scalars0 = next_solver()
    for place_in_order in range(2 if chunks > 2 else 1, chunks):
        make_and_send(order[place_in_order])
        first_pass_inner(order[place_in_order - 1])
    scalars1 = last_solver(*scalars0)
    first_pass_inner(order[-1])

    @pl.when(jnp.logical_not(at_end))
    def _():
        for chunk in order:
            second_pass(chunk)

    end_solver(scalars0[2], *scalars1)
    results = [pltpu.make_async_copy(imputed, imputed_out, out_sem.at[blocks])]
    results[0].start()

    inverse = 1.0 / (samples * n_smp)

    def assemble(block, before):
        chunk, side = block // 2, block % 2
        packed = summed[chunk, 0]
        turned = jnp.transpose(packed)
        if side:
            spare = jnp.where(
                lane[0:1] >= TILE,
                summed[chunk, 1, 0:1],
                pltpu.roll(summed[chunk, 2, 0:1], TILE, 1),
            )
            diagonal = jnp.where(line > lane, packed, jnp.where(line < lane, turned, spare))
        else:
            diagonal = jnp.where(line <= lane, packed, turned)
        after = jnp.transpose(summed[chunk, 1 + side])
        stack = [before[0:TILE], before[TILE:], diagonal[0:TILE], diagonal[TILE:]]
        stack += [after[0:TILE], after[TILE:]]
        flags = two_flags(band_next, place * (cols // TILE) + 2 * block, inverse)
        for index, flag in enumerate(flags):
            value = jnp.where(lane[0:TILE] < TILE, stack[index], stack[index + 1])
            ld_next[pl.ds(index * TILE, TILE), pl.ds(block * PAIR, PAIR)] = value * flag
        columns = pl.ds(block * PAIR, PAIR)
        results.append(
            pltpu.make_async_copy(ld_next.at[:, columns], ld_out.at[:, columns], out_sem.at[block])
        )
        results[-1].start()

    done = set()

    def assemble_ready():
        for block in range(1, blocks):
            needed = {block // 2, (block - 1) // 2}
            if block not in assembled and needed <= done:
                assembled.add(block)
                assemble(block, summed[(block - 1) // 2, 1 + (block - 1) % 2])

    assembled = set()
    for chunk in order:

        @pl.when(at_end)
        def _():
            second_pass(chunk)

        done.add(chunk)
        assemble_ready()

    @pl.when(has_left)
    def _():
        edge_copy().wait_recv()

    @pl.when(jnp.logical_not(has_left))
    def _():
        edge_in[...] = jnp.zeros((PAIR, PAIR), F32)

    assemble(0, edge_in[...])

    for copy in results:
        copy.wait()

    @pl.when(has_left)
    def _():
        for copy in side_copies():
            copy.wait_send()

    @pl.when(has_right)
    def _():
        edge_copy().wait_send()

    for turn in range(3):
        up, down = halo_copies(turn)

        @pl.when(has_prev)
        def _():
            up.wait_send()

        @pl.when(has_next)
        def _():
            down.wait_send()

        for step in range(1, n_smp):
            red_copy(turn, step).wait_send()

    for chunk in range(chunks):
        for copy in running_copies(first_way, chunk):
            copy.wait_send()

        @pl.when(jnp.logical_not(at_end))
        def _():
            for copy in running_copies(second_way, chunk):
                copy.wait_send()


def local(sizes, dosage, allele_mean, snp_scale, band_next, ld_prev, band_prev, zscores, observed):
    n_smp = sizes[0]
    samples, cols = dosage.shape
    rows, traits = zscores.shape
    chunks = cols // CHUNK
    if traits < LANES:
        zscores = jnp.pad(zscores, ((0, 0), (0, LANES - traits)))
    far = pl.BlockSpec(memory_space=pltpu.HBM)
    dma = pltpu.SemaphoreType.DMA
    ld_next, imputed = pl.pallas_call(
        functools.partial(kernel, sizes),
        out_shape=(
            jax.ShapeDtypeStruct((SPAN * TILE, cols), F32),
            jax.ShapeDtypeStruct((rows, LANES), F32),
        ),
        in_specs=[far] * 8,
        out_specs=(far, far),
        scratch_shapes=[
            pltpu.VMEM((SPAN * TILE, cols), F32),
            pltpu.VMEM((rows, LANES), F32),
            pltpu.VMEM((1, allele_mean.shape[0]), F32),
            pltpu.VMEM((1, allele_mean.shape[0]), F32),
            pltpu.SMEM(band_next.shape, jnp.int32),
            pltpu.VMEM((SPAN * TILE, rows), F32),
            pltpu.SMEM(band_prev.shape, jnp.int32),
            pltpu.VMEM((rows, LANES), F32),
            pltpu.VMEM((observed.shape[1], rows), jnp.int32),
            pltpu.VMEM((rows, LANES), F32),
            pltpu.VMEM((samples, cols), BF16),
            pltpu.VMEM((samples, REACH), BF16),
            pltpu.VMEM((samples, REACH), BF16),
            pltpu.VMEM((CHUNK, CHUNK), F32),
            pltpu.VMEM((PAIR, REACH), F32),
            pltpu.VMEM((chunks, 3, PAIR, PAIR), F32),
            pltpu.VMEM((chunks, 3, PAIR, PAIR), F32),
            pltpu.VMEM((2, chunks, 3, PAIR, PAIR), jnp.int16),
            pltpu.VMEM((2, chunks, 3, PAIR, PAIR), jnp.int16),
            pltpu.VMEM((2, chunks, 8, PAIR), F32),
            pltpu.VMEM((2, chunks, 8, PAIR), F32),
            pltpu.VMEM((PAIR, PAIR), F32),
            pltpu.VMEM((3, rows + 2 * REACH, LANES), F32),
            pltpu.VMEM((3, rows + 2 * REACH, 2 * LANES), BF16),
            pltpu.VMEM((rows // PAIR, 2 * PAIR, WIDE), BF16),
            pltpu.VMEM((3, rows, LANES), F32),
            pltpu.VMEM((rows, LANES), F32),
            pltpu.VMEM((rows, LANES), F32),
            pltpu.VMEM((3, n_smp, 8, LANES), F32),
            dma((8,)),
            dma((chunks,)),
            dma((2, SIDES)),
            dma((3, 2)),
            dma((3, 2)),
            dma((3, n_smp)),
            dma((3, n_smp)),
            dma((2, chunks)),
            dma((2, chunks)),
            dma((2, chunks)),
            dma((2, chunks)),
            dma((2,)),
            dma((cols // PAIR + 1,)),
        ],
        compiler_params=pltpu.CompilerParams(
            collective_id=0, has_side_effects=True, vmem_limit_bytes=60 * 1024 * 1024
        ),
    )(
        dosage,
        allele_mean.reshape(1, -1),
        snp_scale.reshape(1, -1),
        band_next,
        jnp.transpose(ld_prev),
        band_prev,
        zscores,
        jnp.transpose(observed),
    )
    return jnp.transpose(ld_next), imputed[:, :traits]


def solution(mesh):
    sizes = (mesh.shape["smp"], mesh.shape["snp"], mesh.shape["pair"])
    return jax.shard_map(
        functools.partial(local, sizes),
        mesh=mesh,
        in_specs=(
            P(("grp", "smp"), ("snp", "pair")),
            P("grp"),
            P("grp"),
            P("grp"),
            P(("grp", "smp"), None),
            P("grp"),
            P(("grp", "smp"), ("snp", "pair")),
            P(("grp", "smp"), ("snp", "pair")),
        ),
        out_specs=(P(("grp", "snp", "pair"), None), P(("grp", "smp"), ("snp", "pair"))),
        check_vma=False,
    )
```

```python
import functools
import jax
import jax.numpy as jnp
from jax import lax
from jax.sharding import PartitionSpec as P
from jax.experimental import pallas as pl
from jax.experimental.pallas import tpu as pltpu

TILE = 64
BMAX = 2
TBLK = 64
SPAN = 2 * BMAX + 1
REACH = TILE * BMAX
PAIR = 2 * TILE
LANES = 128
WIDE = 384
CHUNK = 256
STEP = 512
SIDES = 4
HANDS = 4
CODE_TOP = 32767.0
CODE_LEAST = 1e-30
F32 = jnp.float32
BF16 = jnp.bfloat16
MESH = pl.DeviceIdType.MESH

ridge_term = 1.0


def split_two(value):
    high = value.astype(BF16)
    low = (value - high.astype(F32)).astype(BF16)
    return high, low


def folded(value):
    return jnp.sum(value.reshape(value.shape[0] // 8, 8, value.shape[1]), axis=0)


def total_row(value):
    return jnp.sum(value, axis=0, keepdims=True)


def tile_flags(widths, tile, count):
    here = widths[tile]
    flags = []
    for offset in range(-BMAX, BMAX + 1):
        place = tile + offset
        inside = (place >= 0) & (place < count)
        beside = widths[jnp.clip(place, 0, count - 1)]
        reach = abs(offset)
        flags.append(jnp.where(inside & (here >= reach) & (beside >= reach), 1.0, 0.0).astype(F32))
    return flags


def kernel(
    sizes,
    dosage, mean_far, scale_far, next_far, ld_far, prev_far, z_far, observed_far,
    ld_out, imputed_out,
    ld_next, imputed,
    mean, scale, band_next, ld_prev, band_prev, zscores, observed, seen,
    dos, dos_edge, dos_side, part_own, part_next, gram, summed, code_out, code_in, peak_out, peak_in, edge_in,
    vec, vec_two, band_two, image, res1, img0, red,
    in_sem, dos_sem, side_sem, vec_send, vec_recv, red_send, red_recv,
    code_send, code_recv, peak_send, peak_recv, edge_sem, out_sem,
):
    n_smp, n_snp, n_pair = sizes
    samples, cols = dos.shape
    rows = zscores.shape[0]
    tiles = rows // TILE
    chunks = cols // CHUNK
    blocks = cols // PAIR
    row_blocks = rows // PAIR
    tile_total = band_next.shape[0]
    me = lax.axis_index("smp")
    place = lax.axis_index("snp") * n_pair + lax.axis_index("pair")
    places = n_snp * n_pair
    first_col = place * cols
    order = list(range(1, chunks - 1)) + [0, chunks - 1]

    def at_place(index):
        return {"snp": index // n_pair, "pair": index % n_pair}

    has_left, has_right = place > 0, place < places - 1
    has_prev, has_next = me > 0, me < n_smp - 1
    left_id = at_place(jnp.maximum(place - 1, 0))
    right_id = at_place(jnp.minimum(place + 1, places - 1))

    edge_fetch = pltpu.make_async_copy(dosage.at[:, pl.ds(0, REACH)], dos_edge, in_sem.at[7])
    edge_fetch.start()
    small = []
    for index, (far, near) in enumerate(
        (
            (z_far, zscores),
            (observed_far, observed),
            (prev_far, band_prev),
            (ld_far, ld_prev),
            (mean_far, mean),
            (scale_far, scale),
            (next_far, band_next),
        )
    ):
        small.append(pltpu.make_async_copy(far, near, in_sem.at[index]))
        small[-1].start()
    fetches = []
    for chunk in order:
        span = pl.ds(chunk * CHUNK, CHUNK)
        fetch = pltpu.make_async_copy(dosage.at[:, span], dos.at[:, span], dos_sem.at[chunk])
        fetch.start()
        fetches.append(fetch)

    barrier = pltpu.get_barrier_semaphore()
    for step in range(1, n_smp):
        pl.semaphore_signal(
            barrier, inc=1, device_id={"smp": lax.rem(me + step, n_smp)}, device_id_type=MESH
        )

    @pl.when(has_left)
    def _():
        pl.semaphore_signal(barrier, inc=1, device_id=left_id, device_id_type=MESH)

    @pl.when(has_right)
    def _():
        pl.semaphore_signal(barrier, inc=1, device_id=right_id, device_id_type=MESH)

    def side_copies():
        part = samples // SIDES
        return [
            pltpu.make_async_remote_copy(
                src_ref=dos_edge.at[pl.ds(index * part, part)],
                dst_ref=dos_side.at[pl.ds(index * part, part)],
                send_sem=side_sem.at[0, index],
                recv_sem=side_sem.at[1, index],
                device_id=left_id,
                device_id_type=MESH,
            )
            for index in range(SIDES)
        ]

    for turn in range(3):

        @pl.when(me == 0)
        def _():
            vec[turn, pl.ds(0, REACH), :] = jnp.zeros((REACH, LANES), F32)

        @pl.when(me == n_smp - 1)
        def _():
            vec[turn, pl.ds(REACH + rows, REACH), :] = jnp.zeros((REACH, LANES), F32)

    edge_fetch.wait()
    pl.semaphore_wait(
        barrier,
        n_smp - 1 + jnp.where(has_left, 1, 0) + jnp.where(has_right, 1, 0),
    )

    @pl.when(has_left)
    def _():
        for copy in side_copies():
            copy.start()

    def put_vector(turn, tile, value):
        span = pl.ds(pl.multiple_of(REACH + tile * PAIR, PAIR), PAIR)
        vec[turn, span, :] = value
        high, low = split_two(value)
        vec_two[turn, span, 0:LANES] = high
        vec_two[turn, span, LANES : 2 * LANES] = low

    def own_rows(tile):
        return pl.ds(pl.multiple_of(tile * PAIR, PAIR), PAIR)

    def vec_rows(tile):
        return pl.ds(pl.multiple_of(REACH + tile * PAIR, PAIR), PAIR)

    def halo_copies(turn):
        up = pltpu.make_async_remote_copy(
            src_ref=vec.at[turn, pl.ds(REACH, REACH)],
            dst_ref=vec.at[turn, pl.ds(REACH + rows, REACH)],
            send_sem=vec_send.at[turn, 0],
            recv_sem=vec_recv.at[turn, 0],
            device_id={"smp": jnp.maximum(me - 1, 0)},
            device_id_type=MESH,
        )
        down = pltpu.make_async_remote_copy(
            src_ref=vec.at[turn, pl.ds(rows, REACH)],
            dst_ref=vec.at[turn, pl.ds(0, REACH)],
            send_sem=vec_send.at[turn, 1],
            recv_sem=vec_recv.at[turn, 1],
            device_id={"smp": jnp.minimum(me + 1, n_smp - 1)},
            device_id_type=MESH,
        )
        return up, down

    def send_halos(turn):
        up, down = halo_copies(turn)

        @pl.when(has_prev)
        def _():
            up.start()

        @pl.when(has_next)
        def _():
            down.start()

    def take_halos(turn):
        up, down = halo_copies(turn)

        @pl.when(has_next)
        def _():
            up.wait_recv()

        @pl.when(has_prev)
        def _():
            down.wait_recv()

        for start in (0, REACH + rows):
            high, low = split_two(vec[turn, pl.ds(start, REACH), :])
            vec_two[turn, pl.ds(start, REACH), 0:LANES] = high
            vec_two[turn, pl.ds(start, REACH), LANES : 2 * LANES] = low

    def red_copy(turn, step):
        return pltpu.make_async_remote_copy(
            src_ref=red.at[turn, me],
            dst_ref=red.at[turn, me],
            send_sem=red_send.at[turn, step],
            recv_sem=red_recv.at[turn, step],
            device_id={"smp": lax.rem(me + step, n_smp)},
            device_id_type=MESH,
        )

    def red_arrival(turn, step):
        sender = lax.rem(me - step + n_smp, n_smp)
        return pltpu.make_async_remote_copy(
            src_ref=red.at[turn, sender],
            dst_ref=red.at[turn, sender],
            send_sem=red_send.at[turn, step],
            recv_sem=red_recv.at[turn, step],
            device_id={"smp": lax.rem(me + step, n_smp)},
            device_id_type=MESH,
        )

    def send_sums(turn, sums):
        lines = [total_row(value) for value in sums]
        lines += [jnp.zeros((1, LANES), F32)] * (8 - len(lines))
        red[turn, me] = jnp.concatenate(lines, axis=0)
        for step in range(1, n_smp):
            red_copy(turn, step).start()

    def take_sums(turn):
        for step in range(1, n_smp):
            red_arrival(turn, step).wait_recv()
        whole = red[turn, 0]
        for index in range(1, n_smp):
            whole = whole + red[turn, index]
        return whole

    lane = lax.broadcasted_iota(jnp.int32, (PAIR, LANES), 1)
    line = lax.broadcasted_iota(jnp.int32, (PAIR, LANES), 0)

    small[0].wait()
    small[1].wait()
    for tile in range(row_blocks):
        here = observed[:, pl.ds(tile * PAIR, PAIR)].astype(F32)
        flags = jnp.zeros((LANES, PAIR), F32)
        for index in range(here.shape[0]):
            flags = jnp.where(line // TBLK == index, here[index : index + 1], flags)
        flags = jnp.transpose(flags)
        seen[pl.ds(tile * PAIR, PAIR), :] = flags
        put_vector(0, tile, flags * zscores[pl.ds(tile * PAIR, PAIR), :])

    send_halos(0)

    small[2].wait()
    small[3].wait()

    def two_flags(widths, first_tile, factor):
        left = tile_flags(widths, first_tile, tile_total)
        right = tile_flags(widths, first_tile + 1, tile_total)
        first_lanes = lane[0:1] < TILE
        return [jnp.where(first_lanes, a * factor, b * factor) for a, b in zip(left, right)]

    for tile in range(row_blocks):
        flags = two_flags(band_prev, me * tiles + 2 * tile, 1.0)
        columns = pl.ds(tile * PAIR, PAIR)
        parts = [
            ld_prev[pl.ds(index * TILE, TILE), columns] * flag for index, flag in enumerate(flags)
        ]
        blank = jnp.zeros((TILE, PAIR), F32)
        left, right = parts + [blank], [blank] + parts
        for third in range(3):
            pieces = [
                jnp.where(lane[0:TILE] < TILE, left[index], right[index])
                for index in (2 * third, 2 * third + 1)
            ]
            high, low = split_two(jnp.transpose(jnp.concatenate(pieces, axis=0)))
            band_two[tile, 0:PAIR, third * PAIR : (third + 1) * PAIR] = high
            band_two[tile, PAIR : 2 * PAIR, third * PAIR : (third + 1) * PAIR] = low

    for copy in small[4:]:
        copy.wait()

    ready = set()

    def make_ready(chunk):
        if chunk in ready:
            return
        ready.add(chunk)
        if chunk < chunks:
            fetches[order.index(chunk)].wait()
            return

        @pl.when(has_right)
        def _():
            for copy in side_copies():
                copy.wait_recv()

        @pl.when(jnp.logical_not(has_right))
        def _():
            dos_side[...] = jnp.zeros((samples, REACH), BF16)

    def standards(column, width):
        column = jnp.minimum(first_col + column, mean.shape[1] - width)
        where = pl.ds(pl.multiple_of(column, LANES), width)
        return mean[:, where], scale[:, where]

    def make_gram(chunk):
        make_ready(chunk)
        make_ready(chunk + 1)
        low = chunk * CHUNK
        mean_own, scale_own = standards(low, CHUNK)
        mean_next, scale_next = standards(low + CHUNK, REACH)
        keep = jnp.where(has_right, 1.0, 0.0) if chunk == chunks - 1 else 1.0
        scale_next = scale_next * keep

        def body(index, carry):
            span = pl.ds(pl.multiple_of(index * STEP, STEP), STEP)
            own = dos[span, low : low + CHUNK].astype(F32)
            own = ((own - mean_own) * scale_own).astype(BF16)
            if chunk < chunks - 1:
                beside = dos[span, low + CHUNK : low + CHUNK + REACH].astype(F32)
            else:
                beside = dos_side[span, :].astype(F32)
            beside = ((beside - mean_next) * scale_next).astype(BF16)
            dims = (((0,), (0,)), ((), ()))
            wide = lax.dot_general(own, own, dims, preferred_element_type=F32)
            late = lax.dot_general(own[:, PAIR:], beside, dims, preferred_element_type=F32)
            part_own[...] += wide
            part_next[...] += late
            return carry

        part_own[...] = jnp.zeros((CHUNK, CHUNK), F32)
        part_next[...] = jnp.zeros((PAIR, REACH), F32)
        lax.fori_loop(0, samples // STEP, body, 0)
        first, second = part_own[0:PAIR, 0:PAIR], part_own[PAIR:, PAIR:]
        gram[chunk, 0] = jnp.where(line <= lane, first, second)
        spare = total_row(jnp.where(line == lane, second, 0.0))
        unused = (line < TILE) & (lane >= TILE)
        for side in range(2):
            beside = part_own[0:PAIR, PAIR:] if side == 0 else part_next[...]
            held = spare if side == 0 else pltpu.roll(spare, TILE, 1)
            held = jnp.where(line == 0, held, 0.0)
            gram[chunk, 1 + side] = jnp.where(unused, held, beside)

    half = n_smp // 2
    first_way = jnp.where(me < half, 0, 1)
    second_way = 1 - first_way
    at_end = (me == 0) | (me == n_smp - 1)

    def running_copies(way, chunk):
        ahead = {"smp": jnp.clip(me + 1 - 2 * way, 0, n_smp - 1)}
        return [
            pltpu.make_async_remote_copy(
                src_ref=source.at[way, chunk],
                dst_ref=target.at[way, chunk],
                send_sem=send.at[way, chunk],
                recv_sem=recv.at[way, chunk],
                device_id=ahead,
                device_id_type=MESH,
            )
            for source, target, send, recv in (
                (code_out, code_in, code_send, code_recv),
                (peak_out, peak_in, peak_send, peak_recv),
            )
        ]

    def send_running(way, chunk, values):
        peaks = []
        for index, value in enumerate(values):
            peak = jnp.max(jnp.abs(value), axis=0, keepdims=True)
            factor = CODE_TOP / jnp.maximum(peak, CODE_LEAST)
            code = jnp.round(value * factor).astype(jnp.int32)
            code_out[way, chunk, index] = code.astype(jnp.int16)
            peaks.append(peak)
        peaks += [jnp.zeros((1, LANES), F32)] * (8 - len(peaks))
        peak_out[way, chunk] = jnp.concatenate(peaks, axis=0)
        for copy in running_copies(way, chunk):
            copy.start()

    def take_running(way, chunk):
        for copy in running_copies(way, chunk):
            copy.wait_recv()
        peaks = peak_in[way, chunk] * (1.0 / CODE_TOP)
        return [
            code_in[way, chunk, index].astype(jnp.int32).astype(F32) * peaks[index : index + 1]
            for index in range(3)
        ]

    def first_pass_end(chunk):
        @pl.when(at_end)
        def _():
            values = [gram[chunk, index] for index in range(3)]
            for index in range(3):
                summed[chunk, index] = values[index]
            send_running(first_way, chunk, values)

    def first_pass_inner(chunk):
        @pl.when(jnp.logical_not(at_end))
        def _():
            values = take_running(first_way, chunk)
            values = [value + gram[chunk, index] for index, value in enumerate(values)]
            for index in range(3):
                summed[chunk, index] = values[index]
            send_running(first_way, chunk, values)

    def edge_copy():
        return pltpu.make_async_remote_copy(
            src_ref=summed.at[chunks - 1, 2],
            dst_ref=edge_in,
            send_sem=edge_sem.at[0],
            recv_sem=edge_sem.at[1],
            device_id=right_id,
            device_id_type=MESH,
        )

    def second_pass(chunk):
        values = take_running(second_way, chunk)

        @pl.when(jnp.logical_not(at_end))
        def _():
            send_running(
                second_way,
                chunk,
                [value + gram[chunk, index] for index, value in enumerate(values)],
            )

        for index in range(3):
            summed[chunk, index] += values[index]
        if chunk == chunks - 1:

            @pl.when(has_right)
            def _():
                edge_copy().start()

    def product(turn, tile):
        window = vec_two[turn, pl.ds(pl.multiple_of(tile * PAIR, PAIR), WIDE), :]
        out = jnp.dot(band_two[tile], window, preferred_element_type=F32)
        value = (out[0:PAIR, 0:LANES] + out[PAIR:, LANES:]) + (
            out[0:PAIR, LANES:] + out[PAIR:, 0:LANES]
        )
        image[turn, own_rows(tile), :] = value
        return value

    def operated(turn, tile, vector):
        flag = seen[own_rows(tile), :]
        masked = flag * vector
        return flag * (product(turn, tile) + ridge_term * masked) + (1.0 - flag) * vector

    def over_tiles(turn, body, start):
        inner = max(row_blocks - 2, 0)
        edges = sorted({0, row_blocks - 1})
        carry = start
        if inner:
            unroll = 2 if inner % 2 == 0 else 1
            carry = lax.fori_loop(1, 1 + inner, body, carry, unroll=unroll)
        take_halos(turn)
        for tile in edges:
            carry = body(tile, carry)
        return carry

    nothing = jnp.zeros((8, LANES), F32)

    def start_solver():
        def body(tile, carry):
            square, cross = carry
            here = vec[0, vec_rows(tile), :]
            out = operated(0, tile, here)
            put_vector(1, tile, seen[own_rows(tile), :] * out)
            return square + folded(here * here), cross + folded(here * out)

        square, cross = over_tiles(0, body, (nothing, nothing))
        send_halos(1)
        send_sums(0, [square, cross])

    def next_solver():
        def body(tile, carry):
            img0[own_rows(tile), :] = operated(1, tile, vec[1, vec_rows(tile), :])
            return carry

        over_tiles(1, body, 0)
        whole = take_sums(0)
        norm0, curve0 = whole[0:1], whole[1:2]
        alpha0 = norm0 / curve0

        def update(tile, carry):
            square, cross, mixed = carry
            r0 = vec[0, vec_rows(tile), :]
            w0 = vec[1, vec_rows(tile), :]
            r1 = r0 - alpha0 * w0
            w1 = w0 - alpha0 * img0[own_rows(tile), :]
            res1[own_rows(tile), :] = r1
            put_vector(2, tile, seen[own_rows(tile), :] * w1)
            return (
                square + folded(r1 * r1),
                cross + folded(r1 * w1),
                mixed + folded(r1 * w0 + r0 * w1),
            )

        sums = lax.fori_loop(0, row_blocks, update, (nothing, nothing, nothing))
        send_halos(2)
        send_sums(1, list(sums))
        return norm0, curve0, alpha0

    def last_solver(norm0, curve0, alpha0):
        def body(tile, carry):
            here = vec[2, vec_rows(tile), :]
            imputed[own_rows(tile), :] = operated(2, tile, here)
            return carry

        over_tiles(2, body, 0)
        whole = take_sums(1)
        norm1 = whole[0:1]
        beta1 = norm1 / norm0
        curve1 = whole[1:2] + beta1 * whole[2:3] + beta1 * beta1 * curve0
        alpha1 = norm1 / curve1

        def update(tile, carry):
            square, cross, mixed = carry
            r0 = vec[0, vec_rows(tile), :]
            w0 = vec[1, vec_rows(tile), :]
            r1 = res1[own_rows(tile), :]
            w1 = vec[2, vec_rows(tile), :]
            p1 = r1 + beta1 * r0
            s1 = w1 + beta1 * w0
            z1 = imputed[own_rows(tile), :] + beta1 * img0[own_rows(tile), :]
            r2 = r1 - alpha1 * s1
            w2 = w1 - alpha1 * z1
            return (
                square + folded(r2 * r2),
                cross + folded(r2 * w2),
                mixed + folded(r2 * s1 + p1 * w2),
            )

        sums = lax.fori_loop(0, row_blocks, update, (nothing, nothing, nothing))
        send_sums(2, list(sums))
        return norm1, curve1, alpha1, beta1

    def end_solver(alpha0, norm1, curve1, alpha1, beta1):
        whole = take_sums(2)
        beta2 = whole[0:1] / norm1
        curve2 = whole[1:2] + beta2 * whole[2:3] + beta2 * beta2 * curve1
        alpha2 = whole[0:1] / curve2
        first = (1.0 + beta1, -alpha0)
        second = (
            1.0 + beta2 * first[0],
            -alpha0 - alpha1 * beta1 + beta2 * first[1],
            -alpha1,
        )
        part0 = alpha0 + alpha1 * first[0] + alpha2 * second[0]
        part1 = alpha1 * first[1] + alpha2 * second[1]
        part2 = alpha2 * second[2]

        def body(tile, carry):
            span = own_rows(tile)
            imputed[span, :] = (
                part0 * image[0, span, :] + part1 * image[1, span, :] + part2 * image[2, span, :]
            )
            return carry

        lax.fori_loop(0, row_blocks, body, 0)

    def make_and_send(chunk):
        make_gram(chunk)
        first_pass_end(chunk)

    make_and_send(order[0])
    start_solver()
    if chunks > 2:
        make_and_send(order[1])
        first_pass_inner(order[0])
    scalars0 = next_solver()
    for position in range(2, chunks - 1):
        make_and_send(order[position])
        first_pass_inner(order[position - 1])
    scalars1 = last_solver(*scalars0)
    make_and_send(order[-1])
    for chunk in order[-2:]:
        first_pass_inner(chunk)

    @pl.when(jnp.logical_not(at_end))
    def _():
        for chunk in order:
            second_pass(chunk)

    end_solver(scalars0[2], *scalars1)
    results = [pltpu.make_async_copy(imputed, imputed_out, out_sem.at[blocks])]
    results[0].start()

    inverse = 1.0 / (samples * n_smp)

    def assemble(block, before):
        chunk, side = block // 2, block % 2
        packed = summed[chunk, 0]
        turned = jnp.transpose(packed)
        if side:
            spare = jnp.where(
                lane[0:1] >= TILE,
                summed[chunk, 1, 0:1],
                pltpu.roll(summed[chunk, 2, 0:1], TILE, 1),
            )
            diagonal = jnp.where(line > lane, packed, jnp.where(line < lane, turned, spare))
        else:
            diagonal = jnp.where(line <= lane, packed, turned)
        after = jnp.transpose(summed[chunk, 1 + side])
        stack = [before[0:TILE], before[TILE:], diagonal[0:TILE], diagonal[TILE:]]
        stack += [after[0:TILE], after[TILE:]]
        flags = two_flags(band_next, place * (cols // TILE) + 2 * block, inverse)
        for index, flag in enumerate(flags):
            value = jnp.where(lane[0:TILE] < TILE, stack[index], stack[index + 1])
            ld_next[pl.ds(index * TILE, TILE), pl.ds(block * PAIR, PAIR)] = value * flag
        columns = pl.ds(block * PAIR, PAIR)
        results.append(
            pltpu.make_async_copy(ld_next.at[:, columns], ld_out.at[:, columns], out_sem.at[block])
        )
        results[-1].start()

    done = set()

    def assemble_ready():
        for block in range(1, blocks):
            needed = {block // 2, (block - 1) // 2}
            if block not in assembled and needed <= done:
                assembled.add(block)
                assemble(block, summed[(block - 1) // 2, 1 + (block - 1) % 2])

    assembled = set()
    for chunk in order:

        @pl.when(at_end)
        def _():
            second_pass(chunk)

        done.add(chunk)
        assemble_ready()

    @pl.when(has_left)
    def _():
        edge_copy().wait_recv()

    @pl.when(jnp.logical_not(has_left))
    def _():
        edge_in[...] = jnp.zeros((PAIR, PAIR), F32)

    assemble(0, edge_in[...])

    for copy in results:
        copy.wait()

    @pl.when(has_left)
    def _():
        for copy in side_copies():
            copy.wait_send()

    @pl.when(has_right)
    def _():
        edge_copy().wait_send()

    for turn in range(3):
        up, down = halo_copies(turn)

        @pl.when(has_prev)
        def _():
            up.wait_send()

        @pl.when(has_next)
        def _():
            down.wait_send()

        for step in range(1, n_smp):
            red_copy(turn, step).wait_send()

    for chunk in range(chunks):
        for copy in running_copies(first_way, chunk):
            copy.wait_send()

        @pl.when(jnp.logical_not(at_end))
        def _():
            for copy in running_copies(second_way, chunk):
                copy.wait_send()


def hand_over(ld_held, imputed_held, ld_next, imputed, sems):
    copies = []
    for index, (source, target) in enumerate(((ld_held, ld_next), (imputed_held, imputed))):
        part = source.shape[0] // HANDS
        for piece in range(HANDS):
            span = pl.ds(piece * part, part)
            copies.append(
                pltpu.make_async_copy(source.at[span], target.at[span], sems.at[index, piece])
            )
    for copy in copies:
        copy.start()
    for copy in copies:
        copy.wait()


def local(sizes, dosage, allele_mean, snp_scale, band_next, ld_prev, band_prev, zscores, observed):
    n_smp = sizes[0]
    samples, cols = dosage.shape
    rows, traits = zscores.shape
    chunks = cols // CHUNK
    if traits < LANES:
        zscores = jnp.pad(zscores, ((0, 0), (0, LANES - traits)))
    far = pl.BlockSpec(memory_space=pltpu.HBM)
    dma = pltpu.SemaphoreType.DMA
    ld_next, imputed = pl.pallas_call(
        functools.partial(kernel, sizes),
        out_shape=(
            jax.ShapeDtypeStruct((SPAN * TILE, cols), F32),
            jax.ShapeDtypeStruct((rows, LANES), F32),
        ),
        in_specs=[far] * 8,
        out_specs=(far, far),
        scratch_shapes=[
            pltpu.VMEM((SPAN * TILE, cols), F32),
            pltpu.VMEM((rows, LANES), F32),
            pltpu.VMEM((1, allele_mean.shape[0]), F32),
            pltpu.VMEM((1, allele_mean.shape[0]), F32),
            pltpu.SMEM(band_next.shape, jnp.int32),
            pltpu.VMEM((SPAN * TILE, rows), F32),
            pltpu.SMEM(band_prev.shape, jnp.int32),
            pltpu.VMEM((rows, LANES), F32),
            pltpu.VMEM((observed.shape[1], rows), jnp.int32),
            pltpu.VMEM((rows, LANES), F32),
            pltpu.VMEM((samples, cols), BF16),
            pltpu.VMEM((samples, REACH), BF16),
            pltpu.VMEM((samples, REACH), BF16),
            pltpu.VMEM((CHUNK, CHUNK), F32),
            pltpu.VMEM((PAIR, REACH), F32),
            pltpu.VMEM((chunks, 3, PAIR, PAIR), F32),
            pltpu.VMEM((chunks, 3, PAIR, PAIR), F32),
            pltpu.VMEM((2, chunks, 3, PAIR, PAIR), jnp.int16),
            pltpu.VMEM((2, chunks, 3, PAIR, PAIR), jnp.int16),
            pltpu.VMEM((2, chunks, 8, PAIR), F32),
            pltpu.VMEM((2, chunks, 8, PAIR), F32),
            pltpu.VMEM((PAIR, PAIR), F32),
            pltpu.VMEM((3, rows + 2 * REACH, LANES), F32),
            pltpu.VMEM((3, rows + 2 * REACH, 2 * LANES), BF16),
            pltpu.VMEM((rows // PAIR, 2 * PAIR, WIDE), BF16),
            pltpu.VMEM((3, rows, LANES), F32),
            pltpu.VMEM((rows, LANES), F32),
            pltpu.VMEM((rows, LANES), F32),
            pltpu.VMEM((3, n_smp, 8, LANES), F32),
            dma((8,)),
            dma((chunks,)),
            dma((2, SIDES)),
            dma((3, 2)),
            dma((3, 2)),
            dma((3, n_smp)),
            dma((3, n_smp)),
            dma((2, chunks)),
            dma((2, chunks)),
            dma((2, chunks)),
            dma((2, chunks)),
            dma((2,)),
            dma((cols // PAIR + 1,)),
        ],
        compiler_params=pltpu.CompilerParams(
            collective_id=0, has_side_effects=True, vmem_limit_bytes=60 * 1024 * 1024
        ),
    )(
        dosage,
        allele_mean.reshape(1, -1),
        snp_scale.reshape(1, -1),
        band_next,
        jnp.transpose(ld_prev),
        band_prev,
        zscores,
        jnp.transpose(observed),
    )
    ld_next, imputed = pl.pallas_call(
        hand_over,
        out_shape=(
            jax.ShapeDtypeStruct(ld_next.shape, F32),
            jax.ShapeDtypeStruct(imputed.shape, F32),
        ),
        in_specs=[far, far],
        out_specs=(far, far),
        scratch_shapes=[dma((2, HANDS))],
        compiler_params=pltpu.CompilerParams(vmem_limit_bytes=60 * 1024 * 1024),
    )(ld_next, imputed)
    return jnp.transpose(ld_next), imputed[:, :traits]


def solution(mesh):
    sizes = (mesh.shape["smp"], mesh.shape["snp"], mesh.shape["pair"])
    return jax.shard_map(
        functools.partial(local, sizes),
        mesh=mesh,
        in_specs=(
            P(("grp", "smp"), ("snp", "pair")),
            P("grp"),
            P("grp"),
            P("grp"),
            P(("grp", "smp"), None),
            P("grp"),
            P(("grp", "smp"), ("snp", "pair")),
            P(("grp", "smp"), ("snp", "pair")),
        ),
        out_specs=(P(("grp", "snp", "pair"), None), P(("grp", "smp"), ("snp", "pair"))),
        check_vma=False,
    )
```

```python
import functools
import jax
import jax.numpy as jnp
from jax import lax
from jax.sharding import PartitionSpec as P
from jax.experimental import pallas as pl
from jax.experimental.pallas import tpu as pltpu

TILE = 64
BMAX = 2
TBLK = 64
SPAN = 2 * BMAX + 1
REACH = TILE * BMAX
PAIR = 2 * TILE
LANES = 128
WIDE = 384
CHUNK = 256
STEP = 512
HANDS = 4
CODE_TOP = 32767.0
CODE_LEAST = 1e-30
F32 = jnp.float32
BF16 = jnp.bfloat16
MESH = pl.DeviceIdType.MESH

ridge_term = 1.0


def split_two(value):
    high = value.astype(BF16)
    low = (value - high.astype(F32)).astype(BF16)
    return high, low


def folded(value):
    return jnp.sum(value.reshape(value.shape[0] // 8, 8, value.shape[1]), axis=0)


def total_row(value):
    return jnp.sum(value, axis=0, keepdims=True)


def tile_flags(widths, tile, count):
    here = widths[tile]
    flags = []
    for offset in range(-BMAX, BMAX + 1):
        place = tile + offset
        inside = (place >= 0) & (place < count)
        beside = widths[jnp.clip(place, 0, count - 1)]
        reach = abs(offset)
        flags.append(jnp.where(inside & (here >= reach) & (beside >= reach), 1.0, 0.0).astype(F32))
    return flags


def kernel(
    sizes,
    dosage, mean_far, scale_far, next_far, ld_far, prev_far, z_far, observed_far,
    ld_out, imputed_out,
    ld_next, imputed,
    mean, scale, band_next, ld_prev, band_prev, zscores, observed, seen,
    dos, dos_side, part_own, part_next, gram, summed, code_out, code_in, peak_out, peak_in, edge_in,
    vec, vec_two, band_two, image, res1, img0, red,
    in_sem, dos_sem, side_sem, vec_send, vec_recv, red_send, red_recv,
    code_send, code_recv, peak_send, peak_recv, edge_sem, out_sem,
):
    n_smp, n_snp, n_pair = sizes
    samples, cols = dos.shape
    rows = zscores.shape[0]
    tiles = rows // TILE
    chunks = cols // CHUNK
    blocks = cols // PAIR
    row_blocks = rows // PAIR
    tile_total = band_next.shape[0]
    me = lax.axis_index("smp")
    place = lax.axis_index("snp") * n_pair + lax.axis_index("pair")
    places = n_snp * n_pair
    first_col = place * cols
    order = list(range(1, chunks)) + [0]

    def at_place(index):
        return {"snp": index // n_pair, "pair": index % n_pair}

    has_left, has_right = place > 0, place < places - 1
    has_prev, has_next = me > 0, me < n_smp - 1
    left_id = at_place(jnp.maximum(place - 1, 0))
    right_id = at_place(jnp.minimum(place + 1, places - 1))

    small = []
    for index, (far, near) in enumerate(
        (
            (z_far, zscores),
            (observed_far, observed),
            (prev_far, band_prev),
            (ld_far, ld_prev),
            (mean_far, mean),
            (scale_far, scale),
            (next_far, band_next),
        )
    ):
        small.append(pltpu.make_async_copy(far, near, in_sem.at[index]))
        small[-1].start()
    fetches = []
    for chunk in order:
        span = pl.ds(chunk * CHUNK, CHUNK)
        fetch = pltpu.make_async_copy(dosage.at[:, span], dos.at[:, span], dos_sem.at[chunk])
        fetch.start()
        fetches.append(fetch)

    barrier = pltpu.get_barrier_semaphore()
    for step in range(1, n_smp):
        pl.semaphore_signal(
            barrier, inc=1, device_id={"smp": lax.rem(me + step, n_smp)}, device_id_type=MESH
        )

    @pl.when(has_left)
    def _():
        pl.semaphore_signal(barrier, inc=1, device_id=left_id, device_id_type=MESH)

    @pl.when(has_right)
    def _():
        pl.semaphore_signal(barrier, inc=1, device_id=right_id, device_id_type=MESH)

    side_copy = pltpu.make_async_remote_copy(
        src_ref=dosage.at[:, pl.ds(0, REACH)],
        dst_ref=dos_side,
        send_sem=side_sem.at[0],
        recv_sem=side_sem.at[1],
        device_id=left_id,
        device_id_type=MESH,
    )

    for turn in range(3):

        @pl.when(me == 0)
        def _():
            vec[turn, pl.ds(0, REACH), :] = jnp.zeros((REACH, LANES), F32)

        @pl.when(me == n_smp - 1)
        def _():
            vec[turn, pl.ds(REACH + rows, REACH), :] = jnp.zeros((REACH, LANES), F32)

    def put_vector(turn, tile, value):
        span = pl.ds(pl.multiple_of(REACH + tile * PAIR, PAIR), PAIR)
        vec[turn, span, :] = value
        high, low = split_two(value)
        vec_two[turn, span, 0:LANES] = high
        vec_two[turn, span, LANES : 2 * LANES] = low

    def own_rows(tile):
        return pl.ds(pl.multiple_of(tile * PAIR, PAIR), PAIR)

    def vec_rows(tile):
        return pl.ds(pl.multiple_of(REACH + tile * PAIR, PAIR), PAIR)

    def halo_copies(turn):
        up = pltpu.make_async_remote_copy(
            src_ref=vec.at[turn, pl.ds(REACH, REACH)],
            dst_ref=vec.at[turn, pl.ds(REACH + rows, REACH)],
            send_sem=vec_send.at[turn, 0],
            recv_sem=vec_recv.at[turn, 0],
            device_id={"smp": jnp.maximum(me - 1, 0)},
            device_id_type=MESH,
        )
        down = pltpu.make_async_remote_copy(
            src_ref=vec.at[turn, pl.ds(rows, REACH)],
            dst_ref=vec.at[turn, pl.ds(0, REACH)],
            send_sem=vec_send.at[turn, 1],
            recv_sem=vec_recv.at[turn, 1],
            device_id={"smp": jnp.minimum(me + 1, n_smp - 1)},
            device_id_type=MESH,
        )
        return up, down

    def send_halos(turn):
        up, down = halo_copies(turn)

        @pl.when(has_prev)
        def _():
            up.start()

        @pl.when(has_next)
        def _():
            down.start()

    def take_halos(turn):
        up, down = halo_copies(turn)

        @pl.when(has_next)
        def _():
            up.wait_recv()

        @pl.when(has_prev)
        def _():
            down.wait_recv()

        for start in (0, REACH + rows):
            high, low = split_two(vec[turn, pl.ds(start, REACH), :])
            vec_two[turn, pl.ds(start, REACH), 0:LANES] = high
            vec_two[turn, pl.ds(start, REACH), LANES : 2 * LANES] = low

    def red_copy(turn, step):
        return pltpu.make_async_remote_copy(
            src_ref=red.at[turn, me],
            dst_ref=red.at[turn, me],
            send_sem=red_send.at[turn, step],
            recv_sem=red_recv.at[turn, step],
            device_id={"smp": lax.rem(me + step, n_smp)},
            device_id_type=MESH,
        )

    def red_arrival(turn, step):
        sender = lax.rem(me - step + n_smp, n_smp)
        return pltpu.make_async_remote_copy(
            src_ref=red.at[turn, sender],
            dst_ref=red.at[turn, sender],
            send_sem=red_send.at[turn, step],
            recv_sem=red_recv.at[turn, step],
            device_id={"smp": lax.rem(me + step, n_smp)},
            device_id_type=MESH,
        )

    def send_sums(turn, sums):
        lines = [total_row(value) for value in sums]
        lines += [jnp.zeros((1, LANES), F32)] * (8 - len(lines))
        red[turn, me] = jnp.concatenate(lines, axis=0)
        for step in range(1, n_smp):
            red_copy(turn, step).start()

    def take_sums(turn):
        for step in range(1, n_smp):
            red_arrival(turn, step).wait_recv()
        whole = red[turn, 0]
        for index in range(1, n_smp):
            whole = whole + red[turn, index]
        return whole

    lane = lax.broadcasted_iota(jnp.int32, (PAIR, LANES), 1)
    line = lax.broadcasted_iota(jnp.int32, (PAIR, LANES), 0)

    small[0].wait()
    small[1].wait()
    for tile in range(row_blocks):
        here = observed[:, pl.ds(tile * PAIR, PAIR)].astype(F32)
        flags = jnp.zeros((LANES, PAIR), F32)
        for index in range(here.shape[0]):
            flags = jnp.where(line // TBLK == index, here[index : index + 1], flags)
        flags = jnp.transpose(flags)
        seen[pl.ds(tile * PAIR, PAIR), :] = flags
        put_vector(0, tile, flags * zscores[pl.ds(tile * PAIR, PAIR), :])

    pl.semaphore_wait(
        barrier,
        n_smp - 1 + jnp.where(has_left, 1, 0) + jnp.where(has_right, 1, 0),
    )

    @pl.when(has_left)
    def _():
        side_copy.start()

    send_halos(0)

    small[2].wait()
    small[3].wait()

    def two_flags(widths, first_tile, factor):
        left = tile_flags(widths, first_tile, tile_total)
        right = tile_flags(widths, first_tile + 1, tile_total)
        first_lanes = lane[0:1] < TILE
        return [jnp.where(first_lanes, a * factor, b * factor) for a, b in zip(left, right)]

    for tile in range(row_blocks):
        flags = two_flags(band_prev, me * tiles + 2 * tile, 1.0)
        columns = pl.ds(tile * PAIR, PAIR)
        parts = [
            ld_prev[pl.ds(index * TILE, TILE), columns] * flag for index, flag in enumerate(flags)
        ]
        blank = jnp.zeros((TILE, PAIR), F32)
        left, right = parts + [blank], [blank] + parts
        for third in range(3):
            pieces = [
                jnp.where(lane[0:TILE] < TILE, left[index], right[index])
                for index in (2 * third, 2 * third + 1)
            ]
            high, low = split_two(jnp.transpose(jnp.concatenate(pieces, axis=0)))
            band_two[tile, 0:PAIR, third * PAIR : (third + 1) * PAIR] = high
            band_two[tile, PAIR : 2 * PAIR, third * PAIR : (third + 1) * PAIR] = low

    for copy in small[4:]:
        copy.wait()

    ready = set()

    def make_ready(chunk):
        if chunk in ready:
            return
        ready.add(chunk)
        if chunk < chunks:
            fetches[order.index(chunk)].wait()
            return

        @pl.when(has_right)
        def _():
            side_copy.wait_recv()

        @pl.when(jnp.logical_not(has_right))
        def _():
            dos_side[...] = jnp.zeros((samples, REACH), BF16)

    def standards(column, width):
        column = jnp.minimum(first_col + column, mean.shape[1] - width)
        where = pl.ds(pl.multiple_of(column, LANES), width)
        return mean[:, where], scale[:, where]

    def make_gram(chunk):
        make_ready(chunk)
        make_ready(chunk + 1)
        low = chunk * CHUNK
        mean_own, scale_own = standards(low, CHUNK)
        mean_next, scale_next = standards(low + CHUNK, REACH)
        keep = jnp.where(has_right, 1.0, 0.0) if chunk == chunks - 1 else 1.0
        scale_next = scale_next * keep

        def body(index, carry):
            span = pl.ds(pl.multiple_of(index * STEP, STEP), STEP)
            own = dos[span, low : low + CHUNK].astype(F32)
            own = ((own - mean_own) * scale_own).astype(BF16)
            if chunk < chunks - 1:
                beside = dos[span, low + CHUNK : low + CHUNK + REACH].astype(F32)
            else:
                beside = dos_side[span, :].astype(F32)
            beside = ((beside - mean_next) * scale_next).astype(BF16)
            dims = (((0,), (0,)), ((), ()))
            wide = lax.dot_general(own, own, dims, preferred_element_type=F32)
            late = lax.dot_general(own[:, PAIR:], beside, dims, preferred_element_type=F32)
            part_own[...] += wide
            part_next[...] += late
            return carry

        part_own[...] = jnp.zeros((CHUNK, CHUNK), F32)
        part_next[...] = jnp.zeros((PAIR, REACH), F32)
        lax.fori_loop(0, samples // STEP, body, 0)
        first, second = part_own[0:PAIR, 0:PAIR], part_own[PAIR:, PAIR:]
        gram[chunk, 0] = jnp.where(line <= lane, first, second)
        spare = total_row(jnp.where(line == lane, second, 0.0))
        unused = (line < TILE) & (lane >= TILE)
        for side in range(2):
            beside = part_own[0:PAIR, PAIR:] if side == 0 else part_next[...]
            held = spare if side == 0 else pltpu.roll(spare, TILE, 1)
            held = jnp.where(line == 0, held, 0.0)
            gram[chunk, 1 + side] = jnp.where(unused, held, beside)

    half = n_smp // 2
    first_way = jnp.where(me < half, 0, 1)
    second_way = 1 - first_way
    at_end = (me == 0) | (me == n_smp - 1)

    def running_copies(way, chunk):
        ahead = {"smp": jnp.clip(me + 1 - 2 * way, 0, n_smp - 1)}
        return [
            pltpu.make_async_remote_copy(
                src_ref=source.at[way, chunk],
                dst_ref=target.at[way, chunk],
                send_sem=send.at[way, chunk],
                recv_sem=recv.at[way, chunk],
                device_id=ahead,
                device_id_type=MESH,
            )
            for source, target, send, recv in (
                (code_out, code_in, code_send, code_recv),
                (peak_out, peak_in, peak_send, peak_recv),
            )
        ]

    def send_running(way, chunk, values):
        peaks = []
        for index, value in enumerate(values):
            peak = jnp.max(jnp.abs(value), axis=0, keepdims=True)
            factor = CODE_TOP / jnp.maximum(peak, CODE_LEAST)
            code = jnp.round(value * factor).astype(jnp.int32)
            code_out[way, chunk, index] = code.astype(jnp.int16)
            peaks.append(peak)
        peaks += [jnp.zeros((1, LANES), F32)] * (8 - len(peaks))
        peak_out[way, chunk] = jnp.concatenate(peaks, axis=0)
        for copy in running_copies(way, chunk):
            copy.start()

    def take_running(way, chunk):
        for copy in running_copies(way, chunk):
            copy.wait_recv()
        peaks = peak_in[way, chunk] * (1.0 / CODE_TOP)
        return [
            code_in[way, chunk, index].astype(jnp.int32).astype(F32) * peaks[index : index + 1]
            for index in range(3)
        ]

    def first_pass_end(chunk):
        @pl.when(at_end)
        def _():
            values = [gram[chunk, index] for index in range(3)]
            for index in range(3):
                summed[chunk, index] = values[index]
            send_running(first_way, chunk, values)

    def first_pass_inner(chunk):
        @pl.when(jnp.logical_not(at_end))
        def _():
            values = take_running(first_way, chunk)
            values = [value + gram[chunk, index] for index, value in enumerate(values)]
            for index in range(3):
                summed[chunk, index] = values[index]
            send_running(first_way, chunk, values)

    def edge_copy():
        return pltpu.make_async_remote_copy(
            src_ref=summed.at[chunks - 1, 2],
            dst_ref=edge_in,
            send_sem=edge_sem.at[0],
            recv_sem=edge_sem.at[1],
            device_id=right_id,
            device_id_type=MESH,
        )

    def second_pass(chunk):
        values = take_running(second_way, chunk)

        @pl.when(jnp.logical_not(at_end))
        def _():
            send_running(
                second_way,
                chunk,
                [value + gram[chunk, index] for index, value in enumerate(values)],
            )

        for index in range(3):
            summed[chunk, index] += values[index]
        if chunk == chunks - 1:

            @pl.when(has_right)
            def _():
                edge_copy().start()

    def product(turn, tile):
        window = vec_two[turn, pl.ds(pl.multiple_of(tile * PAIR, PAIR), WIDE), :]
        out = jnp.dot(band_two[tile], window, preferred_element_type=F32)
        value = (out[0:PAIR, 0:LANES] + out[PAIR:, LANES:]) + (
            out[0:PAIR, LANES:] + out[PAIR:, 0:LANES]
        )
        image[turn, own_rows(tile), :] = value
        return value

    def operated(turn, tile, vector):
        flag = seen[own_rows(tile), :]
        masked = flag * vector
        return flag * (product(turn, tile) + ridge_term * masked) + (1.0 - flag) * vector

    def over_tiles(turn, body, start):
        inner = max(row_blocks - 2, 0)
        edges = sorted({0, row_blocks - 1})
        carry = start
        if inner:
            unroll = 2 if inner % 2 == 0 else 1
            carry = lax.fori_loop(1, 1 + inner, body, carry, unroll=unroll)
        take_halos(turn)
        for tile in edges:
            carry = body(tile, carry)
        return carry

    nothing = jnp.zeros((8, LANES), F32)

    def start_solver():
        def body(tile, carry):
            square, cross = carry
            here = vec[0, vec_rows(tile), :]
            out = operated(0, tile, here)
            put_vector(1, tile, seen[own_rows(tile), :] * out)
            return square + folded(here * here), cross + folded(here * out)

        square, cross = over_tiles(0, body, (nothing, nothing))
        send_halos(1)
        send_sums(0, [square, cross])

    def next_solver():
        def body(tile, carry):
            img0[own_rows(tile), :] = operated(1, tile, vec[1, vec_rows(tile), :])
            return carry

        over_tiles(1, body, 0)
        whole = take_sums(0)
        norm0, curve0 = whole[0:1], whole[1:2]
        alpha0 = norm0 / curve0

        def update(tile, carry):
            square, cross, mixed = carry
            r0 = vec[0, vec_rows(tile), :]
            w0 = vec[1, vec_rows(tile), :]
            r1 = r0 - alpha0 * w0
            w1 = w0 - alpha0 * img0[own_rows(tile), :]
            res1[own_rows(tile), :] = r1
            put_vector(2, tile, seen[own_rows(tile), :] * w1)
            return (
                square + folded(r1 * r1),
                cross + folded(r1 * w1),
                mixed + folded(r1 * w0 + r0 * w1),
            )

        sums = lax.fori_loop(0, row_blocks, update, (nothing, nothing, nothing))
        send_halos(2)
        send_sums(1, list(sums))
        return norm0, curve0, alpha0

    def last_solver(norm0, curve0, alpha0):
        def body(tile, carry):
            here = vec[2, vec_rows(tile), :]
            imputed[own_rows(tile), :] = operated(2, tile, here)
            return carry

        over_tiles(2, body, 0)
        whole = take_sums(1)
        norm1 = whole[0:1]
        beta1 = norm1 / norm0
        curve1 = whole[1:2] + beta1 * whole[2:3] + beta1 * beta1 * curve0
        alpha1 = norm1 / curve1

        def update(tile, carry):
            square, cross, mixed = carry
            r0 = vec[0, vec_rows(tile), :]
            w0 = vec[1, vec_rows(tile), :]
            r1 = res1[own_rows(tile), :]
            w1 = vec[2, vec_rows(tile), :]
            p1 = r1 + beta1 * r0
            s1 = w1 + beta1 * w0
            z1 = imputed[own_rows(tile), :] + beta1 * img0[own_rows(tile), :]
            r2 = r1 - alpha1 * s1
            w2 = w1 - alpha1 * z1
            return (
                square + folded(r2 * r2),
                cross + folded(r2 * w2),
                mixed + folded(r2 * s1 + p1 * w2),
            )

        sums = lax.fori_loop(0, row_blocks, update, (nothing, nothing, nothing))
        send_sums(2, list(sums))
        return norm1, curve1, alpha1, beta1

    def end_solver(alpha0, norm1, curve1, alpha1, beta1):
        whole = take_sums(2)
        beta2 = whole[0:1] / norm1
        curve2 = whole[1:2] + beta2 * whole[2:3] + beta2 * beta2 * curve1
        alpha2 = whole[0:1] / curve2
        first = (1.0 + beta1, -alpha0)
        second = (
            1.0 + beta2 * first[0],
            -alpha0 - alpha1 * beta1 + beta2 * first[1],
            -alpha1,
        )
        part0 = alpha0 + alpha1 * first[0] + alpha2 * second[0]
        part1 = alpha1 * first[1] + alpha2 * second[1]
        part2 = alpha2 * second[2]

        def body(tile, carry):
            span = own_rows(tile)
            imputed[span, :] = (
                part0 * image[0, span, :] + part1 * image[1, span, :] + part2 * image[2, span, :]
            )
            return carry

        lax.fori_loop(0, row_blocks, body, 0)

    def make_and_send(chunk):
        make_gram(chunk)
        first_pass_end(chunk)

    make_and_send(order[0])
    start_solver()
    if chunks > 2:
        make_and_send(order[1])
        first_pass_inner(order[0])
    scalars0 = next_solver()
    for place_in_order in range(2 if chunks > 2 else 1, chunks):
        make_and_send(order[place_in_order])
        first_pass_inner(order[place_in_order - 1])
    scalars1 = last_solver(*scalars0)
    first_pass_inner(order[-1])

    @pl.when(jnp.logical_not(at_end))
    def _():
        for chunk in order:
            second_pass(chunk)

    end_solver(scalars0[2], *scalars1)
    results = [pltpu.make_async_copy(imputed, imputed_out, out_sem.at[blocks])]
    results[0].start()

    inverse = 1.0 / (samples * n_smp)

    def assemble(block, before):
        chunk, side = block // 2, block % 2
        packed = summed[chunk, 0]
        turned = jnp.transpose(packed)
        if side:
            spare = jnp.where(
                lane[0:1] >= TILE,
                summed[chunk, 1, 0:1],
                pltpu.roll(summed[chunk, 2, 0:1], TILE, 1),
            )
            diagonal = jnp.where(line > lane, packed, jnp.where(line < lane, turned, spare))
        else:
            diagonal = jnp.where(line <= lane, packed, turned)
        after = jnp.transpose(summed[chunk, 1 + side])
        stack = [before[0:TILE], before[TILE:], diagonal[0:TILE], diagonal[TILE:]]
        stack += [after[0:TILE], after[TILE:]]
        flags = two_flags(band_next, place * (cols // TILE) + 2 * block, inverse)
        for index, flag in enumerate(flags):
            value = jnp.where(lane[0:TILE] < TILE, stack[index], stack[index + 1])
            ld_next[pl.ds(index * TILE, TILE), pl.ds(block * PAIR, PAIR)] = value * flag
        columns = pl.ds(block * PAIR, PAIR)
        results.append(
            pltpu.make_async_copy(ld_next.at[:, columns], ld_out.at[:, columns], out_sem.at[block])
        )
        results[-1].start()

    done = set()

    def assemble_ready():
        for block in range(1, blocks):
            needed = {block // 2, (block - 1) // 2}
            if block not in assembled and needed <= done:
                assembled.add(block)
                assemble(block, summed[(block - 1) // 2, 1 + (block - 1) % 2])

    assembled = set()
    for chunk in order:

        @pl.when(at_end)
        def _():
            second_pass(chunk)

        done.add(chunk)
        assemble_ready()

    @pl.when(has_left)
    def _():
        edge_copy().wait_recv()

    @pl.when(jnp.logical_not(has_left))
    def _():
        edge_in[...] = jnp.zeros((PAIR, PAIR), F32)

    assemble(0, edge_in[...])

    for copy in results:
        copy.wait()

    @pl.when(has_left)
    def _():
        side_copy.wait_send()

    @pl.when(has_right)
    def _():
        edge_copy().wait_send()

    for turn in range(3):
        up, down = halo_copies(turn)

        @pl.when(has_prev)
        def _():
            up.wait_send()

        @pl.when(has_next)
        def _():
            down.wait_send()

        for step in range(1, n_smp):
            red_copy(turn, step).wait_send()

    for chunk in range(chunks):
        for copy in running_copies(first_way, chunk):
            copy.wait_send()

        @pl.when(jnp.logical_not(at_end))
        def _():
            for copy in running_copies(second_way, chunk):
                copy.wait_send()


def hand_over(ld_held, imputed_held, ld_next, imputed, ld_near, imputed_near, sems):
    arrays = ((ld_held, ld_near, ld_next), (imputed_held, imputed_near, imputed))
    inward, outward = [], []
    for index, (source, near, target) in enumerate(arrays):
        part = source.shape[0] // HANDS
        for piece in range(HANDS):
            span = pl.ds(piece * part, part)
            sem = sems.at[0, index, piece]
            inward.append(pltpu.make_async_copy(source.at[span], near.at[span], sem))
            sem = sems.at[1, index, piece]
            outward.append(pltpu.make_async_copy(near.at[span], target.at[span], sem))
    for copy in inward:
        copy.start()
    for arrive, leave in zip(inward, outward):
        arrive.wait()
        leave.start()
    for copy in outward:
        copy.wait()


def local(sizes, dosage, allele_mean, snp_scale, band_next, ld_prev, band_prev, zscores, observed):
    n_smp = sizes[0]
    samples, cols = dosage.shape
    rows, traits = zscores.shape
    chunks = cols // CHUNK
    if traits < LANES:
        zscores = jnp.pad(zscores, ((0, 0), (0, LANES - traits)))
    far = pl.BlockSpec(memory_space=pltpu.HBM)
    dma = pltpu.SemaphoreType.DMA
    ld_next, imputed = pl.pallas_call(
        functools.partial(kernel, sizes),
        out_shape=(
            jax.ShapeDtypeStruct((SPAN * TILE, cols), F32),
            jax.ShapeDtypeStruct((rows, LANES), F32),
        ),
        in_specs=[far] * 8,
        out_specs=(far, far),
        scratch_shapes=[
            pltpu.VMEM((SPAN * TILE, cols), F32),
            pltpu.VMEM((rows, LANES), F32),
            pltpu.VMEM((1, allele_mean.shape[0]), F32),
            pltpu.VMEM((1, allele_mean.shape[0]), F32),
            pltpu.SMEM(band_next.shape, jnp.int32),
            pltpu.VMEM((SPAN * TILE, rows), F32),
            pltpu.SMEM(band_prev.shape, jnp.int32),
            pltpu.VMEM((rows, LANES), F32),
            pltpu.VMEM((observed.shape[1], rows), jnp.int32),
            pltpu.VMEM((rows, LANES), F32),
            pltpu.VMEM((samples, cols), BF16),
            pltpu.VMEM((samples, REACH), BF16),
            pltpu.VMEM((CHUNK, CHUNK), F32),
            pltpu.VMEM((PAIR, REACH), F32),
            pltpu.VMEM((chunks, 3, PAIR, PAIR), F32),
            pltpu.VMEM((chunks, 3, PAIR, PAIR), F32),
            pltpu.VMEM((2, chunks, 3, PAIR, PAIR), jnp.int16),
            pltpu.VMEM((2, chunks, 3, PAIR, PAIR), jnp.int16),
            pltpu.VMEM((2, chunks, 8, PAIR), F32),
            pltpu.VMEM((2, chunks, 8, PAIR), F32),
            pltpu.VMEM((PAIR, PAIR), F32),
            pltpu.VMEM((3, rows + 2 * REACH, LANES), F32),
            pltpu.VMEM((3, rows + 2 * REACH, 2 * LANES), BF16),
            pltpu.VMEM((rows // PAIR, 2 * PAIR, WIDE), BF16),
            pltpu.VMEM((3, rows, LANES), F32),
            pltpu.VMEM((rows, LANES), F32),
            pltpu.VMEM((rows, LANES), F32),
            pltpu.VMEM((3, n_smp, 8, LANES), F32),
            dma((7,)),
            dma((chunks,)),
            dma((2,)),
            dma((3, 2)),
            dma((3, 2)),
            dma((3, n_smp)),
            dma((3, n_smp)),
            dma((2, chunks)),
            dma((2, chunks)),
            dma((2, chunks)),
            dma((2, chunks)),
            dma((2,)),
            dma((cols // PAIR + 1,)),
        ],
        compiler_params=pltpu.CompilerParams(
            collective_id=0, has_side_effects=True, vmem_limit_bytes=60 * 1024 * 1024
        ),
    )(
        dosage,
        allele_mean.reshape(1, -1),
        snp_scale.reshape(1, -1),
        band_next,
        jnp.transpose(ld_prev),
        band_prev,
        zscores,
        jnp.transpose(observed),
    )
    ld_next, imputed = pl.pallas_call(
        hand_over,
        out_shape=(
            jax.ShapeDtypeStruct(ld_next.shape, F32),
            jax.ShapeDtypeStruct(imputed.shape, F32),
        ),
        in_specs=[far, far],
        out_specs=(far, far),
        scratch_shapes=[
            pltpu.VMEM(ld_next.shape, F32),
            pltpu.VMEM(imputed.shape, F32),
            dma((2, 2, HANDS)),
        ],
        compiler_params=pltpu.CompilerParams(vmem_limit_bytes=60 * 1024 * 1024),
    )(ld_next, imputed)
    return jnp.transpose(ld_next), imputed[:, :traits]


def solution(mesh):
    sizes = (mesh.shape["smp"], mesh.shape["snp"], mesh.shape["pair"])
    return jax.shard_map(
        functools.partial(local, sizes),
        mesh=mesh,
        in_specs=(
            P(("grp", "smp"), ("snp", "pair")),
            P("grp"),
            P("grp"),
            P("grp"),
            P(("grp", "smp"), None),
            P("grp"),
            P(("grp", "smp"), ("snp", "pair")),
            P(("grp", "smp"), ("snp", "pair")),
        ),
        out_specs=(P(("grp", "snp", "pair"), None), P(("grp", "smp"), ("snp", "pair"))),
        check_vma=False,
    )
```
